128 devices in a mesh: size: 8 (over z, x_lo), gz: 16 (over x_hi, y, core).
Axes of the slice: x: 4 (x_hi: 2, x_lo: 2; x = x_hi * 2 + x_lo), y: 4, z: 4, core: 2. Of those that a mesh axis runs over, the one named last changes fastest.
Arguments:
- tissue: int32 [512, 128, 128], P('gz'), may hold values from 0 to 2
- vessel_pressure: float32 [512, 128, 128], P('gz', 'size'), may hold values from -12 to 12
- cond_table: float32 [3], replicated, may hold values from 0.4 to 1.2
- leak_table: float32 [3], replicated, may hold values from 0.2 to 2
- bind_table: float32 [8, 3], P('size'), may hold values from 0.05 to 1
- hindrance: float32 [8], P('size'), may hold values from 0.2 to 1
- diffusivity: float32 [8], P('size'), may hold values from 0.1 to 0.6
- free_conc: float32 [8, 512, 128, 128], P('size', 'gz'), may hold values from 0 to 2
- bound_conc: float32 [8, 512, 128, 128], P('size', 'gz'), may hold values from 0 to 1
Outputs:
- pressure: float32 [512, 128, 128], P('gz', 'size')
- free_out: float32 [8, 512, 128, 128], P('size', 'gz')
- bound_out: float32 [8, 512, 128, 128], P('size', 'gz')
The draws below stay inside these ranges and needn't reach their ends.
Inputs may be any that keep to these rules, and one draw needn't show every extreme that they name: 0 marks a vessel cell, 1 necrotic tissue, 2 viable tissue.
All inputs are finite; a program needn't handle non-finite values.
Results may differ from the reference program's by a relative error of at most 0.0001.
Values sent between devices are 32-bit elements; how exact they have to be, the bound alone decides.
A program may use at most 128 MiB of HBM per device.

```python
import math
import jax
import jax.numpy as jnp

NY = 128
ITERS = 2
TSTEPS = 2
NX = 128
NZ = 512
SIZES = 8


def draw_vessel_pressure(key, part):
    depth = (jnp.arange(NZ, dtype=jnp.float32) / NZ)[:, None, None]
    across = (jnp.arange(NX, dtype=jnp.float32) / NX)[None, :, None]
    scale = 1.0 + depth + across
    base = jnp.clip(jax.random.normal(key, (NZ, NX, NY), jnp.float32), -4.0, 4.0)
    return base * scale


def touch_ends(drawn, rng, low, top_value):
    spot = [jax.random.randint(jax.random.fold_in(rng, axis), (), 0, length) for axis, length in enumerate(drawn.shape)]
    widest = drawn.shape.index(max(drawn.shape))
    neighbour = spot[:widest] + [(spot[widest] + 1) % drawn.shape[widest]] + spot[widest + 1:]
    return drawn.at[tuple(spot)].set(low).at[tuple(neighbour)].set(top_value)


def block_levels(key, extent, pieces, smallest, largest):
    factor_of, own = 1.0, jax.random.fold_in(key, 6)
    for dim, blocks in pieces:
        draws = jnp.exp(jax.random.uniform(jax.random.fold_in(own, dim), (blocks,), jnp.float32, smallest / len(pieces), largest / len(pieces)))
        factor_of = factor_of * jnp.repeat(draws, extent[dim] // blocks).reshape([-1 if axis == dim else 1 for axis in range(len(extent))])
    return factor_of


def setup_inputs(seed: int = 0) -> dict:
    arg_keys = jax.random.split(jax.random.key(seed), 10)
    return {
        "tissue": touch_ends(jax.random.randint(arg_keys[0], (NZ, NX, NY), 0, 3), jax.random.fold_in(arg_keys[0], 1), 0, 2).astype(jnp.int32),
        "vessel_pressure": draw_vessel_pressure(jax.random.fold_in(arg_keys[9], 71), 0),
        "cond_table": jnp.clip(jnp.exp(jax.random.uniform(arg_keys[2], (3,), jnp.float32, math.log(0.4), math.log(1.2))), 0.4, 1.2),
        "leak_table": jnp.clip(jnp.exp(jax.random.uniform(arg_keys[3], (3,), jnp.float32, math.log(0.2), math.log(2.0))), 0.2, 2.0),
        "bind_table": jnp.clip(jnp.exp(math.log(1.0) - 2.9957323 * jax.random.uniform(arg_keys[4], (SIZES, 3), jnp.float32) ** block_levels(arg_keys[4], (SIZES, 3), ((0, 8),), -0.2, 0.2)), 0.05, 1.0),
        "hindrance": jnp.clip(jnp.exp(math.log(1.0) - 1.609438 * jax.random.uniform(arg_keys[5], (SIZES,), jnp.float32) ** block_levels(arg_keys[5], (SIZES,), ((0, 8),), -0.2, 0.2)), 0.2, 1.0),
        "diffusivity": jnp.clip(jnp.exp(math.log(0.6) - 1.7917595 * jax.random.uniform(arg_keys[6], (SIZES,), jnp.float32) ** block_levels(arg_keys[6], (SIZES,), ((0, 8),), -0.2, 0.2)), 0.1, 0.6),
        "free_conc": jnp.clip(2.0 * jax.random.uniform(arg_keys[7], (SIZES, NZ, NX, NY), jnp.float32) ** block_levels(arg_keys[7], (SIZES, NZ, NX, NY), ((0, 8), (1, 16)), -0.2, 0.2), 0.0, 2.0),
        "bound_conc": jnp.clip(1.0 * jax.random.uniform(arg_keys[8], (SIZES, NZ, NX, NY), jnp.float32) ** block_levels(arg_keys[8], (SIZES, NZ, NX, NY), ((0, 8), (1, 16)), -0.2, 0.2), 0.0, 1.0),
    }


time_step = 0.1


def lookup(table, labels):
    return jnp.where(labels == 0, table[0], jnp.where(labels == 1, table[1], table[2]))


def neighbours(padded):
    total = padded[2:, 1:-1, 1:-1] + padded[:-2, 1:-1, 1:-1]
    total = total + padded[1:-1, 2:, 1:-1] + padded[1:-1, :-2, 1:-1]
    total = total + padded[1:-1, 1:-1, 2:] + padded[1:-1, 1:-1, :-2]
    return total


def apply_operator(vector, conduct, leak):
    scaled = conduct * vector
    padded = jnp.pad(scaled, 1)
    return conduct * (6.0 * scaled - neighbours(padded)) + leak * vector


def along_line(array, along_dim):
    return array[tuple(slice(None) if k == along_dim else slice(1, -1) for k in range(3))]


def lower_part(array, along_dim):
    return array[tuple(slice(0, -1) if k == along_dim else slice(None) for k in range(3))]


def upper_part(array, along_dim):
    return array[tuple(slice(1, None) if k == along_dim else slice(None) for k in range(3))]


def transport_step(conc_pad, fields_pad, hinder, diffuse):
    divergence = None
    for along_dim in range(3):
        conc_line = along_line(conc_pad, along_dim)
        press_line = along_line(fields_pad[0], along_dim)
        cond_line = along_line(fields_pad[1], along_dim)
        conc_low = lower_part(conc_line, along_dim)
        conc_high = upper_part(conc_line, along_dim)
        velocity = hinder * lower_part(cond_line, along_dim) * upper_part(cond_line, along_dim) * (lower_part(press_line, along_dim) - upper_part(press_line, along_dim))
        flux = jnp.maximum(velocity, 0.0) * conc_low + jnp.minimum(velocity, 0.0) * conc_high + diffuse * (conc_low - conc_high)
        term = upper_part(flux, along_dim) - lower_part(flux, along_dim)
        divergence = term if divergence is None else divergence + term
    conc = conc_pad[1:-1, 1:-1, 1:-1]
    rate = fields_pad[2][1:-1, 1:-1, 1:-1]
    bind = rate * conc
    return conc - time_step * (divergence + bind), bind


def reference(tissue, vessel_pressure, cond_table, leak_table, bind_table, hindrance, diffusivity, free_conc, bound_conc):
    conduct = lookup(cond_table, tissue)
    leak = lookup(leak_table, tissue)
    diag = 6.0 * conduct * conduct + leak
    source = leak * vessel_pressure
    solution = jnp.zeros_like(source)
    residual = source
    precond = residual / diag
    direction = precond
    rho_now = jnp.sum(residual * precond)
    for iteration in range(ITERS):
        image = apply_operator(direction, conduct, leak)
        alpha = rho_now / jnp.sum(direction * image)
        solution = solution + alpha * direction
        residual = residual - alpha * image
        if iteration + 1 < ITERS:
            precond = residual / diag
            rho_next = jnp.sum(residual * precond)
            direction = precond + (rho_next / rho_now) * direction
            rho_now = rho_next
    free_list = []
    bound_list = []
    for class_index in range(SIZES):
        rate = lookup(bind_table[class_index], tissue)
        fields_pad = jnp.pad(jnp.stack([solution, conduct, rate]), ((0, 0), (1, 1), (1, 1), (1, 1)))
        conc = free_conc[class_index]
        bound = bound_conc[class_index]
        for sweep in range(TSTEPS):
            conc, bind = transport_step(jnp.pad(conc, 1), fields_pad, hindrance[class_index], diffusivity[class_index])
            bound = bound + time_step * bind
        free_list.append(conc)
        bound_list.append(bound)
    return solution, jnp.stack(free_list), jnp.stack(bound_list)
```

```python
import functools

import jax
import jax.numpy as jnp
from jax import lax
from jax.experimental import pallas as pl
from jax.experimental.pallas import tpu as pltpu
from jax.sharding import PartitionSpec as P

MESH = pl.DeviceIdType.MESH
TIME_STEP = 0.1
EDGE = 8


def select(labels, values):
    first, second = labels == 0, labels == 1
    return [jnp.where(first, v[0], jnp.where(second, v[1], v[2])) for v in values]


def two_sum(a, b):
    total = a + b
    part = total - a
    return total, (a - (total - part)) + (b - part)


def split(a):
    wide = 4097.0 * a
    high = wide - (wide - a)
    return high, a - high


def two_prod(a, b):
    product = a * b
    ah, al = split(a)
    bh, bl = split(b)
    return product, ((ah * bh - product) + ah * bl + al * bh) + al * bl


def pair_sub_product(x, a, b):
    p, e = two_prod(a[0], b[0])
    e = e + (a[0] * b[1] + a[1] * b[0])
    s, r = two_sum(x[0], -p)
    r = r + (x[1] - e)
    return two_sum(s, r)


def pair_ratio(x, y):
    q = x[0] / y[0]
    rest = pair_sub_product(x, (q, jnp.zeros_like(q)), y)
    return two_sum(q, (rest[0] + rest[1]) / y[0])


def scalar_tables(cond_ref, leak_ref):
    cond = [cond_ref[i] for i in range(3)]
    leak = [leak_ref[i] for i in range(3)]
    inverse = []
    for k, l in zip(cond, leak):
        inverse.append((1.0 / jnp.full((8, 128), 6.0 * k * k + l, jnp.float32))[0, 0])
    return cond, leak, inverse


def lane_neighbours(q, lane, ny):
    up = jnp.where(lane == ny - 1, 0.0, pltpu.roll(q, ny - 1, 1))
    down = jnp.where(lane == 0, 0.0, pltpu.roll(q, 1, 1))
    return up + down


def exchange_kernel(
    n_size, n_gz, cond_ref, leak_ref, vp, tissue, conc,
    slab, thalo, chalo, scal,
    ext, tex, qs, qv, ys, tile, red_size, red_gz, total_tile,
    local_sem, near_send, near_recv, block_send, block_recv, low_send, low_recv, high_send, high_recv,
    ring_send, ring_recv, grid_send, grid_recv,
):
    s, g = lax.axis_index("size"), lax.axis_index("gz")
    nz, bx, ny = vp.shape
    half = bx // 2
    nx = tissue.shape[1]

    ext[...] = jnp.zeros_like(ext)
    tex[...] = jnp.full_like(tex, 3)

    def remote(src, dst, send, recv, to_s, to_g):
        return pltpu.make_async_remote_copy(
            src_ref=src, dst_ref=dst, send_sem=send, recv_sem=recv,
            device_id={"size": to_s, "gz": to_g}, device_id_type=MESH)

    own_rows = pl.ds(pl.multiple_of(s * bx, 8), bx)

    barrier = pltpu.get_barrier_semaphore()

    def greet(to_s, to_g):
        pl.semaphore_signal(barrier, inc=1, device_id={"size": to_s, "gz": to_g}, device_id_type=MESH)

    greeted = 0
    for j in range(n_size):
        peer = lax.rem(s + j, n_size)
        for d in (0, 1, n_gz - 1):
            if j or d:
                greet(peer, lax.rem(g + d, n_gz))
                greeted += 1
    for j in range(2, n_gz - 1):
        greet(s, lax.rem(g + j, n_gz))
        greeted += 1

    inner = pltpu.make_async_copy(vp, ext.at[pl.ds(2, nz), pl.ds(half, bx)], local_sem.at[0])
    inner.start()
    own = pltpu.make_async_copy(vp, slab.at[pl.ds(3, nz), own_rows], local_sem.at[1])
    own.start()

    wide = bx + 2 * half

    def tissue_rows(which):
        if which == "low":
            return pl.ds(0, bx + half), pl.ds(half, bx + half)
        if which == "high":
            return pl.ds(nx - bx - half, bx + half), pl.ds(0, bx + half)
        return pl.ds(pl.multiple_of(s * bx - half, 8), wide), pl.ds(0, wide)

    cases = (("low", s == 0), ("high", s == n_size - 1), ("mid", (s > 0) & (s < n_size - 1)))

    def tex_copy(which):
        src, dst = tissue_rows(which)
        return pltpu.make_async_copy(tissue.at[:, src], tex.at[pl.ds(2, nz), dst], local_sem.at[2])

    for which, cond in cases:
        @pl.when(cond)
        def _(which=which):
            tex_copy(which).start()

    pl.semaphore_wait(barrier, greeted)

    lows, highs = pl.ds(0, half), pl.ds(half, half)
    above, below = pl.ds(half + bx, half), pl.ds(0, half)
    middle = pl.ds(half, bx)
    has_low, has_high = g > 0, g < n_gz - 1
    x_low, x_high = s > 0, s < n_size - 1
    near = [
        (x_high, x_low, vp.at[:, highs], ext.at[pl.ds(2, nz), below], 0, s + 1, g),
        (x_low, x_high, vp.at[:, lows], ext.at[pl.ds(2, nz), above], 1, s - 1, g),
        (has_high, has_low, vp.at[pl.ds(nz - 2, 2)], ext.at[pl.ds(0, 2), middle], 2, s, g + 1),
        (has_low, has_high, vp.at[pl.ds(0, 2)], ext.at[pl.ds(nz + 2, 2), middle], 3, s, g - 1),
        (x_high & has_high, x_low & has_low, vp.at[pl.ds(nz - 1, 1), highs], ext.at[pl.ds(1, 1), below], 4, s + 1, g + 1),
        (x_low & has_high, x_high & has_low, vp.at[pl.ds(nz - 1, 1), lows], ext.at[pl.ds(1, 1), above], 5, s - 1, g + 1),
        (x_high & has_low, x_low & has_high, vp.at[pl.ds(0, 1), highs], ext.at[pl.ds(nz + 2, 1), below], 6, s + 1, g - 1),
        (x_low & has_low, x_high & has_high, vp.at[pl.ds(0, 1), lows], ext.at[pl.ds(nz + 2, 1), above], 7, s - 1, g - 1),
    ]
    for which, cond in cases:
        src, dst = tissue_rows(which)
        near.append((has_high & cond, has_low & cond, tissue.at[pl.ds(nz - 2, 2), src], tex.at[pl.ds(0, 2), dst], 8, s, g + 1))
        near.append((has_low & cond, has_high & cond, tissue.at[pl.ds(0, 2), src], tex.at[pl.ds(nz + 2, 2), dst], 9, s, g - 1))
    late = [
        (has_high, has_low, tissue.at[pl.ds(nz - 3, 3)], thalo.at[pl.ds(0, 3)], 10, s, g + 1),
        (has_low, has_high, tissue.at[pl.ds(0, 3)], thalo.at[pl.ds(3, 3)], 11, s, g - 1),
        (has_high, has_low, conc.at[pl.ds(nz - 2, 2)], chalo.at[pl.ds(0, 2)], 12, s, g + 1),
        (has_low, has_high, conc.at[pl.ds(0, 2)], chalo.at[pl.ds(2, 2)], 13, s, g - 1),
    ]

    def start_all(copies):
        for cond, _, src, dst, i, to_s, to_g in copies:
            @pl.when(cond)
            def _(src=src, dst=dst, i=i, to_s=to_s, to_g=to_g):
                remote(src, dst, near_send.at[i], near_recv.at[i], to_s, to_g).start()

    def wait_all(copies):
        for sent, cond, src, dst, i, to_s, to_g in copies:
            @pl.when(cond)
            def _(src=src, dst=dst, i=i):
                remote(src, dst, near_send.at[i], near_recv.at[i], s, g).wait_recv()

            @pl.when(sent)
            def _(src=src, dst=dst, i=i):
                remote(src, dst, near_send.at[i], near_recv.at[i], s, g).wait_send()

    start_all(near)

    def block_copy(j):
        return remote(vp, slab.at[pl.ds(3, nz), own_rows], block_send.at[j], block_recv.at[s], lax.rem(s + j, n_size), g)

    order = sorted(range(1, n_size), key=lambda j: min(j, n_size - j))
    for j in order:
        block_copy(j).start()
    start_all(late)

    def low_copy(j):
        return remote(vp.at[pl.ds(nz - 3, 3)], slab.at[pl.ds(0, 3), own_rows], low_send.at[j], low_recv.at[s], lax.rem(s + j, n_size), g + 1)

    def high_copy(j):
        return remote(vp.at[pl.ds(0, 3)], slab.at[pl.ds(nz + 3, 3), own_rows], high_send.at[j], high_recv.at[s], lax.rem(s + j, n_size), g - 1)

    @pl.when(has_high)
    def _():
        for j in range(n_size):
            low_copy(j).start()

    @pl.when(has_low)
    def _():
        for j in range(n_size):
            high_copy(j).start()

    cond, leak, inverse = scalar_tables(cond_ref, leak_ref)
    first = [l * i for l, i in zip(leak, inverse)]
    second = [k * l * i for k, l, i in zip(cond, leak, inverse)]
    lane = lax.broadcasted_iota(jnp.int32, (wide, ny), 1)

    inner.wait()
    for which, c in cases:
        @pl.when(c)
        def _(which=which):
            tex_copy(which).wait()
    wait_all(near)

    def scale(e, _):
        (t2,) = select(tex[e], [second])
        qs[e] = t2 * ext[e]
        return 0

    lax.fori_loop(0, nz + 4, scale, 0)

    def stencil(ref, e):
        q = ref[e]
        total = ref[e - 1] + ref[e + 1] + pltpu.roll(q, 1, 0) + pltpu.roll(q, wide - 1, 0)
        return 6.0 * q - (total + lane_neighbours(q, lane, ny))

    def add_product(acc, a, b):
        p, e = two_prod(a, b)
        h, r = two_sum(acc[0], p)
        return h, acc[1] + (e + r)

    def apply(e):
        labels = tex[e]
        k, l, i, t1 = select(labels, [cond, leak, inverse, first])
        k = jnp.where(labels == 3, 0.0, k)
        field = ext[e]
        z = t1 * field
        az = l * z + k * stencil(qs, e)
        y = i * az
        qv[e] = k * y
        ys[e] = y
        return l * field, z, az, y

    def mine(x):
        return x[half:half + bx]

    def first_sums(e, accs):
        r0, z, az, y = (mine(x) for x in apply(e))
        return (add_product(accs[0], r0, z), add_product(accs[1], z, az), add_product(accs[2], y, az))

    apply(1)
    apply(nz + 2)
    zero = jnp.zeros((bx, ny), jnp.float32)
    sums = lax.fori_loop(2, nz + 2, first_sums, ((zero, zero),) * 3)

    def last_sum(e, acc):
        labels = tex[e]
        k, l = select(labels, [cond, leak])
        y = ys[e]
        ay = l * y + k * stencil(qv, e)
        return add_product(acc, mine(y), mine(ay))

    sums = (*sums, lax.fori_loop(2, nz + 2, last_sum, (zero, zero)))

    row = lax.broadcasted_iota(jnp.int32, (8, ny), 0)
    packed = jnp.zeros((8, ny), jnp.float32)
    for m, (h, l) in enumerate(sums):
        hs, ls = h[0:8], l[0:8]
        for r in range(8, bx, 8):
            hs, e = two_sum(hs, h[r:r + 8])
            ls = ls + l[r:r + 8] + e
        for shift in (4, 2, 1):
            hs, e = two_sum(hs, pltpu.roll(hs, shift, 0))
            ls = ls + pltpu.roll(ls, shift, 0) + e
        packed = jnp.where(row == m, hs, jnp.where(row == m + 4, ls, packed))
    tile[...] = packed

    def add_tiles(parts):
        total, errors = parts[0], jnp.zeros((8, ny), jnp.float32)
        for part in parts[1:]:
            total, e = two_sum(total, part)
            errors = errors + e
        return total + pltpu.roll(jnp.where(row < 4, errors, 0.0), 4, 0)

    def reduce(src, slots, index, count, axis, send, recv):
        for j in range(1, count):
            to = lax.rem(index + j, count)
            dev = (to, g) if axis == "size" else (s, to)
            remote(src, slots.at[index], send.at[j], recv.at[index], *dev).start()
        parts = []
        for j in range(1, count):
            frm = lax.rem(index + j, count)
            remote(src, slots.at[frm], send.at[j], recv.at[frm], s, g).wait()
        slots[index] = src[...]
        return add_tiles([slots[i] for i in range(count)])

    total_tile[...] = reduce(tile, red_size, s, n_size, "size", ring_send, ring_recv)
    total = reduce(total_tile, red_gz, g, n_gz, "gz", grid_send, grid_recv)

    errors = jnp.zeros_like(total)
    shift = ny // 2
    while shift:
        total, e = two_sum(total, pltpu.roll(total, shift, 1))
        errors = errors + pltpu.roll(errors, shift, 1) + e
        shift //= 2
    lower = pltpu.roll(total, 4, 0) + errors
    b = [(total[m:m + 1], lower[m:m + 1]) for m in range(4)]
    t = pair_ratio(b[1], b[0])
    v = pair_sub_product(b[2], t, b[1])
    w = pair_sub_product(pair_sub_product(b[3], t, b[2]), t, v)
    b0, b1, v, w, t = b[0][0], b[1][0], v[0], w[0], t[0]
    det = b1 * w - v * v
    x_part = b0 * w / det
    y_part = -(b0 * v) / det
    scal[...] = jnp.where(row == 0, x_part + y_part * (1.0 - t), -y_part)

    for j in range(1, n_size):
        block_copy(j).wait_send()
        frm = lax.rem(s + j, n_size)
        remote(vp, slab.at[pl.ds(3, nz), own_rows], block_send.at[j], block_recv.at[frm], s, g).wait_recv()
    own.wait()

    @pl.when(has_high)
    def _():
        for j in range(n_size):
            low_copy(j).wait_send()
            remote(vp.at[pl.ds(0, 3)], slab.at[pl.ds(nz + 3, 3), own_rows], high_send.at[j], high_recv.at[j], s, g).wait_recv()

    @pl.when(has_low)
    def _():
        for j in range(n_size):
            high_copy(j).wait_send()
            remote(vp.at[pl.ds(0, 3)], slab.at[pl.ds(0, 3), own_rows], low_send.at[j], low_recv.at[j], s, g).wait_recv()

    wait_all(late)


def exchange(n_size, n_gz, cond_table, leak_table, vp, tissue, conc):
    nz, bx, ny = vp.shape
    nx = tissue.shape[1]
    anywhere = pl.BlockSpec(memory_space=pl.ANY)
    scalars = pl.BlockSpec(memory_space=pltpu.SMEM)
    dma = pltpu.SemaphoreType.DMA
    return pl.pallas_call(
        functools.partial(exchange_kernel, n_size, n_gz),
        out_shape=(
            jax.ShapeDtypeStruct((nz + 6, nx, ny), jnp.float32),
            jax.ShapeDtypeStruct((6, nx, ny), jnp.int32),
            jax.ShapeDtypeStruct((4, nx, ny), jnp.float32),
            jax.ShapeDtypeStruct((8, ny), jnp.float32),
        ),
        in_specs=[scalars, scalars, anywhere, anywhere, anywhere],
        out_specs=(anywhere, anywhere, anywhere, pl.BlockSpec(memory_space=pltpu.VMEM)),
        scratch_shapes=[
            pltpu.VMEM((nz + 4, 2 * bx, ny), jnp.float32),
            pltpu.VMEM((nz + 4, 2 * bx, ny), jnp.int32),
            pltpu.VMEM((nz + 4, 2 * bx, ny), jnp.float32),
            pltpu.VMEM((nz + 4, 2 * bx, ny), jnp.float32),
            pltpu.VMEM((nz + 4, 2 * bx, ny), jnp.float32),
            pltpu.VMEM((8, ny), jnp.float32),
            pltpu.VMEM((n_size, 8, ny), jnp.float32),
            pltpu.VMEM((n_gz, 8, ny), jnp.float32),
            pltpu.VMEM((8, ny), jnp.float32),
            dma((3,)),
            dma((14,)), dma((14,)),
            dma((n_size,)), dma((n_size,)),
            dma((n_size,)), dma((n_size,)),
            dma((n_size,)), dma((n_size,)),
            dma((n_size,)), dma((n_size,)),
            dma((n_gz,)), dma((n_gz,)),
        ],
        compiler_params=pltpu.CompilerParams(collective_id=0, has_side_effects=True, vmem_limit_bytes=16 << 20),
        name="exchange",
    )(cond_table, leak_table, vp, tissue, conc)


def transport_kernel(
    n_gz, cond_ref, leak_ref, bind_ref, hinder_ref, diffuse_ref, scal, slab, tissue, thalo, conc, chalo, bound,
    pressure, free_out, bound_out,
    vps, tis, c0, c1, bnd, out, qs, ps, ks, coef_z, wx, coefs, sems, out_sems, pressure_sem,
):
    s, g = lax.axis_index("size"), lax.axis_index("gz")
    nz, nx, ny = conc.shape
    bx = pressure.shape[1]
    rows = 32 if nx % 32 == 0 else nx
    chunk = 8
    n_chunks = nz // chunk
    has_low, has_high = g > 0, g < n_gz - 1
    inside = pl.ds(EDGE, nx)

    def chunk_copies(i):
        z0 = i * chunk
        return [
            pltpu.make_async_copy(slab.at[pl.ds(z0 + 3, chunk)], vps.at[pl.ds(z0 + 3, chunk)], sems.at[i, 0]),
            pltpu.make_async_copy(tissue.at[pl.ds(z0, chunk)], tis.at[pl.ds(z0 + 3, chunk)], sems.at[i, 1]),
            pltpu.make_async_copy(conc.at[pl.ds(z0, chunk)], c0.at[pl.ds(z0 + 2, chunk), inside], sems.at[i, 2]),
            pltpu.make_async_copy(bound.at[pl.ds(z0, chunk)], bnd.at[pl.ds(z0, chunk)], sems.at[i, 3]),
        ]

    def halo_copies(high):
        i, h, v, c = n_chunks + int(high), 3 * high, nz + 3 if high else 0, nz + 2 if high else 0
        return [
            pltpu.make_async_copy(slab.at[pl.ds(v, 3)], vps.at[pl.ds(v, 3)], sems.at[i, 0]),
            pltpu.make_async_copy(thalo.at[pl.ds(h, 3)], tis.at[pl.ds(v, 3)], sems.at[i, 1]),
            pltpu.make_async_copy(chalo.at[pl.ds(2 * high, 2)], c0.at[pl.ds(c, 2), inside], sems.at[i, 2]),
        ]

    def each(copies, what):
        for copy in copies:
            getattr(copy, what)()

    @pl.when(has_low)
    def _():
        each(halo_copies(False), "start")

    for i in range(n_chunks):
        each(chunk_copies(i), "start")

    @pl.when(has_high)
    def _():
        each(halo_copies(True), "start")

    edge_rows = jnp.zeros((EDGE, ny), jnp.float32)

    def clear(i, _):
        for ref in (c0, c1, qs, ps, ks):
            ref[i, pl.ds(0, EDGE), :] = edge_rows
            ref[i, pl.ds(EDGE + nx, EDGE), :] = edge_rows
        return 0

    lax.fori_loop(0, nz + 4, clear, 0)
    for i in (nz + 4, nz + 5):
        qs[i, pl.ds(0, EDGE), :] = edge_rows
        qs[i, pl.ds(EDGE + nx, EDGE), :] = edge_rows
    wx[pl.ds(0, EDGE), :] = edge_rows

    def blank(high):
        v, c = (nz + 3, nz + 2) if high else (0, 0)
        for i in range(3):
            vps[v + i] = jnp.zeros((nx, ny), jnp.float32)
            tis[v + i] = jnp.zeros((nx, ny), jnp.int32)
        for i in range(2):
            c0[c + i, inside, :] = jnp.zeros((nx, ny), jnp.float32)

    @pl.when(g == 0)
    def _():
        blank(False)

    @pl.when(g == n_gz - 1)
    def _():
        blank(True)

    cond, leak, inverse = scalar_tables(cond_ref, leak_ref)
    x_part, y_part = scal[0, 0], scal[1, 0]
    hinder = TIME_STEP * hinder_ref[0]
    diffuse = TIME_STEP * diffuse_ref[0]
    rate = [TIME_STEP * bind_ref[0, i] for i in range(3)]
    second = [k * l * i for k, l, i in zip(cond, leak, inverse)]
    z_part = [x_part * l * i for l, i in zip(leak, inverse)]
    n_part = [y_part * k * i for k, i in zip(cond, inverse)]
    lane = lax.broadcasted_iota(jnp.int32, (rows, ny), 1)
    first_lane, last_lane = lane == 0, lane == ny - 1
    diffuse_low = jnp.where(first_lane, 0.0, diffuse)
    diffuse_high = jnp.where(last_lane, 0.0, diffuse)
    starts = range(0, nx, rows)

    def scale(p):
        for r in starts:
            block = pl.ds(r, rows)
            (t2,) = select(tis[p + 3, block, :], [second])
            qs[p + 3, pl.ds(EDGE + r, rows), :] = t2 * vps[p + 3, block, :]

    def press(p):
        for r in starts:
            block = pl.ds(r, rows)
            here = pl.ds(EDGE + r, rows)
            k, zp, npart = select(tis[p + 3, block, :], [cond, z_part, n_part])
            q = qs[p + 3, here, :]
            total = qs[p + 2, here, :] + qs[p + 4, here, :]
            total = total + qs[p + 3, pl.ds(EDGE + r - 1, rows), :] + qs[p + 3, pl.ds(EDGE + r + 1, rows), :]
            total = total + jnp.where(first_lane, 0.0, pltpu.roll(q, 1, 1)) + jnp.where(last_lane, 0.0, pltpu.roll(q, ny - 1, 1))
            ps[p + 2, here, :] = zp * vps[p + 3, block, :] + npart * total
            ks[p + 2, here, :] = k

        @pl.when(((p < 0) & (g == 0)) | ((p >= nz) & (g == n_gz - 1)))
        def _():
            ks[p + 2, inside, :] = jnp.zeros((nx, ny), jnp.float32)

    def z_face(p, r):
        here = pl.ds(EDGE + r, rows)
        k, press_here = ks[p + 2, here, :] * hinder, ps[p + 2, here, :]
        w = k * ks[p + 3, here, :] * (press_here - ps[p + 3, here, :])
        return k, press_here, w

    def faces(p, slot, before):
        for r in starts:
            block = pl.ds(r, rows)
            here = pl.ds(EDGE + r, rows)
            k, press_here, w = z_face(p, r)
            a = jnp.maximum(w, 0.0) + diffuse
            b = a - w
            coef_z[slot, 0, block, :] = a
            coef_z[slot, 1, block, :] = b
            after = pl.ds(EDGE + r + 1, rows)
            w_x = k * ks[p + 2, after, :] * (press_here - ps[p + 2, after, :])
            wx[here, :] = w_x
            a_x = jnp.maximum(w_x, 0.0) + diffuse
            b_x = a_x - w_x
            w_low = wx[pl.ds(EDGE + r - 1, rows), :]
            a_x_low = jnp.maximum(w_low, 0.0) + diffuse
            b_x_low = a_x_low - w_low
            k_here = ks[p + 2, here, :]
            w_y = k * pltpu.roll(k_here, ny - 1, 1) * (press_here - pltpu.roll(press_here, ny - 1, 1))
            w_y = jnp.where(last_lane, 0.0, w_y)
            up = jnp.maximum(w_y, 0.0)
            a_y = up + diffuse
            b_y = (up - w_y) + diffuse_high
            w_low = pltpu.roll(w_y, 1, 1)
            up = jnp.maximum(w_low, 0.0)
            a_y_low = up + diffuse_low
            b_y_low = (up - w_low) + diffuse
            (bind,) = select(tis[p + 3, block, :], [rate])
            centre = (a + a_x) + (a_y + b_x_low) + (b_y_low + coef_z[before, 1, block, :]) + bind
            coefs[slot, 0, block, :] = 1.0 - centre
            coefs[slot, 1, block, :] = a_x_low
            coefs[slot, 2, block, :] = b_x
            coefs[slot, 3, block, :] = a_y_low
            coefs[slot, 4, block, :] = b_y

    def advance(src, p, slot, before, r):
        block = pl.ds(r, rows)
        here = pl.ds(EDGE + r, rows)
        c = src[p + 2, here, :]
        value = coefs[slot, 0, block, :] * c
        value = value + coef_z[slot, 1, block, :] * src[p + 3, here, :] + coef_z[before, 0, block, :] * src[p + 1, here, :]
        value = value + coefs[slot, 1, block, :] * src[p + 2, pl.ds(EDGE + r - 1, rows), :]
        value = value + coefs[slot, 2, block, :] * src[p + 2, pl.ds(EDGE + r + 1, rows), :]
        value = value + coefs[slot, 3, block, :] * pltpu.roll(c, 1, 1)
        value = value + coefs[slot, 4, block, :] * pltpu.roll(c, ny - 1, 1)
        return c, value

    def first_step(p, slot, before):
        for r in starts:
            _, value = advance(c0, p, slot, before, r)
            c1[p + 2, pl.ds(EDGE + r, rows), :] = value

        @pl.when(((p < 0) & (g == 0)) | ((p >= nz) & (g == n_gz - 1)))
        def _():
            c1[p + 2, inside, :] = jnp.zeros((nx, ny), jnp.float32)

    def second_step(p, slot, before):
        for r in starts:
            block = pl.ds(r, rows)
            c, value = advance(c1, p, slot, before, r)
            out[p, block, :] = value
            (bind,) = select(tis[p + 3, block, :], [rate])
            bnd[p, block, :] = bnd[p, block, :] + bind * (c0[p + 2, pl.ds(EDGE + r, rows), :] + c)

    def out_copies(i):
        z0 = pl.ds(i * chunk, chunk)
        return [
            pltpu.make_async_copy(out.at[z0], free_out.at[z0], out_sems.at[i, 0]),
            pltpu.make_async_copy(bnd.at[z0], bound_out.at[z0], out_sems.at[i, 1]),
        ]

    @pl.when(has_low)
    def _():
        each(halo_copies(False), "wait")

    each(chunk_copies(0), "wait")

    for p in range(-3, 1):
        scale(p)
    for p in (-2, -1):
        press(p)
    for r in starts:
        w = z_face(-2, r)[2]
        a = jnp.maximum(w, 0.0) + diffuse
        coef_z[1, 0, pl.ds(r, rows), :] = a
        coef_z[1, 1, pl.ds(r, rows), :] = a - w
    scale(1)
    press(0)
    faces(-1, 2, 1)
    first_step(-1, 2, 1)

    def body(p, _):
        slot, before, older = lax.rem(p, 3), lax.rem(p + 2, 3), lax.rem(p + 1, 3)
        group = lax.div(p + 2, chunk)

        @pl.when((lax.rem(p + 2, chunk) == 0) & (group < n_chunks))
        def _():
            each(chunk_copies(group), "wait")

        @pl.when((p == nz - 2) & has_high)
        def _():
            each(halo_copies(True), "wait")

        scale(p + 2)
        press(p + 1)
        faces(p, slot, before)
        first_step(p, slot, before)

        @pl.when(p > 0)
        def _():
            second_step(p - 1, before, older)

        @pl.when((p > 0) & (lax.rem(p, chunk) == 0))
        def _():
            each(out_copies(lax.div(p, chunk) - 1), "start")

        return 0

    lax.fori_loop(0, nz + 1, body, 0)
    own = pltpu.make_async_copy(
        ps.at[pl.ds(2, nz), pl.ds(pl.multiple_of(EDGE + s * bx, 8), bx)], pressure, pressure_sem)
    own.start()
    for i in range(n_chunks):
        each(out_copies(i), "wait")
    own.wait()


def transport(n_gz, bx, cond_table, leak_table, bind_table, hindrance, diffusivity, scal, slab, tissue, thalo, conc, chalo, bound):
    nz, nx, ny = conc.shape
    anywhere = pl.BlockSpec(memory_space=pl.ANY)
    scalars = pl.BlockSpec(memory_space=pltpu.SMEM)
    wide = nx + 2 * EDGE
    f32 = jnp.float32
    dma = pltpu.SemaphoreType.DMA
    n_chunks = nz // 8
    return pl.pallas_call(
        functools.partial(transport_kernel, n_gz),
        out_shape=(
            jax.ShapeDtypeStruct((nz, bx, ny), f32),
            jax.ShapeDtypeStruct((nz, nx, ny), f32),
            jax.ShapeDtypeStruct((nz, nx, ny), f32),
        ),
        in_specs=[scalars] * 5 + [pl.BlockSpec(memory_space=pltpu.VMEM)] + [anywhere] * 6,
        out_specs=(anywhere, anywhere, anywhere),
        scratch_shapes=[
            pltpu.VMEM((nz + 6, nx, ny), f32),
            pltpu.VMEM((nz + 6, nx, ny), jnp.int32),
            pltpu.VMEM((nz + 4, wide, ny), f32),
            pltpu.VMEM((nz + 4, wide, ny), f32),
            pltpu.VMEM((nz, nx, ny), f32),
            pltpu.VMEM((nz, nx, ny), f32),
            pltpu.VMEM((nz + 6, wide, ny), f32),
            pltpu.VMEM((nz + 4, wide, ny), f32),
            pltpu.VMEM((nz + 4, wide, ny), f32),
            pltpu.VMEM((3, 2, nx, ny), f32),
            pltpu.VMEM((wide, ny), f32),
            pltpu.VMEM((3, 5, nx, ny), f32),
            dma((n_chunks + 2, 4)),
            dma((n_chunks, 2)),
            dma,
        ],
        compiler_params=pltpu.CompilerParams(vmem_limit_bytes=40 << 20),
        name="transport",
    )(cond_table, leak_table, bind_table, hindrance, diffusivity, scal, slab, tissue, thalo, conc, chalo, bound)


def solution(mesh):
    n_size, n_gz = mesh.shape["size"], mesh.shape["gz"]

    def local(tissue, vessel_pressure, cond_table, leak_table, bind_table, hindrance, diffusivity, free_conc, bound_conc):
        conc, bound = free_conc[0], bound_conc[0]
        slab, thalo, chalo, scal = exchange(n_size, n_gz, cond_table, leak_table, vessel_pressure, tissue, conc)
        pressure, free, held = transport(
            n_gz, vessel_pressure.shape[1], cond_table, leak_table, bind_table, hindrance, diffusivity,
            scal, slab, tissue, thalo, conc, chalo, bound)
        return pressure, free[None], held[None]

    return jax.shard_map(
        local,
        mesh=mesh,
        in_specs=(
            P("gz", None, None), P("gz", "size", None), P(), P(), P("size", None), P("size"), P("size"),
            P("size", "gz", None, None), P("size", "gz", None, None),
        ),
        out_specs=(P("gz", "size", None), P("size", "gz", None, None), P("size", "gz", None, None)),
        check_vma=False,
    )
```

```python
import functools

import jax
import jax.numpy as jnp
from jax import lax
from jax.experimental import pallas as pl
from jax.experimental.pallas import tpu as pltpu
from jax.sharding import PartitionSpec as P

MESH = pl.DeviceIdType.MESH
TIME_STEP = 0.1
EDGE = 8
CHUNKS = 4


def each(copies, what):
    for copy in copies:
        getattr(copy, what)()


def select(labels, values):
    first, second = labels == 0, labels == 1
    return [jnp.where(first, v[0], jnp.where(second, v[1], v[2])) for v in values]


def two_sum(a, b):
    total = a + b
    part = total - a
    return total, (a - (total - part)) + (b - part)


def split(a):
    wide = 4097.0 * a
    high = wide - (wide - a)
    return high, a - high


def two_prod(a, b):
    product = a * b
    ah, al = split(a)
    bh, bl = split(b)
    return product, ((ah * bh - product) + ah * bl + al * bh) + al * bl


def pair_sub_product(x, a, b):
    p, e = two_prod(a[0], b[0])
    e = e + (a[0] * b[1] + a[1] * b[0])
    s, r = two_sum(x[0], -p)
    r = r + (x[1] - e)
    return two_sum(s, r)


def pair_ratio(x, y):
    q = x[0] / y[0]
    rest = pair_sub_product(x, (q, jnp.zeros_like(q)), y)
    return two_sum(q, (rest[0] + rest[1]) / y[0])


def scalar_tables(cond_ref, leak_ref):
    cond = [cond_ref[i] for i in range(3)]
    leak = [leak_ref[i] for i in range(3)]
    inverse = []
    for k, l in zip(cond, leak):
        inverse.append((1.0 / jnp.full((8, 128), 6.0 * k * k + l, jnp.float32))[0, 0])
    return cond, leak, inverse


def lane_neighbours(q, lane, ny):
    up = jnp.where(lane == ny - 1, 0.0, pltpu.roll(q, ny - 1, 1))
    down = jnp.where(lane == 0, 0.0, pltpu.roll(q, 1, 1))
    return up + down


def exchange_kernel(
    n_size, n_gz, cond_ref, leak_ref, vp, tissue, conc,
    slab, thalo, chalo, scal,
    ext, tex, qs, qv, ys, packed_out, packed_in, tile, red_size, red_gz, total_tile,
    local_sem, near_send, near_recv, block_send, block_recv,
    ring_send, ring_recv, grid_send, grid_recv,
):
    s, g = lax.axis_index("size"), lax.axis_index("gz")
    nz, bx, ny = vp.shape
    half = bx // 2
    nx = tissue.shape[1]

    ext[...] = jnp.zeros_like(ext)
    tex[...] = jnp.full_like(tex, 3)

    def remote(src, dst, send, recv, to_s, to_g):
        return pltpu.make_async_remote_copy(
            src_ref=src, dst_ref=dst, send_sem=send, recv_sem=recv,
            device_id={"size": to_s, "gz": to_g}, device_id_type=MESH)

    own_rows = pl.ds(pl.multiple_of(s * bx, 8), bx)

    barrier = pltpu.get_barrier_semaphore()

    def greet(to_s, to_g):
        pl.semaphore_signal(barrier, inc=1, device_id={"size": to_s, "gz": to_g}, device_id_type=MESH)

    greeted = 0
    for j in range(n_size):
        peer = lax.rem(s + j, n_size)
        for d in ((0,) if 1 < j < n_size - 1 else (0, 1, n_gz - 1)):
            if j or d:
                greet(peer, lax.rem(g + d, n_gz))
                greeted += 1
    for j in range(2, n_gz - 1):
        greet(s, lax.rem(g + j, n_gz))
        greeted += 1

    inner = pltpu.make_async_copy(vp, ext.at[pl.ds(2, nz), pl.ds(half, bx)], local_sem.at[0])
    inner.start()
    own = pltpu.make_async_copy(vp, slab.at[pl.ds(3, nz), own_rows], local_sem.at[1])
    own.start()

    wide = bx + 2 * half

    def tissue_rows(which):
        if which == "low":
            return pl.ds(0, bx + half), pl.ds(half, bx + half)
        if which == "high":
            return pl.ds(nx - bx - half, bx + half), pl.ds(0, bx + half)
        return pl.ds(pl.multiple_of(s * bx - half, 8), wide), pl.ds(0, wide)

    cases = (("low", s == 0), ("high", s == n_size - 1), ("mid", (s > 0) & (s < n_size - 1)))

    def tex_copy(which):
        src, dst = tissue_rows(which)
        return pltpu.make_async_copy(tissue.at[:, src], tex.at[pl.ds(2, nz), dst], local_sem.at[2])

    for which, cond in cases:
        @pl.when(cond)
        def _(which=which):
            tex_copy(which).start()

    inner.wait()

    def pack(e, _):
        for i, r in enumerate((half, half + 1, half + bx - 2, half + bx - 1)):
            packed_out[i, pl.ds(e, 1), :] = ext[e + 2, pl.ds(r, 1), :]
        return 0

    lax.fori_loop(0, nz, pack, 0, unroll=4)
    pl.semaphore_wait(barrier, greeted)

    lows, highs = pl.ds(0, half), pl.ds(half, half)
    above, below = pl.ds(half + bx, half), pl.ds(0, half)
    middle = pl.ds(half, bx)
    has_low, has_high = g > 0, g < n_gz - 1
    x_low, x_high = s > 0, s < n_size - 1
    near = [
        (x_high, x_low, packed_out.at[pl.ds(2, 2)], packed_in.at[pl.ds(0, 2)], 0, s + 1, g),
        (x_low, x_high, packed_out.at[pl.ds(0, 2)], packed_in.at[pl.ds(2, 2)], 1, s - 1, g),
        (has_high, has_low, vp.at[pl.ds(nz - 2, 2)], ext.at[pl.ds(0, 2), middle], 2, s, g + 1),
        (has_low, has_high, vp.at[pl.ds(0, 2)], ext.at[pl.ds(nz + 2, 2), middle], 3, s, g - 1),
        (x_high & has_high, x_low & has_low, vp.at[pl.ds(nz - 1, 1), highs], ext.at[pl.ds(1, 1), below], 4, s + 1, g + 1),
        (x_low & has_high, x_high & has_low, vp.at[pl.ds(nz - 1, 1), lows], ext.at[pl.ds(1, 1), above], 5, s - 1, g + 1),
        (x_high & has_low, x_low & has_high, vp.at[pl.ds(0, 1), highs], ext.at[pl.ds(nz + 2, 1), below], 6, s + 1, g - 1),
        (x_low & has_low, x_high & has_high, vp.at[pl.ds(0, 1), lows], ext.at[pl.ds(nz + 2, 1), above], 7, s - 1, g - 1),
    ]
    for which, cond in cases:
        src, dst = tissue_rows(which)
        near.append((has_high & cond, has_low & cond, tissue.at[pl.ds(nz - 2, 2), src], tex.at[pl.ds(0, 2), dst], 8, s, g + 1))
        near.append((has_low & cond, has_high & cond, tissue.at[pl.ds(0, 2), src], tex.at[pl.ds(nz + 2, 2), dst], 9, s, g - 1))
    late = [
        (has_high, has_low, tissue.at[pl.ds(nz - 3, 3)], thalo.at[pl.ds(0, 3)], 10, s, g + 1),
        (has_low, has_high, tissue.at[pl.ds(0, 3)], thalo.at[pl.ds(3, 3)], 11, s, g - 1),
        (has_high, has_low, conc.at[pl.ds(nz - 2, 2)], chalo.at[pl.ds(0, 2)], 12, s, g + 1),
        (has_low, has_high, conc.at[pl.ds(0, 2)], chalo.at[pl.ds(2, 2)], 13, s, g - 1),
    ]

    def start_all(copies):
        for cond, _, src, dst, i, to_s, to_g in copies:
            @pl.when(cond)
            def _(src=src, dst=dst, i=i, to_s=to_s, to_g=to_g):
                remote(src, dst, near_send.at[i], near_recv.at[i], to_s, to_g).start()

    def wait_all(copies):
        for sent, cond, src, dst, i, to_s, to_g in copies:
            @pl.when(cond)
            def _(src=src, dst=dst, i=i):
                remote(src, dst, near_send.at[i], near_recv.at[i], s, g).wait_recv()

            @pl.when(sent)
            def _(src=src, dst=dst, i=i):
                remote(src, dst, near_send.at[i], near_recv.at[i], s, g).wait_send()

    start_all(near)

    n_z = n_size // 2
    z, x = lax.div(s, 2), lax.rem(s, 2)
    z_up, z_down, z_far = lax.rem(z + 1, n_z), lax.rem(z + n_z - 1, n_z), lax.rem(z + 2, n_z)
    across = 2 * z + 1 - x
    up, down, far = 2 * z_up + x, 2 * z_down + x, 2 * z_far + x
    up_across, down_across, far_across = 2 * z_up + 1 - x, 2 * z_down + 1 - x, 2 * z_far + 1 - x
    depth = nz // CHUNKS
    part = depth // 2
    order = [0, CHUNKS - 1, *range(1, CHUNKS - 1)]

    def piece(block, c, kind, to, first=0, count=depth, own=False):
        planes = pl.ds(3 + c * depth + first, count)
        where = pl.ds(pl.multiple_of(block * bx, 8), bx)
        src = vp.at[pl.ds(c * depth + first, count)] if own else slab.at[planes, where]
        return remote(src, slab.at[planes, where], block_send.at[kind, c], block_recv.at[kind, c], to, g)

    def own_pieces(c):
        return [piece(s, c, 0, across, own=True), piece(s, c, 1, up, own=True), piece(s, c, 2, down, own=True)]

    def from_across(c):
        return [piece(across, c, 3, up), piece(across, c, 4, down)]

    def from_down(c):
        return [piece(down, c, 5, up, 0, part)]

    def from_up(c):
        return [piece(up, c, 6, down, part, depth - part)]

    def from_far(c):
        return [piece(far, c, 7, across)]

    def hand_on(c):
        piece(across, c, 0, s).wait_recv()
        each(from_across(c), "start")
        piece(down, c, 1, s).wait_recv()
        each(from_down(c), "start")
        piece(up, c, 2, s).wait_recv()
        each(from_up(c), "start")

    def hand_far(c):
        piece(far, c, 5, s, 0, part).wait_recv()
        piece(far, c, 6, s, part, depth - part).wait_recv()
        each(from_far(c), "start")

    def finish(c):
        piece(down_across, c, 3, s).wait_recv()
        piece(up_across, c, 4, s).wait_recv()
        piece(far_across, c, 7, s).wait_recv()

    for c in order:
        each(own_pieces(c), "start")
    start_all(late)

    edges = [
        (has_high, has_low, slab.at[pl.ds(nz, 3)], slab.at[pl.ds(0, 3)], 14, s, g + 1),
        (has_low, has_high, slab.at[pl.ds(3, 3)], slab.at[pl.ds(nz + 3, 3)], 15, s, g - 1),
    ]

    cond, leak, inverse = scalar_tables(cond_ref, leak_ref)
    first = [l * i for l, i in zip(leak, inverse)]
    second = [k * l * i for k, l, i in zip(cond, leak, inverse)]
    lane = lax.broadcasted_iota(jnp.int32, (wide, ny), 1)

    for which, c in cases:
        @pl.when(c)
        def _(which=which):
            tex_copy(which).wait()
    wait_all(near)

    def unpack(low):
        def rows_in(e, _):
            for i in range(2):
                r = half - 2 + i if low else half + bx + i
                ext[e + 2, pl.ds(r, 1), :] = packed_in[i if low else 2 + i, pl.ds(e, 1), :]
            return 0
        lax.fori_loop(0, nz, rows_in, 0, unroll=4)

    @pl.when(x_low)
    def _():
        unpack(True)

    @pl.when(x_high)
    def _():
        unpack(False)

    def scale(e, _):
        (t2,) = select(tex[e], [second])
        qs[e] = t2 * ext[e]
        return 0

    lax.fori_loop(0, nz + 4, scale, 0)

    def stencil(ref, e):
        q = ref[e]
        total = ref[e - 1] + ref[e + 1] + pltpu.roll(q, 1, 0) + pltpu.roll(q, wide - 1, 0)
        return 6.0 * q - (total + lane_neighbours(q, lane, ny))

    def add_product(acc, a, b):
        p, e = two_prod(a, b)
        h, r = two_sum(acc[0], p)
        return h, acc[1] + (e + r)

    def apply(e):
        labels = tex[e]
        k, l, i, t1 = select(labels, [cond, leak, inverse, first])
        k = jnp.where(labels == 3, 0.0, k)
        field = ext[e]
        z = t1 * field
        az = l * z + k * stencil(qs, e)
        y = i * az
        qv[e] = k * y
        ys[e] = y
        return l * field, z, az, y

    def mine(x):
        return x[half:half + bx]

    def first_sums(e, accs):
        r0, z, az, y = (mine(x) for x in apply(e))
        return (add_product(accs[0], r0, z), add_product(accs[1], z, az), add_product(accs[2], y, az))

    apply(1)
    apply(nz + 2)
    zero = jnp.zeros((bx, ny), jnp.float32)
    sums = lax.fori_loop(2, nz + 2, first_sums, ((zero, zero),) * 3)

    def last_sum(e, acc):
        labels = tex[e]
        k, l = select(labels, [cond, leak])
        y = ys[e]
        ay = l * y + k * stencil(qv, e)
        return add_product(acc, mine(y), mine(ay))

    sums = (*sums, lax.fori_loop(2, nz + 2, last_sum, (zero, zero)))

    row = lax.broadcasted_iota(jnp.int32, (8, ny), 0)
    packed = jnp.zeros((8, ny), jnp.float32)
    for m, (h, l) in enumerate(sums):
        hs, ls = h[0:8], l[0:8]
        for r in range(8, bx, 8):
            hs, e = two_sum(hs, h[r:r + 8])
            ls = ls + l[r:r + 8] + e
        for shift in (4, 2, 1):
            hs, e = two_sum(hs, pltpu.roll(hs, shift, 0))
            ls = ls + pltpu.roll(ls, shift, 0) + e
        packed = jnp.where(row == m, hs, jnp.where(row == m + 4, ls, packed))
    tile[...] = packed

    def add_tiles(parts):
        total, errors = parts[0], jnp.zeros((8, ny), jnp.float32)
        for part in parts[1:]:
            total, e = two_sum(total, part)
            errors = errors + e
        return total + pltpu.roll(jnp.where(row < 4, errors, 0.0), 4, 0)

    def reduce(src, slots, index, count, axis, send, recv, between):
        for j in range(1, count):
            to = lax.rem(index + j, count)
            dev = (to, g) if axis == "size" else (s, to)
            remote(src, slots.at[index], send.at[j], recv.at[index], *dev).start()
        between()
        for j in range(1, count):
            frm = lax.rem(index + j, count)
            remote(src, slots.at[frm], send.at[j], recv.at[frm], s, g).wait()
        slots[index] = src[...]
        return add_tiles([slots[i] for i in range(count)])

    def first_half():
        for c in order[:CHUNKS // 2]:
            hand_on(c)

    def second_half():
        for c in order[:CHUNKS // 2]:
            hand_far(c)
        for c in order[CHUNKS // 2:]:
            hand_on(c)

    total_tile[...] = reduce(tile, red_size, s, n_size, "size", ring_send, ring_recv, first_half)
    total = reduce(total_tile, red_gz, g, n_gz, "gz", grid_send, grid_recv, second_half)

    errors = jnp.zeros_like(total)
    shift = ny // 2
    while shift:
        total, e = two_sum(total, pltpu.roll(total, shift, 1))
        errors = errors + pltpu.roll(errors, shift, 1) + e
        shift //= 2
    lower = pltpu.roll(total, 4, 0) + errors
    b = [(total[m:m + 1], lower[m:m + 1]) for m in range(4)]
    t = pair_ratio(b[1], b[0])
    v = pair_sub_product(b[2], t, b[1])
    w = pair_sub_product(pair_sub_product(b[3], t, b[2]), t, v)
    b0, b1, v, w, t = b[0][0], b[1][0], v[0], w[0], t[0]
    det = b1 * w - v * v
    x_part = b0 * w / det
    y_part = -(b0 * v) / det
    scal[...] = jnp.where(row == 0, x_part + y_part * (1.0 - t), -y_part)

    own.wait()
    for c in order[:2]:
        finish(c)
    start_all(edges)
    for c in order[CHUNKS // 2:]:
        hand_far(c)
    for c in order[2:]:
        finish(c)
    for c in order:
        each(own_pieces(c) + from_across(c) + from_down(c) + from_up(c) + from_far(c), "wait_send")
    wait_all(late)
    wait_all(edges)


def exchange(n_size, n_gz, cond_table, leak_table, vp, tissue, conc):
    nz, bx, ny = vp.shape
    nx = tissue.shape[1]
    anywhere = pl.BlockSpec(memory_space=pl.ANY)
    scalars = pl.BlockSpec(memory_space=pltpu.SMEM)
    hbm = pl.BlockSpec(memory_space=pltpu.HBM)
    dma = pltpu.SemaphoreType.DMA
    return pl.pallas_call(
        functools.partial(exchange_kernel, n_size, n_gz),
        out_shape=(
            jax.ShapeDtypeStruct((nz + 6, nx, ny), jnp.float32),
            jax.ShapeDtypeStruct((6, nx, ny), jnp.int32),
            jax.ShapeDtypeStruct((4, nx, ny), jnp.float32),
            jax.ShapeDtypeStruct((8, ny), jnp.float32),
        ),
        in_specs=[scalars, scalars, hbm, hbm, hbm],
        out_specs=(anywhere, anywhere, anywhere, pl.BlockSpec(memory_space=pltpu.VMEM)),
        scratch_shapes=[
            pltpu.VMEM((nz + 4, 2 * bx, ny), jnp.float32),
            pltpu.VMEM((nz + 4, 2 * bx, ny), jnp.int32),
            pltpu.VMEM((nz + 4, 2 * bx, ny), jnp.float32),
            pltpu.VMEM((nz + 4, 2 * bx, ny), jnp.float32),
            pltpu.VMEM((nz + 4, 2 * bx, ny), jnp.float32),
            pltpu.VMEM((4, nz, ny), jnp.float32),
            pltpu.VMEM((4, nz, ny), jnp.float32),
            pltpu.VMEM((8, ny), jnp.float32),
            pltpu.VMEM((n_size, 8, ny), jnp.float32),
            pltpu.VMEM((n_gz, 8, ny), jnp.float32),
            pltpu.VMEM((8, ny), jnp.float32),
            dma((3,)),
            dma((16,)), dma((16,)),
            dma((8, CHUNKS)), dma((8, CHUNKS)),
            dma((n_size,)), dma((n_size,)),
            dma((n_gz,)), dma((n_gz,)),
        ],
        compiler_params=pltpu.CompilerParams(collective_id=0, has_side_effects=True, vmem_limit_bytes=60 << 20),
        name="exchange",
    )(cond_table, leak_table, vp, tissue, conc)


def transport_kernel(
    n_gz, cond_ref, leak_ref, bind_ref, hinder_ref, diffuse_ref, scal, slab, tissue, thalo, conc, chalo, bound,
    pressure, free_out, bound_out,
    vps, tis, c0, c1, bnd, out, qs, ps, ks, coef_z, wx, coefs, sems, out_sems, pressure_sem,
):
    s, g = lax.axis_index("size"), lax.axis_index("gz")
    nz, nx, ny = conc.shape
    bx = pressure.shape[1]
    rows = 32 if nx % 32 == 0 else nx
    chunk = 8
    n_chunks = nz // chunk
    has_low, has_high = g > 0, g < n_gz - 1
    inside = pl.ds(EDGE, nx)

    def chunk_copies(i):
        z0 = i * chunk
        return [
            pltpu.make_async_copy(slab.at[pl.ds(z0 + 3, chunk)], vps.at[pl.ds(z0 + 3, chunk)], sems.at[i, 0]),
            pltpu.make_async_copy(tissue.at[pl.ds(z0, chunk)], tis.at[pl.ds(z0 + 3, chunk)], sems.at[i, 1]),
            pltpu.make_async_copy(conc.at[pl.ds(z0, chunk)], c0.at[pl.ds(z0 + 2, chunk), inside], sems.at[i, 2]),
            pltpu.make_async_copy(bound.at[pl.ds(z0, chunk)], bnd.at[pl.ds(z0, chunk)], sems.at[i, 3]),
        ]

    def halo_copies(high):
        i, h, v, c = n_chunks + int(high), 3 * high, nz + 3 if high else 0, nz + 2 if high else 0
        return [
            pltpu.make_async_copy(slab.at[pl.ds(v, 3)], vps.at[pl.ds(v, 3)], sems.at[i, 0]),
            pltpu.make_async_copy(thalo.at[pl.ds(h, 3)], tis.at[pl.ds(v, 3)], sems.at[i, 1]),
            pltpu.make_async_copy(chalo.at[pl.ds(2 * high, 2)], c0.at[pl.ds(c, 2), inside], sems.at[i, 2]),
        ]

    @pl.when(has_low)
    def _():
        each(halo_copies(False), "start")

    for i in range(n_chunks):
        each(chunk_copies(i), "start")

    @pl.when(has_high)
    def _():
        each(halo_copies(True), "start")

    edge_rows = jnp.zeros((EDGE, ny), jnp.float32)

    def clear(i, _):
        for ref in (c0, c1, qs, ps, ks):
            ref[i, pl.ds(0, EDGE), :] = edge_rows
            ref[i, pl.ds(EDGE + nx, EDGE), :] = edge_rows
        return 0

    lax.fori_loop(0, nz + 4, clear, 0)
    for i in (nz + 4, nz + 5):
        qs[i, pl.ds(0, EDGE), :] = edge_rows
        qs[i, pl.ds(EDGE + nx, EDGE), :] = edge_rows
    wx[pl.ds(0, EDGE), :] = edge_rows

    def blank(high):
        v, c = (nz + 3, nz + 2) if high else (0, 0)
        for i in range(3):
            vps[v + i] = jnp.zeros((nx, ny), jnp.float32)
            tis[v + i] = jnp.zeros((nx, ny), jnp.int32)
        for i in range(2):
            c0[c + i, inside, :] = jnp.zeros((nx, ny), jnp.float32)

    @pl.when(g == 0)
    def _():
        blank(False)

    @pl.when(g == n_gz - 1)
    def _():
        blank(True)

    cond, leak, inverse = scalar_tables(cond_ref, leak_ref)
    x_part, y_part = scal[0, 0], scal[1, 0]
    hinder = TIME_STEP * hinder_ref[0]
    diffuse = TIME_STEP * diffuse_ref[0]
    rate = [TIME_STEP * bind_ref[0, i] for i in range(3)]
    second = [k * l * i for k, l, i in zip(cond, leak, inverse)]
    z_part = [x_part * l * i for l, i in zip(leak, inverse)]
    n_part = [y_part * k * i for k, i in zip(cond, inverse)]
    lane = lax.broadcasted_iota(jnp.int32, (rows, ny), 1)
    first_lane, last_lane = lane == 0, lane == ny - 1
    diffuse_low = jnp.where(first_lane, 0.0, diffuse)
    diffuse_high = jnp.where(last_lane, 0.0, diffuse)
    starts = range(0, nx, rows)

    def scale(p):
        for r in starts:
            block = pl.ds(r, rows)
            (t2,) = select(tis[p + 3, block, :], [second])
            qs[p + 3, pl.ds(EDGE + r, rows), :] = t2 * vps[p + 3, block, :]

    def press(p):
        for r in starts:
            block = pl.ds(r, rows)
            here = pl.ds(EDGE + r, rows)
            k, zp, npart = select(tis[p + 3, block, :], [cond, z_part, n_part])
            q = qs[p + 3, here, :]
            total = qs[p + 2, here, :] + qs[p + 4, here, :]
            total = total + qs[p + 3, pl.ds(EDGE + r - 1, rows), :] + qs[p + 3, pl.ds(EDGE + r + 1, rows), :]
            total = total + jnp.where(first_lane, 0.0, pltpu.roll(q, 1, 1)) + jnp.where(last_lane, 0.0, pltpu.roll(q, ny - 1, 1))
            ps[p + 2, here, :] = zp * vps[p + 3, block, :] + npart * total
            ks[p + 2, here, :] = k

        @pl.when(((p < 0) & (g == 0)) | ((p >= nz) & (g == n_gz - 1)))
        def _():
            ks[p + 2, inside, :] = jnp.zeros((nx, ny), jnp.float32)

    def z_face(p, r):
        here = pl.ds(EDGE + r, rows)
        k, press_here = ks[p + 2, here, :] * hinder, ps[p + 2, here, :]
        w = k * ks[p + 3, here, :] * (press_here - ps[p + 3, here, :])
        return k, press_here, w

    def faces(p, slot, before):
        for r in starts:
            block = pl.ds(r, rows)
            here = pl.ds(EDGE + r, rows)
            k, press_here, w = z_face(p, r)
            a = jnp.maximum(w, 0.0) + diffuse
            b = a - w
            coef_z[slot, 0, block, :] = a
            coef_z[slot, 1, block, :] = b
            after = pl.ds(EDGE + r + 1, rows)
            w_x = k * ks[p + 2, after, :] * (press_here - ps[p + 2, after, :])
            wx[here, :] = w_x
            a_x = jnp.maximum(w_x, 0.0) + diffuse
            b_x = a_x - w_x
            w_low = wx[pl.ds(EDGE + r - 1, rows), :]
            a_x_low = jnp.maximum(w_low, 0.0) + diffuse
            b_x_low = a_x_low - w_low
            k_here = ks[p + 2, here, :]
            w_y = k * pltpu.roll(k_here, ny - 1, 1) * (press_here - pltpu.roll(press_here, ny - 1, 1))
            w_y = jnp.where(last_lane, 0.0, w_y)
            up = jnp.maximum(w_y, 0.0)
            a_y = up + diffuse
            b_y = (up - w_y) + diffuse_high
            w_low = pltpu.roll(w_y, 1, 1)
            up = jnp.maximum(w_low, 0.0)
            a_y_low = up + diffuse_low
            b_y_low = (up - w_low) + diffuse
            (bind,) = select(tis[p + 3, block, :], [rate])
            centre = (a + a_x) + (a_y + b_x_low) + (b_y_low + coef_z[before, 1, block, :]) + bind
            coefs[slot, 0, block, :] = 1.0 - centre
            coefs[slot, 1, block, :] = a_x_low
            coefs[slot, 2, block, :] = b_x
            coefs[slot, 3, block, :] = a_y_low
            coefs[slot, 4, block, :] = b_y

    def advance(src, p, slot, before, r):
        block = pl.ds(r, rows)
        here = pl.ds(EDGE + r, rows)
        c = src[p + 2, here, :]
        value = coefs[slot, 0, block, :] * c
        value = value + coef_z[slot, 1, block, :] * src[p + 3, here, :] + coef_z[before, 0, block, :] * src[p + 1, here, :]
        value = value + coefs[slot, 1, block, :] * src[p + 2, pl.ds(EDGE + r - 1, rows), :]
        value = value + coefs[slot, 2, block, :] * src[p + 2, pl.ds(EDGE + r + 1, rows), :]
        value = value + coefs[slot, 3, block, :] * pltpu.roll(c, 1, 1)
        value = value + coefs[slot, 4, block, :] * pltpu.roll(c, ny - 1, 1)
        return c, value

    def first_step(p, slot, before):
        for r in starts:
            _, value = advance(c0, p, slot, before, r)
            c1[p + 2, pl.ds(EDGE + r, rows), :] = value

        @pl.when(((p < 0) & (g == 0)) | ((p >= nz) & (g == n_gz - 1)))
        def _():
            c1[p + 2, inside, :] = jnp.zeros((nx, ny), jnp.float32)

    def second_step(p, slot, before):
        for r in starts:
            block = pl.ds(r, rows)
            c, value = advance(c1, p, slot, before, r)
            out[p, block, :] = value
            (bind,) = select(tis[p + 3, block, :], [rate])
            bnd[p, block, :] = bnd[p, block, :] + bind * (c0[p + 2, pl.ds(EDGE + r, rows), :] + c)

    def out_copies(i):
        z0 = pl.ds(i * chunk, chunk)
        return [
            pltpu.make_async_copy(out.at[z0], free_out.at[z0], out_sems.at[i, 0]),
            pltpu.make_async_copy(bnd.at[z0], bound_out.at[z0], out_sems.at[i, 1]),
        ]

    @pl.when(has_low)
    def _():
        each(halo_copies(False), "wait")

    each(chunk_copies(0), "wait")

    for p in range(-3, 1):
        scale(p)
    for p in (-2, -1):
        press(p)
    for r in starts:
        w = z_face(-2, r)[2]
        a = jnp.maximum(w, 0.0) + diffuse
        coef_z[1, 0, pl.ds(r, rows), :] = a
        coef_z[1, 1, pl.ds(r, rows), :] = a - w
    scale(1)
    press(0)
    faces(-1, 2, 1)
    first_step(-1, 2, 1)

    def body(p, _):
        slot, before, older = lax.rem(p, 3), lax.rem(p + 2, 3), lax.rem(p + 1, 3)
        group = lax.div(p + 2, chunk)

        @pl.when((lax.rem(p + 2, chunk) == 0) & (group < n_chunks))
        def _():
            each(chunk_copies(group), "wait")

        @pl.when((p == nz - 2) & has_high)
        def _():
            each(halo_copies(True), "wait")

        scale(p + 2)
        press(p + 1)
        faces(p, slot, before)
        first_step(p, slot, before)

        @pl.when(p > 0)
        def _():
            second_step(p - 1, before, older)

        @pl.when((p > 0) & (lax.rem(p, chunk) == 0))
        def _():
            each(out_copies(lax.div(p, chunk) - 1), "start")

        return 0

    lax.fori_loop(0, nz + 1, body, 0)
    own = pltpu.make_async_copy(
        ps.at[pl.ds(2, nz), pl.ds(pl.multiple_of(EDGE + s * bx, 8), bx)], pressure, pressure_sem)
    own.start()
    for i in range(n_chunks):
        each(out_copies(i), "wait")
    own.wait()


def transport(n_gz, bx, cond_table, leak_table, bind_table, hindrance, diffusivity, scal, slab, tissue, thalo, conc, chalo, bound):
    nz, nx, ny = conc.shape
    anywhere = pl.BlockSpec(memory_space=pl.ANY)
    scalars = pl.BlockSpec(memory_space=pltpu.SMEM)
    hbm = pl.BlockSpec(memory_space=pltpu.HBM)
    wide = nx + 2 * EDGE
    f32 = jnp.float32
    dma = pltpu.SemaphoreType.DMA
    n_chunks = nz // 8
    return pl.pallas_call(
        functools.partial(transport_kernel, n_gz),
        out_shape=(
            jax.ShapeDtypeStruct((nz, bx, ny), f32),
            jax.ShapeDtypeStruct((nz, nx, ny), f32),
            jax.ShapeDtypeStruct((nz, nx, ny), f32),
        ),
        in_specs=[scalars] * 5 + [pl.BlockSpec(memory_space=pltpu.VMEM), anywhere, hbm, anywhere, hbm, anywhere, hbm],
        out_specs=(anywhere, anywhere, anywhere),
        scratch_shapes=[
            pltpu.VMEM((nz + 6, nx, ny), f32),
            pltpu.VMEM((nz + 6, nx, ny), jnp.int32),
            pltpu.VMEM((nz + 4, wide, ny), f32),
            pltpu.VMEM((nz + 4, wide, ny), f32),
            pltpu.VMEM((nz, nx, ny), f32),
            pltpu.VMEM((nz, nx, ny), f32),
            pltpu.VMEM((nz + 6, wide, ny), f32),
            pltpu.VMEM((nz + 4, wide, ny), f32),
            pltpu.VMEM((nz + 4, wide, ny), f32),
            pltpu.VMEM((3, 2, nx, ny), f32),
            pltpu.VMEM((wide, ny), f32),
            pltpu.VMEM((3, 5, nx, ny), f32),
            dma((n_chunks + 2, 4)),
            dma((n_chunks, 2)),
            dma,
        ],
        compiler_params=pltpu.CompilerParams(vmem_limit_bytes=60 << 20),
        name="transport",
    )(cond_table, leak_table, bind_table, hindrance, diffusivity, scal, slab, tissue, thalo, conc, chalo, bound)


def solution(mesh):
    n_size, n_gz = mesh.shape["size"], mesh.shape["gz"]

    def local(tissue, vessel_pressure, cond_table, leak_table, bind_table, hindrance, diffusivity, free_conc, bound_conc):
        conc, bound = free_conc[0], bound_conc[0]
        slab, thalo, chalo, scal = exchange(n_size, n_gz, cond_table, leak_table, vessel_pressure, tissue, conc)
        pressure, free, held = transport(
            n_gz, vessel_pressure.shape[1], cond_table, leak_table, bind_table, hindrance, diffusivity,
            scal, slab, tissue, thalo, conc, chalo, bound)
        return pressure, free[None], held[None]

    return jax.shard_map(
        local,
        mesh=mesh,
        in_specs=(
            P("gz", None, None), P("gz", "size", None), P(), P(), P("size", None), P("size"), P("size"),
            P("size", "gz", None, None), P("size", "gz", None, None),
        ),
        out_specs=(P("gz", "size", None), P("size", "gz", None, None), P("size", "gz", None, None)),
        check_vma=False,
    )
```

```python
import functools

import jax
import jax.numpy as jnp
from jax import lax
from jax.experimental import pallas as pl
from jax.experimental.pallas import tpu as pltpu
from jax.sharding import PartitionSpec as P

MESH = pl.DeviceIdType.MESH
TIME_STEP = 0.1
EDGE = 8
CHUNKS = 4


def each(copies, what):
    for copy in copies:
        getattr(copy, what)()


def select(labels, values):
    first, second = labels == 0, labels == 1
    return [jnp.where(first, v[0], jnp.where(second, v[1], v[2])) for v in values]


def two_sum(a, b):
    total = a + b
    part = total - a
    return total, (a - (total - part)) + (b - part)


def split(a):
    wide = 4097.0 * a
    high = wide - (wide - a)
    return high, a - high


def two_prod(a, b):
    product = a * b
    ah, al = split(a)
    bh, bl = split(b)
    return product, ((ah * bh - product) + ah * bl + al * bh) + al * bl


def pair_sub_product(x, a, b):
    p, e = two_prod(a[0], b[0])
    e = e + (a[0] * b[1] + a[1] * b[0])
    s, r = two_sum(x[0], -p)
    r = r + (x[1] - e)
    return two_sum(s, r)


def pair_ratio(x, y):
    q = x[0] / y[0]
    rest = pair_sub_product(x, (q, jnp.zeros_like(q)), y)
    return two_sum(q, (rest[0] + rest[1]) / y[0])


def scalar_tables(cond_ref, leak_ref):
    cond = [cond_ref[i] for i in range(3)]
    leak = [leak_ref[i] for i in range(3)]
    inverse = []
    for k, l in zip(cond, leak):
        inverse.append((1.0 / jnp.full((8, 128), 6.0 * k * k + l, jnp.float32))[0, 0])
    return cond, leak, inverse


def lane_neighbours(q, lane, ny):
    up = jnp.where(lane == ny - 1, 0.0, pltpu.roll(q, ny - 1, 1))
    down = jnp.where(lane == 0, 0.0, pltpu.roll(q, 1, 1))
    return up + down


def exchange_kernel(
    n_size, n_gz, cond_ref, leak_ref, vp, tissue, conc,
    slab, thalo, chalo, scal,
    ext, tex, qs, qv, ys, packed_out, packed_in, tile, red_size, red_gz, total_tile,
    local_sem, near_send, near_recv, block_send, block_recv,
    ring_send, ring_recv, grid_send, grid_recv,
):
    s, g = lax.axis_index("size"), lax.axis_index("gz")
    nz, bx, ny = vp.shape
    half = bx // 2
    nx = tissue.shape[1]

    ext[...] = jnp.zeros_like(ext)
    tex[...] = jnp.full_like(tex, 3)

    def remote(src, dst, send, recv, to_s, to_g):
        return pltpu.make_async_remote_copy(
            src_ref=src, dst_ref=dst, send_sem=send, recv_sem=recv,
            device_id={"size": to_s, "gz": to_g}, device_id_type=MESH)

    own_rows = pl.ds(pl.multiple_of(s * bx, 8), bx)

    barrier = pltpu.get_barrier_semaphore()

    def greet(to_s, to_g):
        pl.semaphore_signal(barrier, inc=1, device_id={"size": to_s, "gz": to_g}, device_id_type=MESH)

    greeted = 0
    for j in range(n_size):
        peer = lax.rem(s + j, n_size)
        for d in ((0,) if 1 < j < n_size - 1 else (0, 1, n_gz - 1)):
            if j or d:
                greet(peer, lax.rem(g + d, n_gz))
                greeted += 1
    for j in range(2, n_gz - 1):
        greet(s, lax.rem(g + j, n_gz))
        greeted += 1

    inner = pltpu.make_async_copy(vp, ext.at[pl.ds(2, nz), pl.ds(half, bx)], local_sem.at[0])
    inner.start()
    own = pltpu.make_async_copy(vp, slab.at[pl.ds(3, nz), own_rows], local_sem.at[1])
    own.start()

    wide = bx + 2 * half

    def tissue_rows(which):
        if which == "low":
            return pl.ds(0, bx + half), pl.ds(half, bx + half)
        if which == "high":
            return pl.ds(nx - bx - half, bx + half), pl.ds(0, bx + half)
        return pl.ds(pl.multiple_of(s * bx - half, 8), wide), pl.ds(0, wide)

    cases = (("low", s == 0), ("high", s == n_size - 1), ("mid", (s > 0) & (s < n_size - 1)))

    def tex_copy(which):
        src, dst = tissue_rows(which)
        return pltpu.make_async_copy(tissue.at[:, src], tex.at[pl.ds(2, nz), dst], local_sem.at[2])

    for which, cond in cases:
        @pl.when(cond)
        def _(which=which):
            tex_copy(which).start()

    inner.wait()

    def pack(e, _):
        for i, r in enumerate((half, half + 1, half + bx - 2, half + bx - 1)):
            packed_out[i, pl.ds(e, 1), :] = ext[e + 2, pl.ds(r, 1), :]
        return 0

    lax.fori_loop(0, nz, pack, 0, unroll=4)
    pl.semaphore_wait(barrier, greeted)

    lows, highs = pl.ds(0, half), pl.ds(half, half)
    above, below = pl.ds(half + bx, half), pl.ds(0, half)
    middle = pl.ds(half, bx)
    has_low, has_high = g > 0, g < n_gz - 1
    x_low, x_high = s > 0, s < n_size - 1
    near = [
        (x_high, x_low, packed_out.at[pl.ds(2, 2)], packed_in.at[pl.ds(0, 2)], 0, s + 1, g),
        (x_low, x_high, packed_out.at[pl.ds(0, 2)], packed_in.at[pl.ds(2, 2)], 1, s - 1, g),
        (has_high, has_low, vp.at[pl.ds(nz - 2, 2)], ext.at[pl.ds(0, 2), middle], 2, s, g + 1),
        (has_low, has_high, vp.at[pl.ds(0, 2)], ext.at[pl.ds(nz + 2, 2), middle], 3, s, g - 1),
        (x_high & has_high, x_low & has_low, vp.at[pl.ds(nz - 1, 1), highs], ext.at[pl.ds(1, 1), below], 4, s + 1, g + 1),
        (x_low & has_high, x_high & has_low, vp.at[pl.ds(nz - 1, 1), lows], ext.at[pl.ds(1, 1), above], 5, s - 1, g + 1),
        (x_high & has_low, x_low & has_high, vp.at[pl.ds(0, 1), highs], ext.at[pl.ds(nz + 2, 1), below], 6, s + 1, g - 1),
        (x_low & has_low, x_high & has_high, vp.at[pl.ds(0, 1), lows], ext.at[pl.ds(nz + 2, 1), above], 7, s - 1, g - 1),
    ]
    for which, cond in cases:
        src, dst = tissue_rows(which)
        near.append((has_high & cond, has_low & cond, tissue.at[pl.ds(nz - 2, 2), src], tex.at[pl.ds(0, 2), dst], 8, s, g + 1))
        near.append((has_low & cond, has_high & cond, tissue.at[pl.ds(0, 2), src], tex.at[pl.ds(nz + 2, 2), dst], 9, s, g - 1))
    late = [
        (has_high, has_low, tissue.at[pl.ds(nz - 3, 3)], thalo.at[pl.ds(0, 3)], 10, s, g + 1),
        (has_low, has_high, tissue.at[pl.ds(0, 3)], thalo.at[pl.ds(3, 3)], 11, s, g - 1),
        (has_high, has_low, conc.at[pl.ds(nz - 2, 2)], chalo.at[pl.ds(0, 2)], 12, s, g + 1),
        (has_low, has_high, conc.at[pl.ds(0, 2)], chalo.at[pl.ds(2, 2)], 13, s, g - 1),
    ]

    def start_all(copies):
        for cond, _, src, dst, i, to_s, to_g in copies:
            @pl.when(cond)
            def _(src=src, dst=dst, i=i, to_s=to_s, to_g=to_g):
                remote(src, dst, near_send.at[i], near_recv.at[i], to_s, to_g).start()

    def wait_all(copies):
        for sent, cond, src, dst, i, to_s, to_g in copies:
            @pl.when(cond)
            def _(src=src, dst=dst, i=i):
                remote(src, dst, near_send.at[i], near_recv.at[i], s, g).wait_recv()

            @pl.when(sent)
            def _(src=src, dst=dst, i=i):
                remote(src, dst, near_send.at[i], near_recv.at[i], s, g).wait_send()

    start_all(near)

    n_z = n_size // 2
    z, x = lax.div(s, 2), lax.rem(s, 2)
    z_up, z_down, z_far = lax.rem(z + 1, n_z), lax.rem(z + n_z - 1, n_z), lax.rem(z + 2, n_z)
    across = 2 * z + 1 - x
    up, down, far = 2 * z_up + x, 2 * z_down + x, 2 * z_far + x
    up_across, down_across, far_across = 2 * z_up + 1 - x, 2 * z_down + 1 - x, 2 * z_far + 1 - x
    depth = nz // CHUNKS
    part = depth // 2
    order = [0, CHUNKS - 1, *range(1, CHUNKS - 1)]

    def piece(block, c, kind, to, first=0, count=depth, own=False):
        planes = pl.ds(3 + c * depth + first, count)
        where = pl.ds(pl.multiple_of(block * bx, 8), bx)
        src = vp.at[pl.ds(c * depth + first, count)] if own else slab.at[planes, where]
        return remote(src, slab.at[planes, where], block_send.at[kind, c], block_recv.at[kind, c], to, g)

    def own_pieces(c):
        return [piece(s, c, 0, across, own=True), piece(s, c, 1, up, own=True), piece(s, c, 2, down, own=True)]

    def from_across(c):
        return [piece(across, c, 3, up), piece(across, c, 4, down)]

    def from_down(c):
        return [piece(down, c, 5, up, 0, part)]

    def from_up(c):
        return [piece(up, c, 6, down, part, depth - part)]

    def from_far(c):
        return [piece(far, c, 7, across)]

    def hand_on(c):
        piece(across, c, 0, s).wait_recv()
        each(from_across(c), "start")
        piece(down, c, 1, s).wait_recv()
        each(from_down(c), "start")
        piece(up, c, 2, s).wait_recv()
        each(from_up(c), "start")

    def hand_far(c):
        piece(far, c, 5, s, 0, part).wait_recv()
        piece(far, c, 6, s, part, depth - part).wait_recv()
        each(from_far(c), "start")

    def finish(c):
        piece(down_across, c, 3, s).wait_recv()
        piece(up_across, c, 4, s).wait_recv()
        piece(far_across, c, 7, s).wait_recv()

    for c in order:
        each(own_pieces(c), "start")
    start_all(late)

    edges = [
        (has_high, has_low, slab.at[pl.ds(nz, 3)], slab.at[pl.ds(0, 3)], 14, s, g + 1),
        (has_low, has_high, slab.at[pl.ds(3, 3)], slab.at[pl.ds(nz + 3, 3)], 15, s, g - 1),
    ]

    cond, leak, inverse = scalar_tables(cond_ref, leak_ref)
    first = [l * i for l, i in zip(leak, inverse)]
    second = [k * l * i for k, l, i in zip(cond, leak, inverse)]
    lane = lax.broadcasted_iota(jnp.int32, (wide, ny), 1)

    for which, c in cases:
        @pl.when(c)
        def _(which=which):
            tex_copy(which).wait()
    wait_all(near)

    def unpack(low):
        def rows_in(e, _):
            for i in range(2):
                r = half - 2 + i if low else half + bx + i
                ext[e + 2, pl.ds(r, 1), :] = packed_in[i if low else 2 + i, pl.ds(e, 1), :]
            return 0
        lax.fori_loop(0, nz, rows_in, 0, unroll=4)

    @pl.when(x_low)
    def _():
        unpack(True)

    @pl.when(x_high)
    def _():
        unpack(False)

    def scale(e, _):
        (t2,) = select(tex[e], [second])
        qs[e] = t2 * ext[e]
        return 0

    lax.fori_loop(0, nz + 4, scale, 0, unroll=4)
    hand_on(order[0])

    def stencil(ref, e):
        q = ref[e]
        total = ref[e - 1] + ref[e + 1] + pltpu.roll(q, 1, 0) + pltpu.roll(q, wide - 1, 0)
        return 6.0 * q - (total + lane_neighbours(q, lane, ny))

    def add_product(acc, a, b):
        h, r = two_sum(acc[0], a[1] * b[1])
        return h, acc[1] + ((a[1] * b[2] + a[2] * b[0]) + r)

    def apply(e):
        labels = tex[e]
        k, l, i, t1 = select(labels, [cond, leak, inverse, first])
        k = jnp.where(labels == 3, 0.0, k)
        field = ext[e]
        z = t1 * field
        az = l * z + k * stencil(qs, e)
        y = i * az
        qv[e] = k * y
        ys[e] = y
        return l * field, z, az, y

    def mine(x):
        x = x[half:half + bx]
        return (x, *split(x))

    def first_sums(e, accs):
        r0, z, az, y = (mine(x) for x in apply(e))
        return (add_product(accs[0], r0, z), add_product(accs[1], z, az), add_product(accs[2], y, az))

    apply(1)
    apply(nz + 2)
    zero = jnp.zeros((bx, ny), jnp.float32)
    sums = lax.fori_loop(2, nz + 2, first_sums, ((zero, zero),) * 3, unroll=2)
    hand_on(order[1])
    hand_far(order[0])

    def last_sum(e, acc):
        labels = tex[e]
        k, l = select(labels, [cond, leak])
        y = ys[e]
        ay = l * y + k * stencil(qv, e)
        return add_product(acc, mine(y), mine(ay))

    sums = (*sums, lax.fori_loop(2, nz + 2, last_sum, (zero, zero), unroll=4))

    row = lax.broadcasted_iota(jnp.int32, (8, ny), 0)
    packed = jnp.zeros((8, ny), jnp.float32)
    for m, (h, l) in enumerate(sums):
        hs, ls = h[0:8], l[0:8]
        for r in range(8, bx, 8):
            hs, e = two_sum(hs, h[r:r + 8])
            ls = ls + l[r:r + 8] + e
        for shift in (4, 2, 1):
            hs, e = two_sum(hs, pltpu.roll(hs, shift, 0))
            ls = ls + pltpu.roll(ls, shift, 0) + e
        packed = jnp.where(row == m, hs, jnp.where(row == m + 4, ls, packed))
    tile[...] = packed

    def add_tiles(parts):
        total, errors = parts[0], jnp.zeros((8, ny), jnp.float32)
        for part in parts[1:]:
            total, e = two_sum(total, part)
            errors = errors + e
        return total + pltpu.roll(jnp.where(row < 4, errors, 0.0), 4, 0)

    def reduce(src, slots, index, count, axis, send, recv, between):
        for j in range(1, count):
            to = lax.rem(index + j, count)
            dev = (to, g) if axis == "size" else (s, to)
            remote(src, slots.at[index], send, recv, *dev).start()
        between()
        arrived = slots.at[pl.ds(0, count - 1)]
        remote(arrived, arrived, send, recv, s, g).wait()
        slots[index] = src[...]
        return add_tiles([slots[i] for i in range(count)])

    def first_half():
        hand_on(order[2])
        hand_far(order[1])

    def second_half():
        hand_on(order[3])
        hand_far(order[2])

    total_tile[...] = reduce(tile, red_size, s, n_size, "size", ring_send, ring_recv, first_half)
    total = reduce(total_tile, red_gz, g, n_gz, "gz", grid_send, grid_recv, second_half)

    errors = jnp.zeros_like(total)
    shift = ny // 2
    while shift:
        total, e = two_sum(total, pltpu.roll(total, shift, 1))
        errors = errors + pltpu.roll(errors, shift, 1) + e
        shift //= 2
    lower = pltpu.roll(total, 4, 0) + errors
    b = [(total[m:m + 1], lower[m:m + 1]) for m in range(4)]
    t = pair_ratio(b[1], b[0])
    v = pair_sub_product(b[2], t, b[1])
    w = pair_sub_product(pair_sub_product(b[3], t, b[2]), t, v)
    b0, b1, v, w, t = b[0][0], b[1][0], v[0], w[0], t[0]
    det = b1 * w - v * v
    x_part = b0 * w / det
    y_part = -(b0 * v) / det
    scal[...] = jnp.where(row == 0, x_part + y_part * (1.0 - t), -y_part)

    own.wait()
    for c in order[:2]:
        finish(c)
    start_all(edges)
    hand_far(order[3])
    for c in order[2:]:
        finish(c)
    for c in order:
        each(own_pieces(c) + from_across(c) + from_down(c) + from_up(c) + from_far(c), "wait_send")
    wait_all(late)
    wait_all(edges)


def exchange(n_size, n_gz, cond_table, leak_table, vp, tissue, conc):
    nz, bx, ny = vp.shape
    nx = tissue.shape[1]
    anywhere = pl.BlockSpec(memory_space=pl.ANY)
    scalars = pl.BlockSpec(memory_space=pltpu.SMEM)
    vmem = pl.BlockSpec(memory_space=pltpu.VMEM)
    hbm = pl.BlockSpec(memory_space=pltpu.HBM)
    dma = pltpu.SemaphoreType.DMA
    return pl.pallas_call(
        functools.partial(exchange_kernel, n_size, n_gz),
        out_shape=(
            jax.ShapeDtypeStruct((nz + 6, nx, ny), jnp.float32),
            jax.ShapeDtypeStruct((6, nx, ny), jnp.int32),
            jax.ShapeDtypeStruct((4, nx, ny), jnp.float32),
            jax.ShapeDtypeStruct((8, ny), jnp.float32),
        ),
        in_specs=[scalars, scalars, hbm, hbm, hbm],
        out_specs=(anywhere, anywhere, anywhere, pl.BlockSpec(memory_space=pltpu.VMEM)),
        scratch_shapes=[
            pltpu.VMEM((nz + 4, 2 * bx, ny), jnp.float32),
            pltpu.VMEM((nz + 4, 2 * bx, ny), jnp.int32),
            pltpu.VMEM((nz + 4, 2 * bx, ny), jnp.float32),
            pltpu.VMEM((nz + 4, 2 * bx, ny), jnp.float32),
            pltpu.VMEM((nz + 4, 2 * bx, ny), jnp.float32),
            pltpu.VMEM((4, nz, ny), jnp.float32),
            pltpu.VMEM((4, nz, ny), jnp.float32),
            pltpu.VMEM((8, ny), jnp.float32),
            pltpu.VMEM((n_size, 8, ny), jnp.float32),
            pltpu.VMEM((n_gz, 8, ny), jnp.float32),
            pltpu.VMEM((8, ny), jnp.float32),
            dma((3,)),
            dma((16,)), dma((16,)),
            dma((8, CHUNKS)), dma((8, CHUNKS)),
            dma, dma, dma, dma,
        ],
        compiler_params=pltpu.CompilerParams(collective_id=0, has_side_effects=True, vmem_limit_bytes=16 << 20),
        name="exchange",
    )(cond_table, leak_table, vp, tissue, conc)


def transport_kernel(
    n_gz, cond_ref, leak_ref, bind_ref, hinder_ref, diffuse_ref, scal, slab, tissue, thalo, conc, chalo, bound,
    pressure, free_out, bound_out,
    c0, c1, bnd, out, qs, ps, ks, flow_x, flow, coefs, sems, out_sems, pressure_sem,
):
    s, g = lax.axis_index("size"), lax.axis_index("gz")
    nz, nx, ny = conc.shape
    bx = pressure.shape[1]
    rows = 64 if nx % 64 == 0 else nx
    chunk = 8
    n_chunks = nz // chunk
    has_low, has_high = g > 0, g < n_gz - 1
    inside = pl.ds(EDGE, nx)

    def chunk_copies(i):
        z0 = i * chunk
        return [
            pltpu.make_async_copy(conc.at[pl.ds(z0, chunk)], c0.at[pl.ds(z0 + 2, chunk), inside], sems.at[i, 0]),
            pltpu.make_async_copy(bound.at[pl.ds(z0, chunk)], bnd.at[pl.ds(z0, chunk)], sems.at[i, 1]),
        ]

    def halo_copies(high):
        i, c = n_chunks + int(high), nz + 2 if high else 0
        return [
            pltpu.make_async_copy(chalo.at[pl.ds(2 * high, 2)], c0.at[pl.ds(c, 2), inside], sems.at[i, 0]),
        ]

    @pl.when(has_low)
    def _():
        each(halo_copies(False), "start")

    for i in range(n_chunks):
        each(chunk_copies(i), "start")

    @pl.when(has_high)
    def _():
        each(halo_copies(True), "start")

    edge_rows = jnp.zeros((EDGE, ny), jnp.float32)

    def clear(i, _):
        for ref in (c0, c1, qs, ps, ks):
            ref[i, pl.ds(0, EDGE), :] = edge_rows
            ref[i, pl.ds(EDGE + nx, EDGE), :] = edge_rows
        return 0

    lax.fori_loop(0, nz + 4, clear, 0)
    for i in (nz + 4, nz + 5):
        qs[i, pl.ds(0, EDGE), :] = edge_rows
        qs[i, pl.ds(EDGE + nx, EDGE), :] = edge_rows
    for i in range(2):
        flow_x[i, pl.ds(0, EDGE), :] = edge_rows

    def blank(high):
        c = nz + 2 if high else 0
        for i in range(2):
            c0[c + i, inside, :] = jnp.zeros((nx, ny), jnp.float32)

    @pl.when(g == 0)
    def _():
        blank(False)

    @pl.when(g == n_gz - 1)
    def _():
        blank(True)

    cond, leak, inverse = scalar_tables(cond_ref, leak_ref)
    x_part, y_part = scal[0, 0], scal[1, 0]
    hinder = TIME_STEP * hinder_ref[0]
    diffuse = TIME_STEP * diffuse_ref[0]
    rate = [TIME_STEP * bind_ref[0, i] for i in range(3)]
    second = [k * l * i for k, l, i in zip(cond, leak, inverse)]
    z_part = [x_part * l * i for l, i in zip(leak, inverse)]
    n_part = [y_part * k * i for k, i in zip(cond, inverse)]
    lane = lax.broadcasted_iota(jnp.int32, (rows, ny), 1)
    first_lane, last_lane = lane == 0, lane == ny - 1
    diffuse_low = jnp.where(first_lane, 0.0, diffuse)
    diffuse_high = jnp.where(last_lane, 0.0, diffuse)
    starts = range(0, nx, rows)

    def kind(p, block):
        if isinstance(p, int) and p < 0:
            return thalo[p + 3, block, :]
        if isinstance(p, int) and p >= nz:
            return thalo[p - nz + 3, block, :]
        return tissue[p, block, :]

    def field(p, block):
        value = slab[p + 3, block, :]
        if isinstance(p, int) and (p < 0 or p >= nz):
            value = jnp.where(has_low if p < 0 else has_high, value, 0.0)
        return value

    def scale(p):
        for r in starts:
            block = pl.ds(r, rows)
            (t2,) = select(kind(p, block), [second])
            qs[p + 3, pl.ds(EDGE + r, rows), :] = t2 * field(p, block)

    def press(p):
        for r in starts:
            block = pl.ds(r, rows)
            here = pl.ds(EDGE + r, rows)
            k, zp, npart = select(kind(p, block), [cond, z_part, n_part])
            q = qs[p + 3, here, :]
            total = qs[p + 2, here, :] + qs[p + 4, here, :]
            total = total + qs[p + 3, pl.ds(EDGE + r - 1, rows), :] + qs[p + 3, pl.ds(EDGE + r + 1, rows), :]
            total = total + jnp.where(first_lane, 0.0, pltpu.roll(q, 1, 1)) + jnp.where(last_lane, 0.0, pltpu.roll(q, ny - 1, 1))
            ps[p + 2, here, :] = zp * field(p, block) + npart * total
            ks[p + 2, here, :] = k

    def outside(p, ref):
        if isinstance(p, int) and (p < 0 or p >= nz):
            @pl.when(g == (0 if p < 0 else n_gz - 1))
            def _():
                ref[p + 2, inside, :] = jnp.zeros((nx, ny), jnp.float32)

    def flows(p):
        slot = lax.rem(p + 4, 2)
        for r in starts:
            block = pl.ds(r, rows)
            here = pl.ds(EDGE + r, rows)
            after = pl.ds(EDGE + r + 1, rows)
            k_here, press_here = ks[p + 2, here, :], ps[p + 2, here, :]
            k = k_here * hinder
            flow[slot, 0, block, :] = k * ks[p + 3, here, :] * (press_here - ps[p + 3, here, :])
            flow_x[slot, here, :] = k * ks[p + 2, after, :] * (press_here - ps[p + 2, after, :])
            w_y = k * pltpu.roll(k_here, ny - 1, 1) * (press_here - pltpu.roll(press_here, ny - 1, 1))
            flow[slot, 1, block, :] = jnp.where(last_lane, 0.0, w_y)

    def first_step(p):
        slot, source, before = lax.rem(p + 4, 4), lax.rem(p + 4, 2), lax.rem(p + 3, 4)
        for r in starts:
            block = pl.ds(r, rows)
            here = pl.ds(EDGE + r, rows)
            w = flow[source, 0, block, :]
            a = jnp.maximum(w, 0.0) + diffuse
            b = a - w
            w_x = flow_x[source, here, :]
            a_x = jnp.maximum(w_x, 0.0) + diffuse
            b_x = a_x - w_x
            w_low = flow_x[source, pl.ds(EDGE + r - 1, rows), :]
            a_x_low = jnp.maximum(w_low, 0.0) + diffuse
            b_x_low = a_x_low - w_low
            w_y = flow[source, 1, block, :]
            up = jnp.maximum(w_y, 0.0)
            a_y = up + diffuse
            b_y = (up - w_y) + diffuse_high
            w_low = pltpu.roll(w_y, 1, 1)
            up = jnp.maximum(w_low, 0.0)
            a_y_low = up + diffuse_low
            b_y_low = (up - w_low) + diffuse
            (bind,) = select(kind(p, block), [rate])
            centre = (a + a_x) + (a_y + b_x_low) + (b_y_low + coefs[before, 6, block, :]) + bind
            centre = 1.0 - centre
            for i, value in enumerate((centre, a_x_low, b_x, a_y_low, b_y, a, b)):
                coefs[slot, i, block, :] = value
            c = c0[p + 2, here, :]
            value = centre * c + (b * c0[p + 3, here, :] + coefs[before, 5, block, :] * c0[p + 1, here, :])
            value = value + (a_x_low * c0[p + 2, pl.ds(EDGE + r - 1, rows), :] + b_x * c0[p + 2, pl.ds(EDGE + r + 1, rows), :])
            value = value + (a_y_low * pltpu.roll(c, 1, 1) + b_y * pltpu.roll(c, ny - 1, 1))
            c1[p + 2, here, :] = value

    def second_step(p):
        slot, before = lax.rem(p + 4, 4), lax.rem(p + 3, 4)
        for r in starts:
            block = pl.ds(r, rows)
            here = pl.ds(EDGE + r, rows)
            c = c1[p + 2, here, :]
            value = coefs[slot, 0, block, :] * c
            value = value + (coefs[slot, 6, block, :] * c1[p + 3, here, :] + coefs[before, 5, block, :] * c1[p + 1, here, :])
            value = value + (coefs[slot, 1, block, :] * c1[p + 2, pl.ds(EDGE + r - 1, rows), :]
                             + coefs[slot, 2, block, :] * c1[p + 2, pl.ds(EDGE + r + 1, rows), :])
            value = value + (coefs[slot, 3, block, :] * pltpu.roll(c, 1, 1) + coefs[slot, 4, block, :] * pltpu.roll(c, ny - 1, 1))
            out[p, block, :] = value
            (bind,) = select(kind(p, block), [rate])
            bnd[p, block, :] = bnd[p, block, :] + bind * (c0[p + 2, here, :] + c)

    def last_copies(i):
        z0 = pl.ds(nz - chunk + i * chunk // 2, chunk // 2)
        return [
            pltpu.make_async_copy(out.at[z0], free_out.at[z0], out_sems.at[n_chunks - 1 + i, 0]),
            pltpu.make_async_copy(bnd.at[z0], bound_out.at[z0], out_sems.at[n_chunks - 1 + i, 1]),
        ]

    def out_copies(i):
        z0 = pl.ds(i * chunk, chunk)
        return [
            pltpu.make_async_copy(out.at[z0], free_out.at[z0], out_sems.at[i, 0]),
            pltpu.make_async_copy(bnd.at[z0], bound_out.at[z0], out_sems.at[i, 1]),
        ]

    def turn(p):
        fixed = isinstance(p, int)
        if not fixed or 0 <= p - 4 < nz:
            second_step(p - 4)
        if not fixed or -1 <= p - 2 <= nz:
            first_step(p - 2)
            outside(p - 2, c1)
        if not fixed or -2 <= p - 1 <= nz:
            flows(p - 1)
        if fixed and p == 0:
            for r in starts:
                block = pl.ds(r, rows)
                w = flow[0, 0, block, :]
                a = jnp.maximum(w, 0.0) + diffuse
                coefs[2, 5, block, :] = a
                coefs[2, 6, block, :] = a - w
        if not fixed or -2 <= p + 1 <= nz + 1:
            press(p + 1)
            outside(p + 1, ks)
        if not fixed or -3 <= p + 3 <= nz + 2:
            scale(p + 3)

    for p in range(-6, 4):
        if p == 1:
            @pl.when(has_low)
            def _():
                each(halo_copies(False), "wait")

            each(chunk_copies(0), "wait")
        turn(p)

    def body(p, _):
        group = lax.div(p + 3, chunk)

        @pl.when((lax.rem(p + 3, chunk) == 0) & (group < n_chunks))
        def _():
            each(chunk_copies(group), "wait")

        turn(p)

        @pl.when((p >= chunk + 3) & (lax.rem(p - 3, chunk) == 0))
        def _():
            each(out_copies(lax.div(p - 3, chunk) - 1), "start")

        return 0

    lax.fori_loop(4, nz - 3, body, 0)

    @pl.when(has_high)
    def _():
        each(halo_copies(True), "wait")

    own = pltpu.make_async_copy(
        ps.at[pl.ds(2, nz), pl.ds(pl.multiple_of(EDGE + s * bx, 8), bx)], pressure, pressure_sem)
    for p in range(nz - 3, nz + 4):
        turn(p)
        if p == nz - 1:
            own.start()
            each(last_copies(0), "start")
    each(last_copies(1), "start")
    for i in range(n_chunks - 1):
        each(out_copies(i), "wait")
    for i in range(2):
        each(last_copies(i), "wait")
    own.wait()


def transport(n_gz, bx, cond_table, leak_table, bind_table, hindrance, diffusivity, scal, slab, tissue, thalo, conc, chalo, bound):
    nz, nx, ny = conc.shape
    anywhere = pl.BlockSpec(memory_space=pl.ANY)
    scalars = pl.BlockSpec(memory_space=pltpu.SMEM)
    vmem = pl.BlockSpec(memory_space=pltpu.VMEM)
    hbm = pl.BlockSpec(memory_space=pltpu.HBM)
    wide = nx + 2 * EDGE
    f32 = jnp.float32
    dma = pltpu.SemaphoreType.DMA
    n_chunks = nz // 8
    return pl.pallas_call(
        functools.partial(transport_kernel, n_gz),
        out_shape=(
            jax.ShapeDtypeStruct((nz, bx, ny), f32),
            jax.ShapeDtypeStruct((nz, nx, ny), f32),
            jax.ShapeDtypeStruct((nz, nx, ny), f32),
        ),
        in_specs=[scalars] * 5 + [vmem] * 4 + [anywhere, anywhere, hbm],
        out_specs=(anywhere, anywhere, anywhere),
        scratch_shapes=[
            pltpu.VMEM((nz + 4, wide, ny), f32),
            pltpu.VMEM((nz + 4, wide, ny), f32),
            pltpu.VMEM((nz, nx, ny), f32),
            pltpu.VMEM((nz, nx, ny), f32),
            pltpu.VMEM((nz + 6, wide, ny), f32),
            pltpu.VMEM((nz + 4, wide, ny), f32),
            pltpu.VMEM((nz + 4, wide, ny), f32),
            pltpu.VMEM((2, wide, ny), f32),
            pltpu.VMEM((2, 2, nx, ny), f32),
            pltpu.VMEM((4, 7, nx, ny), f32),
            dma((n_chunks + 2, 2)),
            dma((n_chunks + 1, 2)),
            dma,
        ],
        compiler_params=pltpu.CompilerParams(vmem_limit_bytes=36 << 20),
        name="transport",
    )(cond_table, leak_table, bind_table, hindrance, diffusivity, scal, slab, tissue, thalo, conc, chalo, in_hbm(bound))


def in_hbm(array):
    return pltpu.with_memory_space_constraint(array, pltpu.HBM)


def solution(mesh):
    n_size, n_gz = mesh.shape["size"], mesh.shape["gz"]

    def local(tissue, vessel_pressure, cond_table, leak_table, bind_table, hindrance, diffusivity, free_conc, bound_conc):
        conc, bound = free_conc[0], bound_conc[0]
        slab, thalo, chalo, scal = exchange(
            n_size, n_gz, *(in_hbm(v) for v in (cond_table, leak_table, vessel_pressure, tissue, conc)))
        pressure, free, held = transport(
            n_gz, vessel_pressure.shape[1], *(in_hbm(v) for v in (cond_table, leak_table, bind_table)), hindrance, diffusivity,
            scal, slab, tissue, thalo, conc, chalo, in_hbm(bound))
        return pressure, free[None], held[None]

    return jax.shard_map(
        local,
        mesh=mesh,
        in_specs=(
            P("gz", None, None), P("gz", "size", None), P(), P(), P("size", None), P("size"), P("size"),
            P("size", "gz", None, None), P("size", "gz", None, None),
        ),
        out_specs=(P("gz", "size", None), P("size", "gz", None, None), P("size", "gz", None, None)),
        check_vma=False,
    )
```

```python
import functools

import jax
import jax.numpy as jnp
from jax import lax
from jax.experimental import pallas as pl
from jax.experimental.pallas import tpu as pltpu
from jax.sharding import PartitionSpec as P

MESH = pl.DeviceIdType.MESH
TIME_STEP = 0.1
EDGE = 8
CHUNKS = 4


def each(copies, what):
    for copy in copies:
        getattr(copy, what)()


def select(labels, values):
    first, second = labels == 0, labels == 1
    return [jnp.where(first, v[0], jnp.where(second, v[1], v[2])) for v in values]


def two_sum(a, b):
    total = a + b
    part = total - a
    return total, (a - (total - part)) + (b - part)


def split(a):
    wide = 4097.0 * a
    high = wide - (wide - a)
    return high, a - high


def two_prod(a, b):
    product = a * b
    ah, al = split(a)
    bh, bl = split(b)
    return product, ((ah * bh - product) + ah * bl + al * bh) + al * bl


def pair_sub_product(x, a, b):
    p, e = two_prod(a[0], b[0])
    e = e + (a[0] * b[1] + a[1] * b[0])
    s, r = two_sum(x[0], -p)
    r = r + (x[1] - e)
    return two_sum(s, r)


def pair_ratio(x, y):
    q = x[0] / y[0]
    rest = pair_sub_product(x, (q, jnp.zeros_like(q)), y)
    return two_sum(q, (rest[0] + rest[1]) / y[0])


def scalar_tables(cond_ref, leak_ref):
    cond = [cond_ref[i] for i in range(3)]
    leak = [leak_ref[i] for i in range(3)]
    inverse = []
    for k, l in zip(cond, leak):
        inverse.append((1.0 / jnp.full((8, 128), 6.0 * k * k + l, jnp.float32))[0, 0])
    return cond, leak, inverse


def lane_neighbours(q, lane, ny):
    up = jnp.where(lane == ny - 1, 0.0, pltpu.roll(q, ny - 1, 1))
    down = jnp.where(lane == 0, 0.0, pltpu.roll(q, 1, 1))
    return up + down


def exchange_kernel(
    n_size, n_gz, cond_ref, leak_ref, vp, tissue, conc,
    slab, thalo, chalo, scal,
    ext, tex, qs, qv, ys, packed_out, packed_in, tile, red_size, red_gz, total_tile,
    local_sem, near_send, near_recv, block_send, block_recv,
    ring_send, ring_recv, grid_send, grid_recv,
):
    s, g = lax.axis_index("size"), lax.axis_index("gz")
    nz, bx, ny = vp.shape
    half = bx // 2
    nx = tissue.shape[1]

    ext[...] = jnp.zeros_like(ext)
    tex[...] = jnp.full_like(tex, 3)

    def remote(src, dst, send, recv, to_s, to_g):
        return pltpu.make_async_remote_copy(
            src_ref=src, dst_ref=dst, send_sem=send, recv_sem=recv,
            device_id={"size": to_s, "gz": to_g}, device_id_type=MESH)

    own_rows = pl.ds(pl.multiple_of(s * bx, 8), bx)

    barrier = pltpu.get_barrier_semaphore()

    def greet(to_s, to_g):
        pl.semaphore_signal(barrier, inc=1, device_id={"size": to_s, "gz": to_g}, device_id_type=MESH)

    greeted = 0
    for j in range(n_size):
        peer = lax.rem(s + j, n_size)
        for d in ((0,) if 1 < j < n_size - 1 else (0, 1, n_gz - 1)):
            if j or d:
                greet(peer, lax.rem(g + d, n_gz))
                greeted += 1
    for j in range(2, n_gz - 1):
        greet(s, lax.rem(g + j, n_gz))
        greeted += 1

    inner = pltpu.make_async_copy(vp, ext.at[pl.ds(2, nz), pl.ds(half, bx)], local_sem.at[0])
    inner.start()
    own = pltpu.make_async_copy(vp, slab.at[pl.ds(3, nz), own_rows], local_sem.at[1])
    own.start()

    wide = bx + 2 * half

    def tissue_rows(which):
        if which == "low":
            return pl.ds(0, bx + half), pl.ds(half, bx + half)
        if which == "high":
            return pl.ds(nx - bx - half, bx + half), pl.ds(0, bx + half)
        return pl.ds(pl.multiple_of(s * bx - half, 8), wide), pl.ds(0, wide)

    cases = (("low", s == 0), ("high", s == n_size - 1), ("mid", (s > 0) & (s < n_size - 1)))

    def tex_copy(which):
        src, dst = tissue_rows(which)
        return pltpu.make_async_copy(tissue.at[:, src], tex.at[pl.ds(2, nz), dst], local_sem.at[2])

    for which, cond in cases:
        @pl.when(cond)
        def _(which=which):
            tex_copy(which).start()

    inner.wait()

    def pack(e, _):
        for i, r in enumerate((half, half + 1, half + bx - 2, half + bx - 1)):
            packed_out[i, pl.ds(e, 1), :] = ext[e + 2, pl.ds(r, 1), :]
        return 0

    lax.fori_loop(0, nz, pack, 0, unroll=4)
    pl.semaphore_wait(barrier, greeted)

    lows, highs = pl.ds(0, half), pl.ds(half, half)
    above, below = pl.ds(half + bx, half), pl.ds(0, half)
    middle = pl.ds(half, bx)
    has_low, has_high = g > 0, g < n_gz - 1
    x_low, x_high = s > 0, s < n_size - 1
    near = [
        (x_high, x_low, packed_out.at[pl.ds(2, 2)], packed_in.at[pl.ds(0, 2)], 0, s + 1, g),
        (x_low, x_high, packed_out.at[pl.ds(0, 2)], packed_in.at[pl.ds(2, 2)], 1, s - 1, g),
        (has_high, has_low, vp.at[pl.ds(nz - 2, 2)], ext.at[pl.ds(0, 2), middle], 2, s, g + 1),
        (has_low, has_high, vp.at[pl.ds(0, 2)], ext.at[pl.ds(nz + 2, 2), middle], 3, s, g - 1),
        (x_high & has_high, x_low & has_low, vp.at[pl.ds(nz - 1, 1), highs], ext.at[pl.ds(1, 1), below], 4, s + 1, g + 1),
        (x_low & has_high, x_high & has_low, vp.at[pl.ds(nz - 1, 1), lows], ext.at[pl.ds(1, 1), above], 5, s - 1, g + 1),
        (x_high & has_low, x_low & has_high, vp.at[pl.ds(0, 1), highs], ext.at[pl.ds(nz + 2, 1), below], 6, s + 1, g - 1),
        (x_low & has_low, x_high & has_high, vp.at[pl.ds(0, 1), lows], ext.at[pl.ds(nz + 2, 1), above], 7, s - 1, g - 1),
    ]
    for which, cond in cases:
        src, dst = tissue_rows(which)
        near.append((has_high & cond, has_low & cond, tissue.at[pl.ds(nz - 2, 2), src], tex.at[pl.ds(0, 2), dst], 8, s, g + 1))
        near.append((has_low & cond, has_high & cond, tissue.at[pl.ds(0, 2), src], tex.at[pl.ds(nz + 2, 2), dst], 9, s, g - 1))
    late = [
        (has_high, has_low, tissue.at[pl.ds(nz - 3, 3)], thalo.at[pl.ds(0, 3)], 10, s, g + 1),
        (has_low, has_high, tissue.at[pl.ds(0, 3)], thalo.at[pl.ds(3, 3)], 11, s, g - 1),
        (has_high, has_low, conc.at[pl.ds(nz - 2, 2)], chalo.at[pl.ds(0, 2)], 12, s, g + 1),
        (has_low, has_high, conc.at[pl.ds(0, 2)], chalo.at[pl.ds(2, 2)], 13, s, g - 1),
    ]

    def start_all(copies):
        for cond, _, src, dst, i, to_s, to_g in copies:
            @pl.when(cond)
            def _(src=src, dst=dst, i=i, to_s=to_s, to_g=to_g):
                remote(src, dst, near_send.at[i], near_recv.at[i], to_s, to_g).start()

    def wait_all(copies):
        for sent, cond, src, dst, i, to_s, to_g in copies:
            @pl.when(cond)
            def _(src=src, dst=dst, i=i):
                remote(src, dst, near_send.at[i], near_recv.at[i], s, g).wait_recv()

            @pl.when(sent)
            def _(src=src, dst=dst, i=i):
                remote(src, dst, near_send.at[i], near_recv.at[i], s, g).wait_send()

    start_all(near)

    n_z = n_size // 2
    z, x = lax.div(s, 2), lax.rem(s, 2)
    z_up, z_down, z_far = lax.rem(z + 1, n_z), lax.rem(z + n_z - 1, n_z), lax.rem(z + 2, n_z)
    across = 2 * z + 1 - x
    up, down, far = 2 * z_up + x, 2 * z_down + x, 2 * z_far + x
    up_across, down_across, far_across = 2 * z_up + 1 - x, 2 * z_down + 1 - x, 2 * z_far + 1 - x
    depth = nz // CHUNKS
    part = depth // 2
    order = [0, CHUNKS - 1, *range(1, CHUNKS - 1)]

    def piece(block, c, kind, to, first=0, count=depth, own=False):
        planes = pl.ds(3 + c * depth + first, count)
        where = pl.ds(pl.multiple_of(block * bx, 8), bx)
        src = vp.at[pl.ds(c * depth + first, count)] if own else slab.at[planes, where]
        return remote(src, slab.at[planes, where], block_send.at[kind, c], block_recv.at[kind, c], to, g)

    def own_pieces(c):
        return [piece(s, c, 0, across, own=True), piece(s, c, 1, up, own=True), piece(s, c, 2, down, own=True)]

    def from_across(c):
        return [piece(across, c, 3, up), piece(across, c, 4, down)]

    def from_down(c):
        return [piece(down, c, 5, up, 0, part)]

    def from_up(c):
        return [piece(up, c, 6, down, part, depth - part)]

    def from_far(c):
        return [piece(far, c, 7, across)]

    def hand_on(c):
        piece(across, c, 0, s).wait_recv()
        each(from_across(c), "start")
        piece(down, c, 1, s).wait_recv()
        each(from_down(c), "start")
        piece(up, c, 2, s).wait_recv()
        each(from_up(c), "start")

    def hand_far(c):
        piece(far, c, 5, s, 0, part).wait_recv()
        piece(far, c, 6, s, part, depth - part).wait_recv()
        each(from_far(c), "start")

    def finish(c):
        piece(down_across, c, 3, s).wait_recv()
        piece(up_across, c, 4, s).wait_recv()
        piece(far_across, c, 7, s).wait_recv()

    for c in order:
        each(own_pieces(c), "start")
    start_all(late)

    edges = [
        (has_high, has_low, slab.at[pl.ds(nz, 3)], slab.at[pl.ds(0, 3)], 14, s, g + 1),
        (has_low, has_high, slab.at[pl.ds(3, 3)], slab.at[pl.ds(nz + 3, 3)], 15, s, g - 1),
    ]

    cond, leak, inverse = scalar_tables(cond_ref, leak_ref)
    first = [l * i for l, i in zip(leak, inverse)]
    second = [k * l * i for k, l, i in zip(cond, leak, inverse)]
    lane = lax.broadcasted_iota(jnp.int32, (wide, ny), 1)

    for which, c in cases:
        @pl.when(c)
        def _(which=which):
            tex_copy(which).wait()
    wait_all(near)

    def unpack(low):
        def rows_in(e, _):
            for i in range(2):
                r = half - 2 + i if low else half + bx + i
                ext[e + 2, pl.ds(r, 1), :] = packed_in[i if low else 2 + i, pl.ds(e, 1), :]
            return 0
        lax.fori_loop(0, nz, rows_in, 0, unroll=4)

    @pl.when(x_low)
    def _():
        unpack(True)

    @pl.when(x_high)
    def _():
        unpack(False)

    def scale(e, _):
        (t2,) = select(tex[e], [second])
        qs[e] = t2 * ext[e]
        return 0

    lax.fori_loop(0, nz + 4, scale, 0, unroll=4)
    def stencil(ref, e):
        q = ref[e]
        total = ref[e - 1] + ref[e + 1] + pltpu.roll(q, 1, 0) + pltpu.roll(q, wide - 1, 0)
        return 6.0 * q - (total + lane_neighbours(q, lane, ny))

    def add_product(acc, a, b):
        h, r = two_sum(acc[0], a[1] * b[1])
        return h, acc[1] + ((a[1] * b[2] + a[2] * b[0]) + r)

    def apply(e):
        labels = tex[e]
        k, l, i, t1 = select(labels, [cond, leak, inverse, first])
        k = jnp.where(labels == 3, 0.0, k)
        field = ext[e]
        z = t1 * field
        az = l * z + k * stencil(qs, e)
        y = i * az
        qv[e] = k * y
        ys[e] = y
        return l * field, z, az, y

    def mine(x):
        x = x[half:half + bx]
        return (x, *split(x))

    def first_sums(e, accs):
        r0, z, az, y = (mine(x) for x in apply(e))
        return (add_product(accs[0], r0, z), add_product(accs[1], z, az), add_product(accs[2], y, az))

    apply(1)
    apply(nz + 2)
    zero = jnp.zeros((bx, ny), jnp.float32)
    sums = lax.fori_loop(2, nz + 2, first_sums, ((zero, zero),) * 3, unroll=2)
    hand_on(order[0])

    def last_sum(e, acc):
        labels = tex[e]
        k, l = select(labels, [cond, leak])
        y = ys[e]
        ay = l * y + k * stencil(qv, e)
        return add_product(acc, mine(y), mine(ay))

    sums = (*sums, lax.fori_loop(2, nz + 2, last_sum, (zero, zero), unroll=4))

    row = lax.broadcasted_iota(jnp.int32, (8, ny), 0)
    packed = jnp.zeros((8, ny), jnp.float32)
    for m, (h, l) in enumerate(sums):
        hs, ls = h[0:8], l[0:8]
        for r in range(8, bx, 8):
            hs, e = two_sum(hs, h[r:r + 8])
            ls = ls + l[r:r + 8] + e
        for shift in (4, 2, 1):
            hs, e = two_sum(hs, pltpu.roll(hs, shift, 0))
            ls = ls + pltpu.roll(ls, shift, 0) + e
        packed = jnp.where(row == m, hs, jnp.where(row == m + 4, ls, packed))
    tile[...] = packed

    def add_tiles(parts):
        total, errors = parts[0], jnp.zeros((8, ny), jnp.float32)
        for part in parts[1:]:
            total, e = two_sum(total, part)
            errors = errors + e
        return total + pltpu.roll(jnp.where(row < 4, errors, 0.0), 4, 0)

    def reduce(src, slots, index, count, axis, send, recv, between):
        for j in range(1, count):
            to = lax.rem(index + j, count)
            dev = (to, g) if axis == "size" else (s, to)
            remote(src, slots.at[index], send, recv, *dev).start()
        between()
        arrived = slots.at[pl.ds(0, count - 1)]
        remote(arrived, arrived, send, recv, s, g).wait()
        slots[index] = src[...]
        return add_tiles([slots[i] for i in range(count)])

    def first_half():
        hand_on(order[1])
        hand_far(order[0])
        hand_on(order[2])
        hand_far(order[1])
        hand_on(order[3])

    def second_half():
        hand_far(order[2])
        hand_far(order[3])
        own.wait()
        for c in order[:2]:
            finish(c)
        start_all(edges)

    total_tile[...] = reduce(tile, red_size, s, n_size, "size", ring_send, ring_recv, first_half)
    total = reduce(total_tile, red_gz, g, n_gz, "gz", grid_send, grid_recv, second_half)

    errors = jnp.zeros_like(total)
    shift = ny // 2
    while shift:
        total, e = two_sum(total, pltpu.roll(total, shift, 1))
        errors = errors + pltpu.roll(errors, shift, 1) + e
        shift //= 2
    lower = pltpu.roll(total, 4, 0) + errors
    b = [(total[m:m + 1], lower[m:m + 1]) for m in range(4)]
    t = pair_ratio(b[1], b[0])
    v = pair_sub_product(b[2], t, b[1])
    w = pair_sub_product(pair_sub_product(b[3], t, b[2]), t, v)
    b0, b1, v, w, t = b[0][0], b[1][0], v[0], w[0], t[0]
    det = b1 * w - v * v
    x_part = b0 * w / det
    y_part = -(b0 * v) / det
    scal[...] = jnp.where(row == 0, x_part + y_part * (1.0 - t), -y_part)

    for c in order[2:]:
        finish(c)
    for c in order:
        each(own_pieces(c) + from_across(c) + from_down(c) + from_up(c) + from_far(c), "wait_send")
    wait_all(late)
    wait_all(edges)


def exchange(n_size, n_gz, cond_table, leak_table, vp, tissue, conc):
    nz, bx, ny = vp.shape
    nx = tissue.shape[1]
    anywhere = pl.BlockSpec(memory_space=pl.ANY)
    scalars = pl.BlockSpec(memory_space=pltpu.SMEM)
    vmem = pl.BlockSpec(memory_space=pltpu.VMEM)
    hbm = pl.BlockSpec(memory_space=pltpu.HBM)
    dma = pltpu.SemaphoreType.DMA
    return pl.pallas_call(
        functools.partial(exchange_kernel, n_size, n_gz),
        out_shape=(
            jax.ShapeDtypeStruct((nz + 6, nx, ny), jnp.float32),
            jax.ShapeDtypeStruct((6, nx, ny), jnp.int32),
            jax.ShapeDtypeStruct((4, nx, ny), jnp.float32),
            jax.ShapeDtypeStruct((8, ny), jnp.float32),
        ),
        in_specs=[scalars, scalars, hbm, hbm, hbm],
        out_specs=(anywhere, anywhere, anywhere, pl.BlockSpec(memory_space=pltpu.VMEM)),
        scratch_shapes=[
            pltpu.VMEM((nz + 4, 2 * bx, ny), jnp.float32),
            pltpu.VMEM((nz + 4, 2 * bx, ny), jnp.int32),
            pltpu.VMEM((nz + 4, 2 * bx, ny), jnp.float32),
            pltpu.VMEM((nz + 4, 2 * bx, ny), jnp.float32),
            pltpu.VMEM((nz + 4, 2 * bx, ny), jnp.float32),
            pltpu.VMEM((4, nz, ny), jnp.float32),
            pltpu.VMEM((4, nz, ny), jnp.float32),
            pltpu.VMEM((8, ny), jnp.float32),
            pltpu.VMEM((n_size, 8, ny), jnp.float32),
            pltpu.VMEM((n_gz, 8, ny), jnp.float32),
            pltpu.VMEM((8, ny), jnp.float32),
            dma((3,)),
            dma((16,)), dma((16,)),
            dma((8, CHUNKS)), dma((8, CHUNKS)),
            dma, dma, dma, dma,
        ],
        compiler_params=pltpu.CompilerParams(collective_id=0, has_side_effects=True, vmem_limit_bytes=16 << 20),
        name="exchange",
    )(cond_table, leak_table, vp, tissue, conc)


def transport_kernel(
    n_gz, cond_ref, leak_ref, bind_ref, hinder_ref, diffuse_ref, scal, slab, tissue, thalo, conc, chalo, bound,
    pressure, free_out, bound_out,
    c0, c1, bnd, out, qs, ps, ks, flow_x, flow, coefs, sems, out_sems, pressure_sem,
):
    s, g = lax.axis_index("size"), lax.axis_index("gz")
    nz, nx, ny = conc.shape
    bx = pressure.shape[1]
    rows = 64 if nx % 64 == 0 else nx
    chunk = 8
    n_chunks = nz // chunk
    has_low, has_high = g > 0, g < n_gz - 1
    inside = pl.ds(EDGE, nx)

    def chunk_copies(i):
        z0 = i * chunk
        return [
            pltpu.make_async_copy(conc.at[pl.ds(z0, chunk)], c0.at[pl.ds(z0 + 2, chunk), inside], sems.at[i, 0]),
            pltpu.make_async_copy(bound.at[pl.ds(z0, chunk)], bnd.at[pl.ds(z0, chunk)], sems.at[i, 1]),
        ]

    def halo_copies(high):
        i, c = n_chunks + int(high), nz + 2 if high else 0
        return [
            pltpu.make_async_copy(chalo.at[pl.ds(2 * high, 2)], c0.at[pl.ds(c, 2), inside], sems.at[i, 0]),
        ]

    @pl.when(has_low)
    def _():
        each(halo_copies(False), "start")

    for i in range(n_chunks):
        each(chunk_copies(i), "start")

    @pl.when(has_high)
    def _():
        each(halo_copies(True), "start")

    edge_rows = jnp.zeros((EDGE, ny), jnp.float32)

    def clear(i, _):
        for ref in (c0, c1, qs, ps, ks):
            ref[i, pl.ds(0, EDGE), :] = edge_rows
            ref[i, pl.ds(EDGE + nx, EDGE), :] = edge_rows
        return 0

    lax.fori_loop(0, nz + 4, clear, 0)
    for i in (nz + 4, nz + 5):
        qs[i, pl.ds(0, EDGE), :] = edge_rows
        qs[i, pl.ds(EDGE + nx, EDGE), :] = edge_rows
    for i in range(2):
        flow_x[i, pl.ds(0, EDGE), :] = edge_rows

    def blank(high):
        c = nz + 2 if high else 0
        for i in range(2):
            c0[c + i, inside, :] = jnp.zeros((nx, ny), jnp.float32)

    @pl.when(g == 0)
    def _():
        blank(False)

    @pl.when(g == n_gz - 1)
    def _():
        blank(True)

    cond, leak, inverse = scalar_tables(cond_ref, leak_ref)
    x_part, y_part = scal[0, 0], scal[1, 0]
    hinder = TIME_STEP * hinder_ref[0]
    diffuse = TIME_STEP * diffuse_ref[0]
    rate = [TIME_STEP * bind_ref[0, i] for i in range(3)]
    second = [k * l * i for k, l, i in zip(cond, leak, inverse)]
    z_part = [x_part * l * i for l, i in zip(leak, inverse)]
    n_part = [y_part * k * i for k, i in zip(cond, inverse)]
    lane = lax.broadcasted_iota(jnp.int32, (rows, ny), 1)
    first_lane, last_lane = lane == 0, lane == ny - 1
    diffuse_low = jnp.where(first_lane, 0.0, diffuse)
    diffuse_high = jnp.where(last_lane, 0.0, diffuse)
    starts = range(0, nx, rows)

    def kind(p, block):
        if isinstance(p, int) and p < 0:
            return thalo[p + 3, block, :]
        if isinstance(p, int) and p >= nz:
            return thalo[p - nz + 3, block, :]
        return tissue[p, block, :]

    def field(p, block):
        value = slab[p + 3, block, :]
        if isinstance(p, int) and (p < 0 or p >= nz):
            value = jnp.where(has_low if p < 0 else has_high, value, 0.0)
        return value

    def scale(p):
        for r in starts:
            block = pl.ds(r, rows)
            (t2,) = select(kind(p, block), [second])
            qs[p + 3, pl.ds(EDGE + r, rows), :] = t2 * field(p, block)

    def press(p):
        for r in starts:
            block = pl.ds(r, rows)
            here = pl.ds(EDGE + r, rows)
            k, zp, npart = select(kind(p, block), [cond, z_part, n_part])
            q = qs[p + 3, here, :]
            total = qs[p + 2, here, :] + qs[p + 4, here, :]
            total = total + qs[p + 3, pl.ds(EDGE + r - 1, rows), :] + qs[p + 3, pl.ds(EDGE + r + 1, rows), :]
            total = total + jnp.where(first_lane, 0.0, pltpu.roll(q, 1, 1)) + jnp.where(last_lane, 0.0, pltpu.roll(q, ny - 1, 1))
            ps[p + 2, here, :] = zp * field(p, block) + npart * total
            ks[p + 2, here, :] = k

    def outside(p, ref):
        if isinstance(p, int) and (p < 0 or p >= nz):
            @pl.when(g == (0 if p < 0 else n_gz - 1))
            def _():
                ref[p + 2, inside, :] = jnp.zeros((nx, ny), jnp.float32)

    def flows(p):
        slot = lax.rem(p + 4, 2)
        for r in starts:
            block = pl.ds(r, rows)
            here = pl.ds(EDGE + r, rows)
            after = pl.ds(EDGE + r + 1, rows)
            k_here, press_here = ks[p + 2, here, :], ps[p + 2, here, :]
            k = k_here * hinder
            flow[slot, 0, block, :] = k * ks[p + 3, here, :] * (press_here - ps[p + 3, here, :])
            flow_x[slot, here, :] = k * ks[p + 2, after, :] * (press_here - ps[p + 2, after, :])
            w_y = k * pltpu.roll(k_here, ny - 1, 1) * (press_here - pltpu.roll(press_here, ny - 1, 1))
            flow[slot, 1, block, :] = jnp.where(last_lane, 0.0, w_y)

    def first_step(p):
        slot, source, before = lax.rem(p + 4, 4), lax.rem(p + 4, 2), lax.rem(p + 3, 4)
        for r in starts:
            block = pl.ds(r, rows)
            here = pl.ds(EDGE + r, rows)
            w = flow[source, 0, block, :]
            a = jnp.maximum(w, 0.0) + diffuse
            b = a - w
            w_x = flow_x[source, here, :]
            a_x = jnp.maximum(w_x, 0.0) + diffuse
            b_x = a_x - w_x
            w_low = flow_x[source, pl.ds(EDGE + r - 1, rows), :]
            a_x_low = jnp.maximum(w_low, 0.0) + diffuse
            b_x_low = a_x_low - w_low
            w_y = flow[source, 1, block, :]
            up = jnp.maximum(w_y, 0.0)
            a_y = up + diffuse
            b_y = (up - w_y) + diffuse_high
            w_low = pltpu.roll(w_y, 1, 1)
            up = jnp.maximum(w_low, 0.0)
            a_y_low = up + diffuse_low
            b_y_low = (up - w_low) + diffuse
            (bind,) = select(kind(p, block), [rate])
            centre = (a + a_x) + (a_y + b_x_low) + (b_y_low + coefs[before, 6, block, :]) + bind
            centre = 1.0 - centre
            for i, value in enumerate((centre, a_x_low, b_x, a_y_low, b_y, a, b)):
                coefs[slot, i, block, :] = value
            c = c0[p + 2, here, :]
            value = centre * c + (b * c0[p + 3, here, :] + coefs[before, 5, block, :] * c0[p + 1, here, :])
            value = value + (a_x_low * c0[p + 2, pl.ds(EDGE + r - 1, rows), :] + b_x * c0[p + 2, pl.ds(EDGE + r + 1, rows), :])
            value = value + (a_y_low * pltpu.roll(c, 1, 1) + b_y * pltpu.roll(c, ny - 1, 1))
            c1[p + 2, here, :] = value

    def second_step(p):
        slot, before = lax.rem(p + 4, 4), lax.rem(p + 3, 4)
        for r in starts:
            block = pl.ds(r, rows)
            here = pl.ds(EDGE + r, rows)
            c = c1[p + 2, here, :]
            value = coefs[slot, 0, block, :] * c
            value = value + (coefs[slot, 6, block, :] * c1[p + 3, here, :] + coefs[before, 5, block, :] * c1[p + 1, here, :])
            value = value + (coefs[slot, 1, block, :] * c1[p + 2, pl.ds(EDGE + r - 1, rows), :]
                             + coefs[slot, 2, block, :] * c1[p + 2, pl.ds(EDGE + r + 1, rows), :])
            value = value + (coefs[slot, 3, block, :] * pltpu.roll(c, 1, 1) + coefs[slot, 4, block, :] * pltpu.roll(c, ny - 1, 1))
            out[p, block, :] = value
            (bind,) = select(kind(p, block), [rate])
            bnd[p, block, :] = bnd[p, block, :] + bind * (c0[p + 2, here, :] + c)

    def last_copies(i):
        z0 = pl.ds(nz - chunk + i * chunk // 2, chunk // 2)
        return [
            pltpu.make_async_copy(out.at[z0], free_out.at[z0], out_sems.at[n_chunks - 1 + i, 0]),
            pltpu.make_async_copy(bnd.at[z0], bound_out.at[z0], out_sems.at[n_chunks - 1 + i, 1]),
        ]

    def out_copies(i):
        z0 = pl.ds(i * chunk, chunk)
        return [
            pltpu.make_async_copy(out.at[z0], free_out.at[z0], out_sems.at[i, 0]),
            pltpu.make_async_copy(bnd.at[z0], bound_out.at[z0], out_sems.at[i, 1]),
        ]

    def turn(p):
        fixed = isinstance(p, int)
        if not fixed or 0 <= p - 4 < nz:
            second_step(p - 4)
        if not fixed or -1 <= p - 2 <= nz:
            first_step(p - 2)
            outside(p - 2, c1)
        if not fixed or -2 <= p - 1 <= nz:
            flows(p - 1)
        if fixed and p == 0:
            for r in starts:
                block = pl.ds(r, rows)
                w = flow[0, 0, block, :]
                a = jnp.maximum(w, 0.0) + diffuse
                coefs[2, 5, block, :] = a
                coefs[2, 6, block, :] = a - w
        if not fixed or -2 <= p + 1 <= nz + 1:
            press(p + 1)
            outside(p + 1, ks)
        if not fixed or -3 <= p + 3 <= nz + 2:
            scale(p + 3)

    for p in range(-6, 4):
        if p == 1:
            @pl.when(has_low)
            def _():
                each(halo_copies(False), "wait")

            each(chunk_copies(0), "wait")
        turn(p)

    def body(p, _):
        group = lax.div(p + 3, chunk)

        @pl.when((lax.rem(p + 3, chunk) == 0) & (group < n_chunks))
        def _():
            each(chunk_copies(group), "wait")

        turn(p)

        @pl.when((p >= chunk + 3) & (lax.rem(p - 3, chunk) == 0))
        def _():
            each(out_copies(lax.div(p - 3, chunk) - 1), "start")

        return 0

    lax.fori_loop(4, nz - 3, body, 0)

    @pl.when(has_high)
    def _():
        each(halo_copies(True), "wait")

    own = pltpu.make_async_copy(
        ps.at[pl.ds(2, nz), pl.ds(pl.multiple_of(EDGE + s * bx, 8), bx)], pressure, pressure_sem)
    for p in range(nz - 3, nz + 4):
        turn(p)
        if p == nz - 1:
            own.start()
            each(last_copies(0), "start")
    each(last_copies(1), "start")
    for i in range(n_chunks - 1):
        each(out_copies(i), "wait")
    for i in range(2):
        each(last_copies(i), "wait")
    own.wait()


def transport(n_gz, bx, cond_table, leak_table, bind_table, hindrance, diffusivity, scal, slab, tissue, thalo, conc, chalo, bound):
    nz, nx, ny = conc.shape
    anywhere = pl.BlockSpec(memory_space=pl.ANY)
    scalars = pl.BlockSpec(memory_space=pltpu.SMEM)
    vmem = pl.BlockSpec(memory_space=pltpu.VMEM)
    hbm = pl.BlockSpec(memory_space=pltpu.HBM)
    wide = nx + 2 * EDGE
    f32 = jnp.float32
    dma = pltpu.SemaphoreType.DMA
    n_chunks = nz // 8
    return pl.pallas_call(
        functools.partial(transport_kernel, n_gz),
        out_shape=(
            jax.ShapeDtypeStruct((nz, bx, ny), f32),
            jax.ShapeDtypeStruct((nz, nx, ny), f32),
            jax.ShapeDtypeStruct((nz, nx, ny), f32),
        ),
        in_specs=[scalars] * 5 + [vmem] * 4 + [anywhere, anywhere, hbm],
        out_specs=(anywhere, anywhere, anywhere),
        scratch_shapes=[
            pltpu.VMEM((nz + 4, wide, ny), f32),
            pltpu.VMEM((nz + 4, wide, ny), f32),
            pltpu.VMEM((nz, nx, ny), f32),
            pltpu.VMEM((nz, nx, ny), f32),
            pltpu.VMEM((nz + 6, wide, ny), f32),
            pltpu.VMEM((nz + 4, wide, ny), f32),
            pltpu.VMEM((nz + 4, wide, ny), f32),
            pltpu.VMEM((2, wide, ny), f32),
            pltpu.VMEM((2, 2, nx, ny), f32),
            pltpu.VMEM((4, 7, nx, ny), f32),
            dma((n_chunks + 2, 2)),
            dma((n_chunks + 1, 2)),
            dma,
        ],
        compiler_params=pltpu.CompilerParams(vmem_limit_bytes=36 << 20),
        name="transport",
    )(cond_table, leak_table, bind_table, hindrance, diffusivity, scal, slab, tissue, thalo, conc, chalo, in_hbm(bound))


def in_hbm(array):
    return pltpu.with_memory_space_constraint(array, pltpu.HBM)


def solution(mesh):
    n_size, n_gz = mesh.shape["size"], mesh.shape["gz"]

    def local(tissue, vessel_pressure, cond_table, leak_table, bind_table, hindrance, diffusivity, free_conc, bound_conc):
        conc, bound = free_conc[0], bound_conc[0]
        slab, thalo, chalo, scal = exchange(
            n_size, n_gz, *(in_hbm(v) for v in (cond_table, leak_table, vessel_pressure, tissue, conc)))
        pressure, free, held = transport(
            n_gz, vessel_pressure.shape[1], *(in_hbm(v) for v in (cond_table, leak_table, bind_table)), hindrance, diffusivity,
            scal, slab, tissue, thalo, conc, chalo, in_hbm(bound))
        return pressure, free[None], held[None]

    return jax.shard_map(
        local,
        mesh=mesh,
        in_specs=(
            P("gz", None, None), P("gz", "size", None), P(), P(), P("size", None), P("size"), P("size"),
            P("size", "gz", None, None), P("size", "gz", None, None),
        ),
        out_specs=(P("gz", "size", None), P("size", "gz", None, None), P("size", "gz", None, None)),
        check_vma=False,
    )
```

```python
import functools

import jax
import jax.numpy as jnp
from jax import lax
from jax.experimental import pallas as pl
from jax.experimental.pallas import tpu as pltpu
from jax.sharding import PartitionSpec as P

MESH = pl.DeviceIdType.MESH
TIME_STEP = 0.1
EDGE = 8
CHUNKS = 4


def each(copies, what):
    for copy in copies:
        getattr(copy, what)()


def select(labels, values):
    first, second = labels == 0, labels == 1
    return [jnp.where(first, v[0], jnp.where(second, v[1], v[2])) for v in values]


def two_sum(a, b):
    total = a + b
    part = total - a
    return total, (a - (total - part)) + (b - part)


def split(a):
    wide = 4097.0 * a
    high = wide - (wide - a)
    return high, a - high


def two_prod(a, b):
    product = a * b
    ah, al = split(a)
    bh, bl = split(b)
    return product, ((ah * bh - product) + ah * bl + al * bh) + al * bl


def pair_sub_product(x, a, b):
    p, e = two_prod(a[0], b[0])
    e = e + (a[0] * b[1] + a[1] * b[0])
    s, r = two_sum(x[0], -p)
    r = r + (x[1] - e)
    return two_sum(s, r)


def pair_ratio(x, y):
    q = x[0] / y[0]
    rest = pair_sub_product(x, (q, jnp.zeros_like(q)), y)
    return two_sum(q, (rest[0] + rest[1]) / y[0])


def scalar_tables(cond_ref, leak_ref):
    cond = [cond_ref[i] for i in range(3)]
    leak = [leak_ref[i] for i in range(3)]
    inverse = []
    for k, l in zip(cond, leak):
        inverse.append((1.0 / jnp.full((8, 128), 6.0 * k * k + l, jnp.float32))[0, 0])
    return cond, leak, inverse


def lane_neighbours(q, lane, ny):
    up = jnp.where(lane == ny - 1, 0.0, pltpu.roll(q, ny - 1, 1))
    down = jnp.where(lane == 0, 0.0, pltpu.roll(q, 1, 1))
    return up + down


def exchange_kernel(
    n_size, n_gz, cond_ref, leak_ref, vp, tissue, conc,
    slab, thalo, chalo, scal,
    ext, tex, qs, qv, ys, packed_out, packed_in, tile, red_size, red_gz, total_tile,
    local_sem, near_send, near_recv, block_send, block_recv,
    ring_send, ring_recv, grid_send, grid_recv,
):
    s, g = lax.axis_index("size"), lax.axis_index("gz")
    nz, bx, ny = vp.shape
    half = bx // 2
    nx = tissue.shape[1]

    ext[...] = jnp.zeros_like(ext)
    tex[...] = jnp.full_like(tex, 3)

    def remote(src, dst, send, recv, to_s, to_g):
        return pltpu.make_async_remote_copy(
            src_ref=src, dst_ref=dst, send_sem=send, recv_sem=recv,
            device_id={"size": to_s, "gz": to_g}, device_id_type=MESH)

    own_rows = pl.ds(pl.multiple_of(s * bx, 8), bx)

    barrier = pltpu.get_barrier_semaphore()

    def greet(to_s, to_g):
        pl.semaphore_signal(barrier, inc=1, device_id={"size": to_s, "gz": to_g}, device_id_type=MESH)

    greeted = 0
    for j in range(n_size):
        peer = lax.rem(s + j, n_size)
        for d in ((0,) if 1 < j < n_size - 1 else (0, 1, n_gz - 1)):
            if j or d:
                greet(peer, lax.rem(g + d, n_gz))
                greeted += 1
    for j in range(2, n_gz - 1):
        greet(s, lax.rem(g + j, n_gz))
        greeted += 1

    inner = pltpu.make_async_copy(vp, ext.at[pl.ds(2, nz), pl.ds(half, bx)], local_sem.at[0])
    inner.start()
    own = pltpu.make_async_copy(vp, slab.at[pl.ds(3, nz), own_rows], local_sem.at[1])
    own.start()

    wide = bx + 2 * half

    def tissue_rows(which):
        if which == "low":
            return pl.ds(0, bx + half), pl.ds(half, bx + half)
        if which == "high":
            return pl.ds(nx - bx - half, bx + half), pl.ds(0, bx + half)
        return pl.ds(pl.multiple_of(s * bx - half, 8), wide), pl.ds(0, wide)

    cases = (("low", s == 0), ("high", s == n_size - 1), ("mid", (s > 0) & (s < n_size - 1)))

    def tex_copy(which):
        src, dst = tissue_rows(which)
        return pltpu.make_async_copy(tissue.at[:, src], tex.at[pl.ds(2, nz), dst], local_sem.at[2])

    for which, cond in cases:
        @pl.when(cond)
        def _(which=which):
            tex_copy(which).start()

    inner.wait()

    def pack(e, _):
        for i, r in enumerate((half, half + 1, half + bx - 2, half + bx - 1)):
            packed_out[i, pl.ds(e, 1), :] = ext[e + 2, pl.ds(r, 1), :]
        return 0

    lax.fori_loop(0, nz, pack, 0, unroll=4)
    pl.semaphore_wait(barrier, greeted)

    lows, highs = pl.ds(0, half), pl.ds(half, half)
    above, below = pl.ds(half + bx, half), pl.ds(0, half)
    middle = pl.ds(half, bx)
    has_low, has_high = g > 0, g < n_gz - 1
    x_low, x_high = s > 0, s < n_size - 1
    near = [
        (x_high, x_low, packed_out.at[pl.ds(2, 2)], packed_in.at[pl.ds(0, 2)], 0, s + 1, g),
        (x_low, x_high, packed_out.at[pl.ds(0, 2)], packed_in.at[pl.ds(2, 2)], 1, s - 1, g),
        (has_high, has_low, vp.at[pl.ds(nz - 2, 2)], ext.at[pl.ds(0, 2), middle], 2, s, g + 1),
        (has_low, has_high, vp.at[pl.ds(0, 2)], ext.at[pl.ds(nz + 2, 2), middle], 3, s, g - 1),
        (x_high & has_high, x_low & has_low, vp.at[pl.ds(nz - 1, 1), highs], ext.at[pl.ds(1, 1), below], 4, s + 1, g + 1),
        (x_low & has_high, x_high & has_low, vp.at[pl.ds(nz - 1, 1), lows], ext.at[pl.ds(1, 1), above], 5, s - 1, g + 1),
        (x_high & has_low, x_low & has_high, vp.at[pl.ds(0, 1), highs], ext.at[pl.ds(nz + 2, 1), below], 6, s + 1, g - 1),
        (x_low & has_low, x_high & has_high, vp.at[pl.ds(0, 1), lows], ext.at[pl.ds(nz + 2, 1), above], 7, s - 1, g - 1),
    ]
    for which, cond in cases:
        src, dst = tissue_rows(which)
        near.append((has_high & cond, has_low & cond, tissue.at[pl.ds(nz - 2, 2), src], tex.at[pl.ds(0, 2), dst], 8, s, g + 1))
        near.append((has_low & cond, has_high & cond, tissue.at[pl.ds(0, 2), src], tex.at[pl.ds(nz + 2, 2), dst], 9, s, g - 1))
    late = [
        (has_high, has_low, tissue.at[pl.ds(nz - 3, 3)], thalo.at[pl.ds(0, 3)], 10, s, g + 1),
        (has_low, has_high, tissue.at[pl.ds(0, 3)], thalo.at[pl.ds(3, 3)], 11, s, g - 1),
        (has_high, has_low, conc.at[pl.ds(nz - 2, 2)], chalo.at[pl.ds(0, 2)], 12, s, g + 1),
        (has_low, has_high, conc.at[pl.ds(0, 2)], chalo.at[pl.ds(2, 2)], 13, s, g - 1),
    ]

    def start_all(copies):
        for cond, _, src, dst, i, to_s, to_g in copies:
            @pl.when(cond)
            def _(src=src, dst=dst, i=i, to_s=to_s, to_g=to_g):
                remote(src, dst, near_send.at[i], near_recv.at[i], to_s, to_g).start()

    def wait_all(copies):
        for sent, cond, src, dst, i, to_s, to_g in copies:
            @pl.when(cond)
            def _(src=src, dst=dst, i=i):
                remote(src, dst, near_send.at[i], near_recv.at[i], s, g).wait_recv()

            @pl.when(sent)
            def _(src=src, dst=dst, i=i):
                remote(src, dst, near_send.at[i], near_recv.at[i], s, g).wait_send()

    start_all(near)

    n_z = n_size // 2
    z, x = lax.div(s, 2), lax.rem(s, 2)
    z_up, z_down, z_far = lax.rem(z + 1, n_z), lax.rem(z + n_z - 1, n_z), lax.rem(z + 2, n_z)
    across = 2 * z + 1 - x
    up, down, far = 2 * z_up + x, 2 * z_down + x, 2 * z_far + x
    up_across, down_across, far_across = 2 * z_up + 1 - x, 2 * z_down + 1 - x, 2 * z_far + 1 - x
    depth = nz // CHUNKS
    part = depth // 2
    order = [0, CHUNKS - 1, *range(1, CHUNKS - 1)]

    def piece(block, c, kind, to, first=0, count=depth, own=False):
        planes = pl.ds(3 + c * depth + first, count)
        where = pl.ds(pl.multiple_of(block * bx, 8), bx)
        src = vp.at[pl.ds(c * depth + first, count)] if own else slab.at[planes, where]
        return remote(src, slab.at[planes, where], block_send.at[kind, c], block_recv.at[kind, c], to, g)

    def own_pieces(c):
        return [piece(s, c, 0, across, own=True), piece(s, c, 1, up, own=True), piece(s, c, 2, down, own=True)]

    def from_across(c):
        return [piece(across, c, 3, up), piece(across, c, 4, down)]

    def from_down(c):
        return [piece(down, c, 5, up, 0, part)]

    def from_up(c):
        return [piece(up, c, 6, down, part, depth - part)]

    def from_far(c):
        return [piece(far, c, 7, across)]

    def hand_on(c):
        piece(across, c, 0, s).wait_recv()
        each(from_across(c), "start")
        piece(down, c, 1, s).wait_recv()
        each(from_down(c), "start")
        piece(up, c, 2, s).wait_recv()
        each(from_up(c), "start")

    def hand_far(c):
        piece(far, c, 5, s, 0, part).wait_recv()
        piece(far, c, 6, s, part, depth - part).wait_recv()
        each(from_far(c), "start")

    def finish(c):
        piece(down_across, c, 3, s).wait_recv()
        piece(up_across, c, 4, s).wait_recv()
        piece(far_across, c, 7, s).wait_recv()

    for c in order:
        each(own_pieces(c), "start")
    start_all(late)

    edges = [
        (has_high, has_low, slab.at[pl.ds(nz, 3)], slab.at[pl.ds(0, 3)], 14, s, g + 1),
        (has_low, has_high, slab.at[pl.ds(3, 3)], slab.at[pl.ds(nz + 3, 3)], 15, s, g - 1),
    ]

    cond, leak, inverse = scalar_tables(cond_ref, leak_ref)
    first = [l * i for l, i in zip(leak, inverse)]
    second = [k * l * i for k, l, i in zip(cond, leak, inverse)]
    lane = lax.broadcasted_iota(jnp.int32, (wide, ny), 1)

    for which, c in cases:
        @pl.when(c)
        def _(which=which):
            tex_copy(which).wait()
    wait_all(near)

    def unpack(low):
        def rows_in(e, _):
            for i in range(2):
                r = half - 2 + i if low else half + bx + i
                ext[e + 2, pl.ds(r, 1), :] = packed_in[i if low else 2 + i, pl.ds(e, 1), :]
            return 0
        lax.fori_loop(0, nz, rows_in, 0, unroll=4)

    @pl.when(x_low)
    def _():
        unpack(True)

    @pl.when(x_high)
    def _():
        unpack(False)

    def scale(e, _):
        (t2,) = select(tex[e], [second])
        qs[e] = t2 * ext[e]
        return 0

    lax.fori_loop(0, nz + 4, scale, 0, unroll=4)
    def stencil(ref, e):
        q = ref[e]
        total = ref[e - 1] + ref[e + 1] + pltpu.roll(q, 1, 0) + pltpu.roll(q, wide - 1, 0)
        return 6.0 * q - (total + lane_neighbours(q, lane, ny))

    def add_product(acc, a, b):
        h, r = two_sum(acc[0], a[1] * b[1])
        return h, acc[1] + ((a[1] * b[2] + a[2] * b[0]) + r)

    def apply(e):
        labels = tex[e]
        k, l, i, t1 = select(labels, [cond, leak, inverse, first])
        k = jnp.where(labels == 3, 0.0, k)
        field = ext[e]
        z = t1 * field
        az = l * z + k * stencil(qs, e)
        y = i * az
        qv[e] = k * y
        ys[e] = y
        return l * field, z, az, y

    def mine(x):
        x = x[half:half + bx]
        return (x, *split(x))

    def first_sums(e, accs):
        r0, z, az, y = (mine(x) for x in apply(e))
        return (add_product(accs[0], r0, z), add_product(accs[1], z, az), add_product(accs[2], y, az))

    apply(1)
    apply(nz + 2)
    zero = jnp.zeros((bx, ny), jnp.float32)
    sums = lax.fori_loop(2, nz + 2, first_sums, ((zero, zero),) * 3, unroll=2)
    hand_on(order[0])

    def last_sum(e, acc):
        labels = tex[e]
        k, l = select(labels, [cond, leak])
        y = ys[e]
        ay = l * y + k * stencil(qv, e)
        return add_product(acc, mine(y), mine(ay))

    sums = (*sums, lax.fori_loop(2, nz + 2, last_sum, (zero, zero), unroll=4))

    row = lax.broadcasted_iota(jnp.int32, (8, ny), 0)
    packed = jnp.zeros((8, ny), jnp.float32)
    for m, (h, l) in enumerate(sums):
        hs, ls = h[0:8], l[0:8]
        for r in range(8, bx, 8):
            hs, e = two_sum(hs, h[r:r + 8])
            ls = ls + l[r:r + 8] + e
        for shift in (4, 2, 1):
            hs, e = two_sum(hs, pltpu.roll(hs, shift, 0))
            ls = ls + pltpu.roll(ls, shift, 0) + e
        packed = jnp.where(row == m, hs, jnp.where(row == m + 4, ls, packed))
    tile[...] = packed

    def add_tiles(parts):
        total, errors = parts[0], jnp.zeros((8, ny), jnp.float32)
        for part in parts[1:]:
            total, e = two_sum(total, part)
            errors = errors + e
        return total + pltpu.roll(jnp.where(row < 4, errors, 0.0), 4, 0)

    def reduce(src, slots, index, count, axis, send, recv, between):
        for j in range(1, count):
            to = lax.rem(index + j, count)
            dev = (to, g) if axis == "size" else (s, to)
            remote(src, slots.at[index], send, recv, *dev).start()
        between()
        arrived = slots.at[pl.ds(0, count - 1)]
        remote(arrived, arrived, send, recv, s, g).wait()
        slots[index] = src[...]
        return add_tiles([slots[i] for i in range(count)])

    def first_half():
        hand_on(order[1])
        hand_far(order[0])
        hand_on(order[2])
        hand_far(order[1])
        hand_on(order[3])

    def second_half():
        hand_far(order[2])
        hand_far(order[3])
        own.wait()
        for c in order[:2]:
            finish(c)
        start_all(edges)

    total_tile[...] = reduce(tile, red_size, s, n_size, "size", ring_send, ring_recv, first_half)
    total = reduce(total_tile, red_gz, g, n_gz, "gz", grid_send, grid_recv, second_half)

    errors = jnp.zeros_like(total)
    shift = ny // 2
    while shift:
        total, e = two_sum(total, pltpu.roll(total, shift, 1))
        errors = errors + pltpu.roll(errors, shift, 1) + e
        shift //= 2
    lower = pltpu.roll(total, 4, 0) + errors
    b = [(total[m:m + 1], lower[m:m + 1]) for m in range(4)]
    t = pair_ratio(b[1], b[0])
    v = pair_sub_product(b[2], t, b[1])
    w = pair_sub_product(pair_sub_product(b[3], t, b[2]), t, v)
    b0, b1, v, w, t = b[0][0], b[1][0], v[0], w[0], t[0]
    det = b1 * w - v * v
    x_part = b0 * w / det
    y_part = -(b0 * v) / det
    scal[...] = jnp.where(row == 0, x_part + y_part * (1.0 - t), -y_part)

    for c in order[2:]:
        finish(c)
    for c in order:
        each(own_pieces(c) + from_across(c) + from_down(c) + from_up(c) + from_far(c), "wait_send")
    wait_all(late)
    wait_all(edges)


def exchange(n_size, n_gz, cond_table, leak_table, vp, tissue, conc):
    nz, bx, ny = vp.shape
    nx = tissue.shape[1]
    anywhere = pl.BlockSpec(memory_space=pl.ANY)
    scalars = pl.BlockSpec(memory_space=pltpu.SMEM)
    vmem = pl.BlockSpec(memory_space=pltpu.VMEM)
    hbm = pl.BlockSpec(memory_space=pltpu.HBM)
    dma = pltpu.SemaphoreType.DMA
    return pl.pallas_call(
        functools.partial(exchange_kernel, n_size, n_gz),
        out_shape=(
            jax.ShapeDtypeStruct((nz + 6, nx, ny), jnp.float32),
            jax.ShapeDtypeStruct((6, nx, ny), jnp.int32),
            jax.ShapeDtypeStruct((4, nx, ny), jnp.float32),
            jax.ShapeDtypeStruct((8, ny), jnp.float32),
        ),
        in_specs=[scalars, scalars, hbm, hbm, hbm],
        out_specs=(anywhere, anywhere, anywhere, pl.BlockSpec(memory_space=pltpu.VMEM)),
        scratch_shapes=[
            pltpu.VMEM((nz + 4, 2 * bx, ny), jnp.float32),
            pltpu.VMEM((nz + 4, 2 * bx, ny), jnp.int32),
            pltpu.VMEM((nz + 4, 2 * bx, ny), jnp.float32),
            pltpu.VMEM((nz + 4, 2 * bx, ny), jnp.float32),
            pltpu.VMEM((nz + 4, 2 * bx, ny), jnp.float32),
            pltpu.VMEM((4, nz, ny), jnp.float32),
            pltpu.VMEM((4, nz, ny), jnp.float32),
            pltpu.VMEM((8, ny), jnp.float32),
            pltpu.VMEM((n_size, 8, ny), jnp.float32),
            pltpu.VMEM((n_gz, 8, ny), jnp.float32),
            pltpu.VMEM((8, ny), jnp.float32),
            dma((3,)),
            dma((16,)), dma((16,)),
            dma((8, CHUNKS)), dma((8, CHUNKS)),
            dma, dma, dma, dma,
        ],
        compiler_params=pltpu.CompilerParams(collective_id=0, has_side_effects=True, vmem_limit_bytes=16 << 20),
        name="exchange",
    )(cond_table, leak_table, vp, tissue, conc)


def transport_kernel(
    n_gz, cond_ref, leak_ref, bind_ref, hinder_ref, diffuse_ref, scal, slab, tissue, thalo, conc, chalo, bound,
    pressure, free_out, bound_out,
    c0, c1, bnd, out, qs, ps, ks, flow_x, flow, coefs, coef_z, sems, out_sems, pressure_sem,
):
    s, g = lax.axis_index("size"), lax.axis_index("gz")
    nz, nx, ny = conc.shape
    bx = pressure.shape[1]
    rows = 64 if nx % 64 == 0 else nx
    chunk = 8
    n_chunks = nz // chunk
    has_low, has_high = g > 0, g < n_gz - 1
    inside = pl.ds(EDGE, nx)

    def chunk_copies(i):
        z0 = i * chunk
        return [
            pltpu.make_async_copy(conc.at[pl.ds(z0, chunk)], c0.at[pl.ds(z0 + 2, chunk), inside], sems.at[i, 0]),
            pltpu.make_async_copy(bound.at[pl.ds(z0, chunk)], bnd.at[pl.ds(z0, chunk)], sems.at[i, 1]),
        ]

    def halo_copies(high):
        i, c = n_chunks + int(high), nz + 2 if high else 0
        return [
            pltpu.make_async_copy(chalo.at[pl.ds(2 * high, 2)], c0.at[pl.ds(c, 2), inside], sems.at[i, 0]),
        ]

    @pl.when(has_low)
    def _():
        each(halo_copies(False), "start")

    for i in range(n_chunks):
        each(chunk_copies(i), "start")

    @pl.when(has_high)
    def _():
        each(halo_copies(True), "start")

    edge_rows = jnp.zeros((EDGE, ny), jnp.float32)

    def clear(i, _):
        for ref in (c0, c1, qs, ps, ks):
            ref[i, pl.ds(0, EDGE), :] = edge_rows
            ref[i, pl.ds(EDGE + nx, EDGE), :] = edge_rows
        return 0

    lax.fori_loop(0, nz + 4, clear, 0)
    for i in (nz + 4, nz + 5):
        qs[i, pl.ds(0, EDGE), :] = edge_rows
        qs[i, pl.ds(EDGE + nx, EDGE), :] = edge_rows
    for i in range(2):
        flow_x[i, pl.ds(0, EDGE), :] = edge_rows

    def blank(high):
        c = nz + 2 if high else 0
        for i in range(2):
            c0[c + i, inside, :] = jnp.zeros((nx, ny), jnp.float32)

    @pl.when(g == 0)
    def _():
        blank(False)

    @pl.when(g == n_gz - 1)
    def _():
        blank(True)

    cond, leak, inverse = scalar_tables(cond_ref, leak_ref)
    x_part, y_part = scal[0, 0], scal[1, 0]
    hinder = TIME_STEP * hinder_ref[0]
    diffuse = TIME_STEP * diffuse_ref[0]
    rate = [TIME_STEP * bind_ref[0, i] for i in range(3)]
    second = [k * l * i for k, l, i in zip(cond, leak, inverse)]
    z_part = [x_part * l * i for l, i in zip(leak, inverse)]
    n_part = [y_part * k * i for k, i in zip(cond, inverse)]
    lane = lax.broadcasted_iota(jnp.int32, (rows, ny), 1)
    first_lane, last_lane = lane == 0, lane == ny - 1
    diffuse_low = jnp.where(first_lane, 0.0, diffuse)
    diffuse_high = jnp.where(last_lane, 0.0, diffuse)
    starts = range(0, nx, rows)

    def kind(p, block):
        if isinstance(p, int) and p < 0:
            return thalo[p + 3, block, :]
        if isinstance(p, int) and p >= nz:
            return thalo[p - nz + 3, block, :]
        return tissue[p, block, :]

    def field(p, block):
        value = slab[p + 3, block, :]
        if isinstance(p, int) and (p < 0 or p >= nz):
            value = jnp.where(has_low if p < 0 else has_high, value, 0.0)
        return value

    def scale(p):
        for r in starts:
            block = pl.ds(r, rows)
            (t2,) = select(kind(p, block), [second])
            qs[p + 3, pl.ds(EDGE + r, rows), :] = t2 * field(p, block)

    def press(p):
        for r in starts:
            block = pl.ds(r, rows)
            here = pl.ds(EDGE + r, rows)
            k, zp, npart = select(kind(p, block), [cond, z_part, n_part])
            q = qs[p + 3, here, :]
            total = qs[p + 2, here, :] + qs[p + 4, here, :]
            total = total + qs[p + 3, pl.ds(EDGE + r - 1, rows), :] + qs[p + 3, pl.ds(EDGE + r + 1, rows), :]
            total = total + jnp.where(first_lane, 0.0, pltpu.roll(q, 1, 1)) + jnp.where(last_lane, 0.0, pltpu.roll(q, ny - 1, 1))
            ps[p + 2, here, :] = zp * field(p, block) + npart * total
            ks[p + 2, here, :] = k

    def outside(p, ref):
        if isinstance(p, int) and (p < 0 or p >= nz):
            @pl.when(g == (0 if p < 0 else n_gz - 1))
            def _():
                ref[p + 2, inside, :] = jnp.zeros((nx, ny), jnp.float32)

    def flows(p):
        slot = lax.rem(p + 4, 2)
        for r in starts:
            block = pl.ds(r, rows)
            here = pl.ds(EDGE + r, rows)
            after = pl.ds(EDGE + r + 1, rows)
            k_here, press_here = ks[p + 2, here, :], ps[p + 2, here, :]
            k = k_here * hinder
            flow[slot, 0, block, :] = k * ks[p + 3, here, :] * (press_here - ps[p + 3, here, :])
            flow_x[slot, here, :] = k * ks[p + 2, after, :] * (press_here - ps[p + 2, after, :])
            w_y = k * pltpu.roll(k_here, ny - 1, 1) * (press_here - pltpu.roll(press_here, ny - 1, 1))
            flow[slot, 1, block, :] = jnp.where(last_lane, 0.0, w_y)

    def first_step(p):
        slot, source, before = lax.rem(p + 4, 4), lax.rem(p + 4, 2), lax.rem(p + 3, 4)
        for r in starts:
            block = pl.ds(r, rows)
            here = pl.ds(EDGE + r, rows)
            a_low, b_low = coef_z[before, 0, block, :], coef_z[before, 1, block, :]
            c, c_above, c_below = c0[p + 2, here, :], c0[p + 3, here, :], c0[p + 1, here, :]
            w = flow[source, 0, block, :]
            a = jnp.maximum(w, 0.0) + diffuse
            b = a - w
            w_x = flow_x[source, here, :]
            a_x = jnp.maximum(w_x, 0.0) + diffuse
            b_x = a_x - w_x
            w_low = flow_x[source, pl.ds(EDGE + r - 1, rows), :]
            a_x_low = jnp.maximum(w_low, 0.0) + diffuse
            b_x_low = a_x_low - w_low
            w_y = flow[source, 1, block, :]
            up = jnp.maximum(w_y, 0.0)
            a_y = up + diffuse
            b_y = (up - w_y) + diffuse_high
            w_low = pltpu.roll(w_y, 1, 1)
            up = jnp.maximum(w_low, 0.0)
            a_y_low = up + diffuse_low
            b_y_low = (up - w_low) + diffuse
            (bind,) = select(kind(p, block), [rate])
            centre = (a + a_x) + (a_y + b_x_low) + (b_y_low + b_low) + bind
            centre = 1.0 - centre
            value = centre * c + (b * c_above + a_low * c_below)
            value = value + (a_x_low * c0[p + 2, pl.ds(EDGE + r - 1, rows), :] + b_x * c0[p + 2, pl.ds(EDGE + r + 1, rows), :])
            value = value + (a_y_low * pltpu.roll(c, 1, 1) + b_y * pltpu.roll(c, ny - 1, 1))
            c1[p + 2, here, :] = value
            for i, value in enumerate((centre, a_x_low, b_x, a_y_low, b_y)):
                coefs[slot, i, block, :] = value
            coef_z[slot, 0, block, :] = a
            coef_z[slot, 1, block, :] = b

    def second_step(p):
        slot, before = lax.rem(p + 4, 4), lax.rem(p + 3, 4)
        for r in starts:
            block = pl.ds(r, rows)
            here = pl.ds(EDGE + r, rows)
            c = c1[p + 2, here, :]
            held, earlier = bnd[p, block, :], c0[p + 2, here, :]
            value = coefs[slot, 0, block, :] * c
            value = value + (coef_z[slot, 1, block, :] * c1[p + 3, here, :] + coef_z[before, 0, block, :] * c1[p + 1, here, :])
            value = value + (coefs[slot, 1, block, :] * c1[p + 2, pl.ds(EDGE + r - 1, rows), :]
                             + coefs[slot, 2, block, :] * c1[p + 2, pl.ds(EDGE + r + 1, rows), :])
            value = value + (coefs[slot, 3, block, :] * pltpu.roll(c, 1, 1) + coefs[slot, 4, block, :] * pltpu.roll(c, ny - 1, 1))
            out[p, block, :] = value
            (bind,) = select(kind(p, block), [rate])
            bnd[p, block, :] = held + bind * (earlier + c)

    def last_copies(i):
        z0 = pl.ds(nz - chunk + i * chunk // 2, chunk // 2)
        return [
            pltpu.make_async_copy(out.at[z0], free_out.at[z0], out_sems.at[n_chunks - 1 + i, 0]),
            pltpu.make_async_copy(bnd.at[z0], bound_out.at[z0], out_sems.at[n_chunks - 1 + i, 1]),
        ]

    def out_copies(i):
        z0 = pl.ds(i * chunk, chunk)
        return [
            pltpu.make_async_copy(out.at[z0], free_out.at[z0], out_sems.at[i, 0]),
            pltpu.make_async_copy(bnd.at[z0], bound_out.at[z0], out_sems.at[i, 1]),
        ]

    def turn(p):
        fixed = isinstance(p, int)
        if not fixed or 0 <= p - 4 < nz:
            second_step(p - 4)
        if not fixed or -1 <= p - 2 <= nz:
            first_step(p - 2)
            outside(p - 2, c1)
        if not fixed or -2 <= p - 1 <= nz:
            flows(p - 1)
        if fixed and p == 0:
            for r in starts:
                block = pl.ds(r, rows)
                w = flow[0, 0, block, :]
                a = jnp.maximum(w, 0.0) + diffuse
                coef_z[2, 0, block, :] = a
                coef_z[2, 1, block, :] = a - w
        if not fixed or -2 <= p + 1 <= nz + 1:
            press(p + 1)
            outside(p + 1, ks)
        if not fixed or -3 <= p + 3 <= nz + 2:
            scale(p + 3)

    for p in range(-6, 4):
        if p == 1:
            @pl.when(has_low)
            def _():
                each(halo_copies(False), "wait")

            each(chunk_copies(0), "wait")
        turn(p)

    def body(p, _):
        group = lax.div(p + 3, chunk)

        @pl.when((lax.rem(p + 3, chunk) == 0) & (group < n_chunks))
        def _():
            each(chunk_copies(group), "wait")

        turn(p)

        @pl.when((p >= chunk + 3) & (lax.rem(p - 3, chunk) == 0))
        def _():
            each(out_copies(lax.div(p - 3, chunk) - 1), "start")

        return 0

    lax.fori_loop(4, nz - 3, body, 0)

    @pl.when(has_high)
    def _():
        each(halo_copies(True), "wait")

    own = pltpu.make_async_copy(
        ps.at[pl.ds(2, nz), pl.ds(pl.multiple_of(EDGE + s * bx, 8), bx)], pressure, pressure_sem)
    for p in range(nz - 3, nz + 4):
        turn(p)
        if p == nz - 1:
            own.start()
            each(last_copies(0), "start")
    each(last_copies(1), "start")
    for i in range(n_chunks - 1):
        each(out_copies(i), "wait")
    for i in range(2):
        each(last_copies(i), "wait")
    own.wait()


def transport(n_gz, bx, cond_table, leak_table, bind_table, hindrance, diffusivity, scal, slab, tissue, thalo, conc, chalo, bound):
    nz, nx, ny = conc.shape
    anywhere = pl.BlockSpec(memory_space=pl.ANY)
    scalars = pl.BlockSpec(memory_space=pltpu.SMEM)
    vmem = pl.BlockSpec(memory_space=pltpu.VMEM)
    hbm = pl.BlockSpec(memory_space=pltpu.HBM)
    wide = nx + 2 * EDGE
    f32 = jnp.float32
    dma = pltpu.SemaphoreType.DMA
    n_chunks = nz // 8
    return pl.pallas_call(
        functools.partial(transport_kernel, n_gz),
        out_shape=(
            jax.ShapeDtypeStruct((nz, bx, ny), f32),
            jax.ShapeDtypeStruct((nz, nx, ny), f32),
            jax.ShapeDtypeStruct((nz, nx, ny), f32),
        ),
        in_specs=[scalars] * 5 + [vmem] * 4 + [anywhere, anywhere, hbm],
        out_specs=(anywhere, anywhere, anywhere),
        scratch_shapes=[
            pltpu.VMEM((nz + 4, wide, ny), f32),
            pltpu.VMEM((nz + 4, wide, ny), f32),
            pltpu.VMEM((nz, nx, ny), f32),
            pltpu.VMEM((nz, nx, ny), f32),
            pltpu.VMEM((nz + 6, wide, ny), f32),
            pltpu.VMEM((nz + 4, wide, ny), f32),
            pltpu.VMEM((nz + 4, wide, ny), f32),
            pltpu.VMEM((2, wide, ny), f32),
            pltpu.VMEM((2, 2, nx, ny), f32),
            pltpu.VMEM((4, 5, nx, ny), f32),
            pltpu.VMEM((4, 2, nx, ny), f32),
            dma((n_chunks + 2, 2)),
            dma((n_chunks + 1, 2)),
            dma,
        ],
        compiler_params=pltpu.CompilerParams(vmem_limit_bytes=36 << 20),
        name="transport",
    )(cond_table, leak_table, bind_table, hindrance, diffusivity, scal, slab, tissue, thalo, conc, chalo, in_hbm(bound))


def in_hbm(array):
    return pltpu.with_memory_space_constraint(array, pltpu.HBM)


def solution(mesh):
    n_size, n_gz = mesh.shape["size"], mesh.shape["gz"]

    def local(tissue, vessel_pressure, cond_table, leak_table, bind_table, hindrance, diffusivity, free_conc, bound_conc):
        conc, bound = free_conc[0], bound_conc[0]
        slab, thalo, chalo, scal = exchange(
            n_size, n_gz, *(in_hbm(v) for v in (cond_table, leak_table, vessel_pressure, tissue, conc)))
        pressure, free, held = transport(
            n_gz, vessel_pressure.shape[1], *(in_hbm(v) for v in (cond_table, leak_table, bind_table)), hindrance, diffusivity,
            scal, slab, tissue, thalo, conc, chalo, in_hbm(bound))
        return pressure, free[None], held[None]

    return jax.shard_map(
        local,
        mesh=mesh,
        in_specs=(
            P("gz", None, None), P("gz", "size", None), P(), P(), P("size", None), P("size"), P("size"),
            P("size", "gz", None, None), P("size", "gz", None, None),
        ),
        out_specs=(P("gz", "size", None), P("size", "gz", None, None), P("size", "gz", None, None)),
        check_vma=False,
    )
```

```python
import functools

import jax
import jax.numpy as jnp
from jax import lax
from jax.experimental import pallas as pl
from jax.experimental.pallas import tpu as pltpu
from jax.sharding import PartitionSpec as P

MESH = pl.DeviceIdType.MESH
TIME_STEP = 0.1
EDGE = 8
CHUNKS = 4


def each(copies, what):
    for copy in copies:
        getattr(copy, what)()


def select(labels, values):
    first, second = labels == 0, labels == 1
    return [jnp.where(first, v[0], jnp.where(second, v[1], v[2])) for v in values]


def two_sum(a, b):
    total = a + b
    part = total - a
    return total, (a - (total - part)) + (b - part)


def split(a):
    wide = 4097.0 * a
    high = wide - (wide - a)
    return high, a - high


def two_prod(a, b):
    product = a * b
    ah, al = split(a)
    bh, bl = split(b)
    return product, ((ah * bh - product) + ah * bl + al * bh) + al * bl


def pair_sub_product(x, a, b):
    p, e = two_prod(a[0], b[0])
    e = e + (a[0] * b[1] + a[1] * b[0])
    s, r = two_sum(x[0], -p)
    r = r + (x[1] - e)
    return two_sum(s, r)


def pair_ratio(x, y):
    q = x[0] / y[0]
    rest = pair_sub_product(x, (q, jnp.zeros_like(q)), y)
    return two_sum(q, (rest[0] + rest[1]) / y[0])


def scalar_tables(cond_ref, leak_ref):
    cond = [cond_ref[i] for i in range(3)]
    leak = [leak_ref[i] for i in range(3)]
    inverse = []
    for k, l in zip(cond, leak):
        inverse.append((1.0 / jnp.full((8, 128), 6.0 * k * k + l, jnp.float32))[0, 0])
    return cond, leak, inverse


def lane_neighbours(q, lane, ny):
    up = jnp.where(lane == ny - 1, 0.0, pltpu.roll(q, ny - 1, 1))
    down = jnp.where(lane == 0, 0.0, pltpu.roll(q, 1, 1))
    return up + down


def exchange_kernel(
    n_size, n_gz, cond_ref, leak_ref, vp, tissue, conc,
    slab, thalo, chalo, scal,
    ext, tex, qs, qv, ys, packed_out, packed_in, tile, red_size, red_gz, total_tile,
    local_sem, near_send, near_recv, block_send, block_recv,
    ring_send, ring_recv, grid_send, grid_recv,
):
    s, g = lax.axis_index("size"), lax.axis_index("gz")
    nz, bx, ny = vp.shape
    half = bx // 2
    nx = tissue.shape[1]

    ext[...] = jnp.zeros_like(ext)
    tex[...] = jnp.full_like(tex, 3)

    def remote(src, dst, send, recv, to_s, to_g):
        return pltpu.make_async_remote_copy(
            src_ref=src, dst_ref=dst, send_sem=send, recv_sem=recv,
            device_id={"size": to_s, "gz": to_g}, device_id_type=MESH)

    own_rows = pl.ds(pl.multiple_of(s * bx, 8), bx)

    barrier = pltpu.get_barrier_semaphore()

    def greet(to_s, to_g):
        pl.semaphore_signal(barrier, inc=1, device_id={"size": to_s, "gz": to_g}, device_id_type=MESH)

    greeted = 0
    for j in range(n_size):
        peer = lax.rem(s + j, n_size)
        for d in ((0,) if 1 < j < n_size - 1 else (0, 1, n_gz - 1)):
            if j or d:
                greet(peer, lax.rem(g + d, n_gz))
                greeted += 1
    for j in range(2, n_gz - 1):
        greet(s, lax.rem(g + j, n_gz))
        greeted += 1

    inner = pltpu.make_async_copy(vp, ext.at[pl.ds(2, nz), pl.ds(half, bx)], local_sem.at[0])
    inner.start()
    own = pltpu.make_async_copy(vp, slab.at[pl.ds(3, nz), own_rows], local_sem.at[1])
    own.start()

    wide = bx + 2 * half

    def tissue_rows(which):
        if which == "low":
            return pl.ds(0, bx + half), pl.ds(half, bx + half)
        if which == "high":
            return pl.ds(nx - bx - half, bx + half), pl.ds(0, bx + half)
        return pl.ds(pl.multiple_of(s * bx - half, 8), wide), pl.ds(0, wide)

    cases = (("low", s == 0), ("high", s == n_size - 1), ("mid", (s > 0) & (s < n_size - 1)))

    def tex_copy(which):
        src, dst = tissue_rows(which)
        return pltpu.make_async_copy(tissue.at[:, src], tex.at[pl.ds(2, nz), dst], local_sem.at[2])

    for which, cond in cases:
        @pl.when(cond)
        def _(which=which):
            tex_copy(which).start()

    inner.wait()

    def pack(e, _):
        for i, r in enumerate((half, half + 1, half + bx - 2, half + bx - 1)):
            packed_out[i, pl.ds(e, 1), :] = ext[e + 2, pl.ds(r, 1), :]
        return 0

    lax.fori_loop(0, nz, pack, 0, unroll=4)
    pl.semaphore_wait(barrier, greeted)

    lows, highs = pl.ds(0, half), pl.ds(half, half)
    above, below = pl.ds(half + bx, half), pl.ds(0, half)
    middle = pl.ds(half, bx)
    has_low, has_high = g > 0, g < n_gz - 1
    x_low, x_high = s > 0, s < n_size - 1
    near = [
        (x_high, x_low, packed_out.at[pl.ds(2, 2)], packed_in.at[pl.ds(0, 2)], 0, s + 1, g),
        (x_low, x_high, packed_out.at[pl.ds(0, 2)], packed_in.at[pl.ds(2, 2)], 1, s - 1, g),
        (has_high, has_low, vp.at[pl.ds(nz - 2, 2)], ext.at[pl.ds(0, 2), middle], 2, s, g + 1),
        (has_low, has_high, vp.at[pl.ds(0, 2)], ext.at[pl.ds(nz + 2, 2), middle], 3, s, g - 1),
        (x_high & has_high, x_low & has_low, vp.at[pl.ds(nz - 1, 1), highs], ext.at[pl.ds(1, 1), below], 4, s + 1, g + 1),
        (x_low & has_high, x_high & has_low, vp.at[pl.ds(nz - 1, 1), lows], ext.at[pl.ds(1, 1), above], 5, s - 1, g + 1),
        (x_high & has_low, x_low & has_high, vp.at[pl.ds(0, 1), highs], ext.at[pl.ds(nz + 2, 1), below], 6, s + 1, g - 1),
        (x_low & has_low, x_high & has_high, vp.at[pl.ds(0, 1), lows], ext.at[pl.ds(nz + 2, 1), above], 7, s - 1, g - 1),
    ]
    for which, cond in cases:
        src, dst = tissue_rows(which)
        near.append((has_high & cond, has_low & cond, tissue.at[pl.ds(nz - 2, 2), src], tex.at[pl.ds(0, 2), dst], 8, s, g + 1))
        near.append((has_low & cond, has_high & cond, tissue.at[pl.ds(0, 2), src], tex.at[pl.ds(nz + 2, 2), dst], 9, s, g - 1))
    late = [
        (has_high, has_low, tissue.at[pl.ds(nz - 3, 3)], thalo.at[pl.ds(0, 3)], 10, s, g + 1),
        (has_low, has_high, tissue.at[pl.ds(0, 3)], thalo.at[pl.ds(3, 3)], 11, s, g - 1),
        (has_high, has_low, conc.at[pl.ds(nz - 2, 2)], chalo.at[pl.ds(0, 2)], 12, s, g + 1),
        (has_low, has_high, conc.at[pl.ds(0, 2)], chalo.at[pl.ds(2, 2)], 13, s, g - 1),
    ]

    def start_all(copies):
        for cond, _, src, dst, i, to_s, to_g in copies:
            @pl.when(cond)
            def _(src=src, dst=dst, i=i, to_s=to_s, to_g=to_g):
                remote(src, dst, near_send.at[i], near_recv.at[i], to_s, to_g).start()

    def wait_all(copies):
        for sent, cond, src, dst, i, to_s, to_g in copies:
            @pl.when(cond)
            def _(src=src, dst=dst, i=i):
                remote(src, dst, near_send.at[i], near_recv.at[i], s, g).wait_recv()

            @pl.when(sent)
            def _(src=src, dst=dst, i=i):
                remote(src, dst, near_send.at[i], near_recv.at[i], s, g).wait_send()

    start_all(near)

    n_z = n_size // 2
    z, x = lax.div(s, 2), lax.rem(s, 2)
    z_up, z_down, z_far = lax.rem(z + 1, n_z), lax.rem(z + n_z - 1, n_z), lax.rem(z + 2, n_z)
    across = 2 * z + 1 - x
    up, down, far = 2 * z_up + x, 2 * z_down + x, 2 * z_far + x
    up_across, down_across, far_across = 2 * z_up + 1 - x, 2 * z_down + 1 - x, 2 * z_far + 1 - x
    depth = nz // CHUNKS
    part = depth // 2
    order = [0, CHUNKS - 1, *range(1, CHUNKS - 1)]

    def piece(block, c, kind, to, first=0, count=depth, own=False):
        planes = pl.ds(3 + c * depth + first, count)
        where = pl.ds(pl.multiple_of(block * bx, 8), bx)
        src = vp.at[pl.ds(c * depth + first, count)] if own else slab.at[planes, where]
        return remote(src, slab.at[planes, where], block_send.at[kind, c], block_recv.at[kind, c], to, g)

    def own_pieces(c):
        return [piece(s, c, 0, across, own=True), piece(s, c, 1, up, own=True), piece(s, c, 2, down, own=True)]

    def from_across(c):
        return [piece(across, c, 3, up), piece(across, c, 4, down)]

    def from_down(c):
        return [piece(down, c, 5, up, 0, part)]

    def from_up(c):
        return [piece(up, c, 6, down, part, depth - part)]

    def from_far(c):
        return [piece(far, c, 7, across)]

    def hand_on(c):
        piece(across, c, 0, s).wait_recv()
        each(from_across(c), "start")
        piece(down, c, 1, s).wait_recv()
        each(from_down(c), "start")
        piece(up, c, 2, s).wait_recv()
        each(from_up(c), "start")

    def hand_far(c):
        piece(far, c, 5, s, 0, part).wait_recv()
        piece(far, c, 6, s, part, depth - part).wait_recv()
        each(from_far(c), "start")

    def finish(c):
        piece(down_across, c, 3, s).wait_recv()
        piece(up_across, c, 4, s).wait_recv()
        piece(far_across, c, 7, s).wait_recv()

    for c in order:
        each(own_pieces(c), "start")
    start_all(late)

    edges = [
        (has_high, has_low, slab.at[pl.ds(nz, 3)], slab.at[pl.ds(0, 3)], 14, s, g + 1),
        (has_low, has_high, slab.at[pl.ds(3, 3)], slab.at[pl.ds(nz + 3, 3)], 15, s, g - 1),
    ]

    cond, leak, inverse = scalar_tables(cond_ref, leak_ref)
    first = [l * i for l, i in zip(leak, inverse)]
    second = [k * l * i for k, l, i in zip(cond, leak, inverse)]
    lane = lax.broadcasted_iota(jnp.int32, (wide, ny), 1)

    for which, c in cases:
        @pl.when(c)
        def _(which=which):
            tex_copy(which).wait()
    wait_all(near)

    def unpack(low):
        def rows_in(e, _):
            for i in range(2):
                r = half - 2 + i if low else half + bx + i
                ext[e + 2, pl.ds(r, 1), :] = packed_in[i if low else 2 + i, pl.ds(e, 1), :]
            return 0
        lax.fori_loop(0, nz, rows_in, 0, unroll=4)

    @pl.when(x_low)
    def _():
        unpack(True)

    @pl.when(x_high)
    def _():
        unpack(False)

    def scale(e, _):
        (t2,) = select(tex[e], [second])
        qs[e] = t2 * ext[e]
        return 0

    lax.fori_loop(0, nz + 4, scale, 0, unroll=4)
    def stencil(ref, e):
        q = ref[e]
        total = ref[e - 1] + ref[e + 1] + pltpu.roll(q, 1, 0) + pltpu.roll(q, wide - 1, 0)
        return 6.0 * q - (total + lane_neighbours(q, lane, ny))

    def add_product(acc, a, b):
        h, r = two_sum(acc[0], a[1] * b[1])
        return h, acc[1] + ((a[1] * b[2] + a[2] * b[0]) + r)

    def apply(e):
        labels = tex[e]
        k, l, i, t1 = select(labels, [cond, leak, inverse, first])
        k = jnp.where(labels == 3, 0.0, k)
        field = ext[e]
        z = t1 * field
        az = l * z + k * stencil(qs, e)
        y = i * az
        qv[e] = k * y
        ys[e] = y
        return l * field, z, az, y

    def mine(x):
        x = x[half:half + bx]
        return (x, *split(x))

    def first_sums(e, accs):
        r0, z, az, y = (mine(x) for x in apply(e))
        return (add_product(accs[0], r0, z), add_product(accs[1], z, az), add_product(accs[2], y, az))

    apply(1)
    apply(nz + 2)
    zero = jnp.zeros((bx, ny), jnp.float32)
    sums = lax.fori_loop(2, nz + 2, first_sums, ((zero, zero),) * 3, unroll=2)
    hand_on(order[0])

    def last_sum(e, acc):
        labels = tex[e]
        k, l = select(labels, [cond, leak])
        y = ys[e]
        ay = l * y + k * stencil(qv, e)
        return add_product(acc, mine(y), mine(ay))

    sums = (*sums, lax.fori_loop(2, nz + 2, last_sum, (zero, zero), unroll=4))

    row = lax.broadcasted_iota(jnp.int32, (8, ny), 0)
    packed = jnp.zeros((8, ny), jnp.float32)
    for m, (h, l) in enumerate(sums):
        hs, ls = h[0:8], l[0:8]
        for r in range(8, bx, 8):
            hs, e = two_sum(hs, h[r:r + 8])
            ls = ls + l[r:r + 8] + e
        for shift in (4, 2, 1):
            hs, e = two_sum(hs, pltpu.roll(hs, shift, 0))
            ls = ls + pltpu.roll(ls, shift, 0) + e
        packed = jnp.where(row == m, hs, jnp.where(row == m + 4, ls, packed))
    tile[...] = packed

    def add_tiles(parts):
        total, errors = parts[0], jnp.zeros((8, ny), jnp.float32)
        for part in parts[1:]:
            total, e = two_sum(total, part)
            errors = errors + e
        return total + pltpu.roll(jnp.where(row < 4, errors, 0.0), 4, 0)

    def reduce(src, slots, index, count, axis, send, recv, between):
        for j in range(1, count):
            to = lax.rem(index + j, count)
            dev = (to, g) if axis == "size" else (s, to)
            remote(src, slots.at[index], send, recv, *dev).start()
        between()
        arrived = slots.at[pl.ds(0, count - 1)]
        remote(arrived, arrived, send, recv, s, g).wait()
        slots[index] = src[...]
        return add_tiles([slots[i] for i in range(count)])

    def first_half():
        hand_on(order[1])
        hand_far(order[0])
        hand_on(order[2])
        hand_far(order[1])
        hand_on(order[3])

    def second_half():
        hand_far(order[2])
        hand_far(order[3])
        own.wait()
        for c in order[:2]:
            finish(c)
        start_all(edges)

    total_tile[...] = reduce(tile, red_size, s, n_size, "size", ring_send, ring_recv, first_half)
    total = reduce(total_tile, red_gz, g, n_gz, "gz", grid_send, grid_recv, second_half)

    errors = jnp.zeros_like(total)
    shift = ny // 2
    while shift:
        total, e = two_sum(total, pltpu.roll(total, shift, 1))
        errors = errors + pltpu.roll(errors, shift, 1) + e
        shift //= 2
    lower = pltpu.roll(total, 4, 0) + errors
    b = [(total[m:m + 1], lower[m:m + 1]) for m in range(4)]
    t = pair_ratio(b[1], b[0])
    v = pair_sub_product(b[2], t, b[1])
    w = pair_sub_product(pair_sub_product(b[3], t, b[2]), t, v)
    b0, b1, v, w, t = b[0][0], b[1][0], v[0], w[0], t[0]
    det = b1 * w - v * v
    x_part = b0 * w / det
    y_part = -(b0 * v) / det
    scal[...] = jnp.where(row == 0, x_part + y_part * (1.0 - t), -y_part)

    for c in order[2:]:
        finish(c)
    for c in order:
        each(own_pieces(c) + from_across(c) + from_down(c) + from_up(c) + from_far(c), "wait_send")
    wait_all(late)
    wait_all(edges)


def exchange(n_size, n_gz, cond_table, leak_table, vp, tissue, conc):
    nz, bx, ny = vp.shape
    nx = tissue.shape[1]
    anywhere = pl.BlockSpec(memory_space=pl.ANY)
    scalars = pl.BlockSpec(memory_space=pltpu.SMEM)
    vmem = pl.BlockSpec(memory_space=pltpu.VMEM)
    hbm = pl.BlockSpec(memory_space=pltpu.HBM)
    dma = pltpu.SemaphoreType.DMA
    return pl.pallas_call(
        functools.partial(exchange_kernel, n_size, n_gz),
        out_shape=(
            jax.ShapeDtypeStruct((nz + 6, nx, ny), jnp.float32),
            jax.ShapeDtypeStruct((6, nx, ny), jnp.int32),
            jax.ShapeDtypeStruct((4, nx, ny), jnp.float32),
            jax.ShapeDtypeStruct((8, ny), jnp.float32),
        ),
        in_specs=[scalars, scalars, hbm, hbm, hbm],
        out_specs=(anywhere, anywhere, anywhere, pl.BlockSpec(memory_space=pltpu.VMEM)),
        scratch_shapes=[
            pltpu.VMEM((nz + 4, 2 * bx, ny), jnp.float32),
            pltpu.VMEM((nz + 4, 2 * bx, ny), jnp.int32),
            pltpu.VMEM((nz + 4, 2 * bx, ny), jnp.float32),
            pltpu.VMEM((nz + 4, 2 * bx, ny), jnp.float32),
            pltpu.VMEM((nz + 4, 2 * bx, ny), jnp.float32),
            pltpu.VMEM((4, nz, ny), jnp.float32),
            pltpu.VMEM((4, nz, ny), jnp.float32),
            pltpu.VMEM((8, ny), jnp.float32),
            pltpu.VMEM((n_size, 8, ny), jnp.float32),
            pltpu.VMEM((n_gz, 8, ny), jnp.float32),
            pltpu.VMEM((8, ny), jnp.float32),
            dma((3,)),
            dma((16,)), dma((16,)),
            dma((8, CHUNKS)), dma((8, CHUNKS)),
            dma, dma, dma, dma,
        ],
        compiler_params=pltpu.CompilerParams(collective_id=0, has_side_effects=True, vmem_limit_bytes=16 << 20),
        name="exchange",
    )(cond_table, leak_table, vp, tissue, conc)


def transport_kernel(
    n_gz, cond_ref, leak_ref, bind_ref, hinder_ref, diffuse_ref, scal, slab, tissue, thalo, conc, chalo, bound,
    pressure, free_out, bound_out,
    c0, c1, bnd, out, qs, ps, ks, flow_x, flow, coefs, coef_z, sems, out_sems, pressure_sem,
):
    s, g = lax.axis_index("size"), lax.axis_index("gz")
    nz, nx, ny = conc.shape
    bx = pressure.shape[1]
    rows = 64 if nx % 64 == 0 else nx
    chunk = 8
    n_chunks = nz // chunk
    has_low, has_high = g > 0, g < n_gz - 1
    inside = pl.ds(EDGE, nx)

    def chunk_copies(i):
        z0 = i * chunk
        return [
            pltpu.make_async_copy(conc.at[pl.ds(z0, chunk)], c0.at[pl.ds(z0 + 2, chunk), inside], sems.at[i, 0]),
            pltpu.make_async_copy(bound.at[pl.ds(z0, chunk)], bnd.at[pl.ds(z0, chunk)], sems.at[i, 1]),
        ]

    def halo_copies(high):
        i, c = n_chunks + int(high), nz + 2 if high else 0
        return [
            pltpu.make_async_copy(chalo.at[pl.ds(2 * high, 2)], c0.at[pl.ds(c, 2), inside], sems.at[i, 0]),
        ]

    @pl.when(has_low)
    def _():
        each(halo_copies(False), "start")

    for i in range(n_chunks):
        each(chunk_copies(i), "start")

    @pl.when(has_high)
    def _():
        each(halo_copies(True), "start")

    edge_rows = jnp.zeros((EDGE, ny), jnp.float32)

    def clear(i, _):
        for ref in (c0, c1, qs, ps, ks):
            ref[i, pl.ds(0, EDGE), :] = edge_rows
            ref[i, pl.ds(EDGE + nx, EDGE), :] = edge_rows
        return 0

    lax.fori_loop(0, nz + 4, clear, 0)
    for i in (nz + 4, nz + 5):
        qs[i, pl.ds(0, EDGE), :] = edge_rows
        qs[i, pl.ds(EDGE + nx, EDGE), :] = edge_rows
    for i in range(2):
        flow_x[i, pl.ds(0, EDGE), :] = edge_rows

    def blank(high):
        c = nz + 2 if high else 0
        for i in range(2):
            c0[c + i, inside, :] = jnp.zeros((nx, ny), jnp.float32)

    @pl.when(g == 0)
    def _():
        blank(False)

    @pl.when(g == n_gz - 1)
    def _():
        blank(True)

    cond, leak, inverse = scalar_tables(cond_ref, leak_ref)
    x_part, y_part = scal[0, 0], scal[1, 0]
    hinder = TIME_STEP * hinder_ref[0]
    diffuse = TIME_STEP * diffuse_ref[0]
    rate = [TIME_STEP * bind_ref[0, i] for i in range(3)]
    second = [k * l * i for k, l, i in zip(cond, leak, inverse)]
    z_part = [x_part * l * i for l, i in zip(leak, inverse)]
    n_part = [y_part * k * i for k, i in zip(cond, inverse)]
    lane = lax.broadcasted_iota(jnp.int32, (rows, ny), 1)
    first_lane, last_lane = lane == 0, lane == ny - 1
    diffuse_low = jnp.where(first_lane, 0.0, diffuse)
    diffuse_high = jnp.where(last_lane, 0.0, diffuse)
    starts = range(0, nx, rows)

    def kind(p, block):
        if isinstance(p, int) and p < 0:
            return thalo[p + 3, block, :]
        if isinstance(p, int) and p >= nz:
            return thalo[p - nz + 3, block, :]
        return tissue[p, block, :]

    def field(p, block):
        value = slab[p + 3, block, :]
        if isinstance(p, int) and (p < 0 or p >= nz):
            value = jnp.where(has_low if p < 0 else has_high, value, 0.0)
        return value

    def scale(p):
        for r in starts:
            block = pl.ds(r, rows)
            (t2,) = select(kind(p, block), [second])
            qs[p + 3, pl.ds(EDGE + r, rows), :] = t2 * field(p, block)

    def press(p):
        for r in starts:
            block = pl.ds(r, rows)
            here = pl.ds(EDGE + r, rows)
            k, zp, npart = select(kind(p, block), [cond, z_part, n_part])
            q = qs[p + 3, here, :]
            total = qs[p + 2, here, :] + qs[p + 4, here, :]
            total = total + qs[p + 3, pl.ds(EDGE + r - 1, rows), :] + qs[p + 3, pl.ds(EDGE + r + 1, rows), :]
            total = total + jnp.where(first_lane, 0.0, pltpu.roll(q, 1, 1)) + jnp.where(last_lane, 0.0, pltpu.roll(q, ny - 1, 1))
            ps[p + 2, here, :] = zp * field(p, block) + npart * total
            ks[p + 2, here, :] = k

    def outside(p, ref):
        if isinstance(p, int) and (p < 0 or p >= nz):
            @pl.when(g == (0 if p < 0 else n_gz - 1))
            def _():
                ref[p + 2, inside, :] = jnp.zeros((nx, ny), jnp.float32)

    def flows(p):
        slot = lax.rem(p + 4, 2)
        for r in starts:
            block = pl.ds(r, rows)
            here = pl.ds(EDGE + r, rows)
            after = pl.ds(EDGE + r + 1, rows)
            k_here, press_here = ks[p + 2, here, :], ps[p + 2, here, :]
            k = k_here * hinder
            flow[slot, 0, block, :] = k * ks[p + 3, here, :] * (press_here - ps[p + 3, here, :])
            flow_x[slot, here, :] = k * ks[p + 2, after, :] * (press_here - ps[p + 2, after, :])
            w_y = k * pltpu.roll(k_here, ny - 1, 1) * (press_here - pltpu.roll(press_here, ny - 1, 1))
            flow[slot, 1, block, :] = jnp.where(last_lane, 0.0, w_y)

    def first_step(p):
        slot, source, before = lax.rem(p + 4, 4), lax.rem(p + 4, 2), lax.rem(p + 3, 4)
        for r in starts:
            block = pl.ds(r, rows)
            here = pl.ds(EDGE + r, rows)
            a_low, b_low = coef_z[before, 0, block, :], coef_z[before, 1, block, :]
            c, c_above, c_below = c0[p + 2, here, :], c0[p + 3, here, :], c0[p + 1, here, :]
            w = flow[source, 0, block, :]
            a = jnp.maximum(w, 0.0) + diffuse
            b = a - w
            w_x = flow_x[source, here, :]
            a_x = jnp.maximum(w_x, 0.0) + diffuse
            b_x = a_x - w_x
            w_low = flow_x[source, pl.ds(EDGE + r - 1, rows), :]
            a_x_low = jnp.maximum(w_low, 0.0) + diffuse
            b_x_low = a_x_low - w_low
            w_y = flow[source, 1, block, :]
            up = jnp.maximum(w_y, 0.0)
            a_y = up + diffuse
            b_y = (up - w_y) + diffuse_high
            w_low = pltpu.roll(w_y, 1, 1)
            up = jnp.maximum(w_low, 0.0)
            a_y_low = up + diffuse_low
            b_y_low = (up - w_low) + diffuse
            (bind,) = select(kind(p, block), [rate])
            centre = (a + a_x) + (a_y + b_x_low) + (b_y_low + b_low) + bind
            centre = 1.0 - centre
            value = centre * c + (b * c_above + a_low * c_below)
            value = value + (a_x_low * c0[p + 2, pl.ds(EDGE + r - 1, rows), :] + b_x * c0[p + 2, pl.ds(EDGE + r + 1, rows), :])
            value = value + (a_y_low * pltpu.roll(c, 1, 1) + b_y * pltpu.roll(c, ny - 1, 1))
            c1[p + 2, here, :] = value
            for i, value in enumerate((centre, a_x_low, b_x, a_y_low, b_y)):
                coefs[slot, i, block, :] = value
            coef_z[slot, 0, block, :] = a
            coef_z[slot, 1, block, :] = b

    def second_step(p):
        slot, before = lax.rem(p + 4, 4), lax.rem(p + 3, 4)
        for r in starts:
            block = pl.ds(r, rows)
            here = pl.ds(EDGE + r, rows)
            c = c1[p + 2, here, :]
            held, earlier = bnd[p, block, :], c0[p + 2, here, :]
            value = coefs[slot, 0, block, :] * c
            value = value + (coef_z[slot, 1, block, :] * c1[p + 3, here, :] + coef_z[before, 0, block, :] * c1[p + 1, here, :])
            value = value + (coefs[slot, 1, block, :] * c1[p + 2, pl.ds(EDGE + r - 1, rows), :]
                             + coefs[slot, 2, block, :] * c1[p + 2, pl.ds(EDGE + r + 1, rows), :])
            value = value + (coefs[slot, 3, block, :] * pltpu.roll(c, 1, 1) + coefs[slot, 4, block, :] * pltpu.roll(c, ny - 1, 1))
            out[p, block, :] = value
            (bind,) = select(kind(p, block), [rate])
            bnd[p, block, :] = held + bind * (earlier + c)

    def last_copies(i):
        first, count = ((nz - 8, 4), (nz - 4, 2), (nz - 2, 2))[i]
        z0 = pl.ds(first, count)
        return [
            pltpu.make_async_copy(out.at[z0], free_out.at[z0], out_sems.at[n_chunks - 1 + i, 0]),
            pltpu.make_async_copy(bnd.at[z0], bound_out.at[z0], out_sems.at[n_chunks - 1 + i, 1]),
        ]

    def out_copies(i):
        z0 = pl.ds(i * chunk, chunk)
        return [
            pltpu.make_async_copy(out.at[z0], free_out.at[z0], out_sems.at[i, 0]),
            pltpu.make_async_copy(bnd.at[z0], bound_out.at[z0], out_sems.at[i, 1]),
        ]

    def turn(p):
        fixed = isinstance(p, int)
        if not fixed or 0 <= p - 4 < nz:
            second_step(p - 4)
        if not fixed or -1 <= p - 2 <= nz:
            first_step(p - 2)
            outside(p - 2, c1)
        if not fixed or -2 <= p - 1 <= nz:
            flows(p - 1)
        if fixed and p == 0:
            for r in starts:
                block = pl.ds(r, rows)
                w = flow[0, 0, block, :]
                a = jnp.maximum(w, 0.0) + diffuse
                coef_z[2, 0, block, :] = a
                coef_z[2, 1, block, :] = a - w
        if not fixed or -2 <= p + 1 <= nz + 1:
            press(p + 1)
            outside(p + 1, ks)
        if not fixed or -3 <= p + 3 <= nz + 2:
            scale(p + 3)

    for p in range(-6, 4):
        if p == 1:
            @pl.when(has_low)
            def _():
                each(halo_copies(False), "wait")

            each(chunk_copies(0), "wait")
        turn(p)

    def body(p, _):
        group = lax.div(p + 3, chunk)

        @pl.when((lax.rem(p + 3, chunk) == 0) & (group < n_chunks))
        def _():
            each(chunk_copies(group), "wait")

        turn(p)

        @pl.when((p >= chunk + 3) & (lax.rem(p - 3, chunk) == 0))
        def _():
            each(out_copies(lax.div(p - 3, chunk) - 1), "start")

        return 0

    lax.fori_loop(4, nz - 3, body, 0)

    @pl.when(has_high)
    def _():
        each(halo_copies(True), "wait")

    own = pltpu.make_async_copy(
        ps.at[pl.ds(2, nz), pl.ds(pl.multiple_of(EDGE + s * bx, 8), bx)], pressure, pressure_sem)
    for p in range(nz - 3, nz + 4):
        turn(p)
        if p == nz - 1:
            own.start()
            each(last_copies(0), "start")
        if p == nz + 1:
            each(last_copies(1), "start")
    each(last_copies(2), "start")
    for i in range(n_chunks - 1):
        each(out_copies(i), "wait")
    for i in range(3):
        each(last_copies(i), "wait")
    own.wait()


def transport(n_gz, bx, cond_table, leak_table, bind_table, hindrance, diffusivity, scal, slab, tissue, thalo, conc, chalo, bound):
    nz, nx, ny = conc.shape
    anywhere = pl.BlockSpec(memory_space=pl.ANY)
    scalars = pl.BlockSpec(memory_space=pltpu.SMEM)
    vmem = pl.BlockSpec(memory_space=pltpu.VMEM)
    hbm = pl.BlockSpec(memory_space=pltpu.HBM)
    wide = nx + 2 * EDGE
    f32 = jnp.float32
    dma = pltpu.SemaphoreType.DMA
    n_chunks = nz // 8
    return pl.pallas_call(
        functools.partial(transport_kernel, n_gz),
        out_shape=(
            jax.ShapeDtypeStruct((nz, bx, ny), f32),
            jax.ShapeDtypeStruct((nz, nx, ny), f32),
            jax.ShapeDtypeStruct((nz, nx, ny), f32),
        ),
        in_specs=[scalars] * 5 + [vmem] * 4 + [anywhere, anywhere, hbm],
        out_specs=(anywhere, anywhere, anywhere),
        scratch_shapes=[
            pltpu.VMEM((nz + 4, wide, ny), f32),
            pltpu.VMEM((nz + 4, wide, ny), f32),
            pltpu.VMEM((nz, nx, ny), f32),
            pltpu.VMEM((nz, nx, ny), f32),
            pltpu.VMEM((nz + 6, wide, ny), f32),
            pltpu.VMEM((nz + 4, wide, ny), f32),
            pltpu.VMEM((nz + 4, wide, ny), f32),
            pltpu.VMEM((2, wide, ny), f32),
            pltpu.VMEM((2, 2, nx, ny), f32),
            pltpu.VMEM((4, 5, nx, ny), f32),
            pltpu.VMEM((4, 2, nx, ny), f32),
            dma((n_chunks + 2, 2)),
            dma((n_chunks + 2, 2)),
            dma,
        ],
        compiler_params=pltpu.CompilerParams(vmem_limit_bytes=36 << 20),
        name="transport",
    )(cond_table, leak_table, bind_table, hindrance, diffusivity, scal, slab, tissue, thalo, conc, chalo, in_hbm(bound))


def in_hbm(array):
    return pltpu.with_memory_space_constraint(array, pltpu.HBM)


def solution(mesh):
    n_size, n_gz = mesh.shape["size"], mesh.shape["gz"]

    def local(tissue, vessel_pressure, cond_table, leak_table, bind_table, hindrance, diffusivity, free_conc, bound_conc):
        conc, bound = free_conc[0], bound_conc[0]
        slab, thalo, chalo, scal = exchange(
            n_size, n_gz, *(in_hbm(v) for v in (cond_table, leak_table, vessel_pressure, tissue, conc)))
        pressure, free, held = transport(
            n_gz, vessel_pressure.shape[1], *(in_hbm(v) for v in (cond_table, leak_table, bind_table)), hindrance, diffusivity,
            scal, slab, tissue, thalo, conc, chalo, in_hbm(bound))
        return pressure, free[None], held[None]

    return jax.shard_map(
        local,
        mesh=mesh,
        in_specs=(
            P("gz", None, None), P("gz", "size", None), P(), P(), P("size", None), P("size"), P("size"),
            P("size", "gz", None, None), P("size", "gz", None, None),
        ),
        out_specs=(P("gz", "size", None), P("size", "gz", None, None), P("size", "gz", None, None)),
        check_vma=False,
    )
```
